128 devices in a mesh: seq: 16 (over z, x), exp: 8 (over y, core).
Axes of the slice: x: 4, y: 4, z: 4, core: 2. Of those that a mesh axis runs over, the one named last changes fastest.
Arguments:
- queries: bfloat16 [3, 2048, 4096], P(None, 'seq', 'exp'), may hold values from -6 to 6
- key_rows: bfloat16 [3, 2048, 1024], P(None, 'seq', 'exp'), may hold values from -6 to 6
- value_rows: bfloat16 [3, 2048, 1024], P(None, 'seq', 'exp'), may hold values from -6 to 6
- residual: bfloat16 [3, 2048, 4096], P(None, ('seq', 'exp')), may hold values from -6 to 6
- w_out: bfloat16 [4096, 4096], P('exp'), may hold values from -3 to 3
- norm_gain: float32 [4096], replicated, may hold values from 0.1 to 1.9
- w_gate: bfloat16 [128, 4096, 768], P(('seq', 'exp')), may hold values from -0.09375 to 0.09375
- w_up: bfloat16 [128, 4096, 768], P(('seq', 'exp')), may hold values from -0.09375 to 0.09375
- w_down: bfloat16 [128, 768, 4096], P(('seq', 'exp')), may hold values from -0.21875 to 0.21875
- routes: int32 [2048, 8], P(('seq', 'exp')), may hold values from 0 to 63, all different within a row; in each aligned block of 16 rows (0 to 15, 16 to 31, ...) at most 3 rows name the same one
- route_gain: float32 [2048, 8], P(('seq', 'exp')), may hold values from 0.03 to 0.3
Outputs:
- layer_out: bfloat16 [3, 2048, 4096], P(None, ('seq', 'exp'))
- probe_products: float32 [2, 2048], P(None, ('seq', 'exp'))
The draws below stay inside these ranges and needn't reach their ends.
Inputs may be any that keep to these rules, and one draw needn't show every extreme that they name: `routes`: each row names 8 different experts; among the 16 rows of one device no expert is named more than 3 times, and in some device's rows some expert is named exactly 3 times.
All inputs are finite; a program needn't handle non-finite values.
Results may differ from the reference program's by a relative error of at most 0.023.
Values may be sent and summed in bfloat16 or wider, within the bound.
A program may use at most 192 MiB of HBM per device.

```python
import math
import jax
import jax.numpy as jnp
import numpy as np
from jax import lax

D = 4096
HEADS = 32
KVH = 8
HD = 128
FH = 768
TOP = 8
E = 64
TOKENS = 2048
LENGTH = 2048
IMAGES = 1
TOK_DEV = 16
CAP = 3


def draw_queries(key, part):
    key = jax.random.fold_in(key, 3)
    shape = (3, TOKENS, KVH, HEADS // KVH, HD)
    base = jax.random.truncated_normal(key, -4.0, 4.0, shape, jnp.float32)
    return base.reshape(3, TOKENS, HEADS * HD).astype(jnp.bfloat16)


def draw_key_rows(key, part):
    key = jax.random.fold_in(key, 5)
    shape = (3, TOKENS, KVH, HD)
    base = jax.random.truncated_normal(key, -4.0, 4.0, shape, jnp.float32)
    return base.reshape(3, TOKENS, KVH * HD).astype(jnp.bfloat16)


def shard_levels(own_key, shape, cuts, smallest, largest):
    loudness = 1.0
    for dim, blocks in cuts:
        draws = jax.random.uniform(jax.random.fold_in(jax.random.fold_in(own_key, 6), dim), (blocks,), jnp.float32, smallest / len(cuts), largest / len(cuts))
        loudness = loudness * jnp.repeat(jnp.exp(draws), shape[dim] // blocks).reshape((-1,) + (1,) * (len(shape) - 1 - dim))
    return loudness


def routed_block(stream_key, own, number, rows, count, top, most, lean):
    ranking = jax.random.permutation(stream_key, count)
    crowded, usual = shares(count, rows * top, most, lean, True), shares(count, rows * top, most, lean, False)
    places = jnp.arange(count)

    def named(tallies, rotation):
        used = int((tallies > 0).sum())
        fixed = max(1, used // 4)
        shifted = fixed + (places - fixed + rotation * (used - fixed)) % max(1, count - fixed)
        return jnp.zeros((count,), jnp.int32).at[ranking[jnp.where(places < fixed, places, shifted)]].set(jnp.asarray(tallies, jnp.int32))

    tallies = jnp.where(number % 4 == 0, named(crowded, number // 4), named(usual, number - number // 4 - 1))
    mixed = jax.random.permutation(jax.random.fold_in(own, 3), count)
    source_of, taker = mixed[0:count // 2 * 2:2], mixed[1:count // 2 * 2:2]
    room = jnp.minimum(tallies[source_of] - 1, most - tallies[taker]) // 2
    room = jnp.where((source_of == ranking[0]) | (taker == ranking[0]) | (tallies[taker] == 0), 0, jnp.maximum(room, 0))
    shifted = jax.random.randint(jax.random.fold_in(own, 4), (count // 2,), 0, 1 << 20) % (room + 1)
    tallies = tallies.at[source_of].add(-shifted).at[taker].add(shifted)
    items = jnp.searchsorted(jnp.cumsum(tallies), jnp.arange(rows * top), side="right").astype(jnp.int32)
    listing = items.reshape(top, rows).T
    listing = listing[jax.random.permutation(jax.random.fold_in(own, 1), rows)]
    rotation = jax.random.randint(jax.random.fold_in(own, 2), (rows, 1), 0, top)
    return jnp.take_along_axis(listing, (jnp.arange(top)[None, :] + rotation) % top, axis=1)


def shares(count, total, most, skew, full):
    portions = [(1 << 20) // math.isqrt(grade ** skew) + 1 for grade in range(1, count + 1)]
    largest = most if full else min(most, max(-(-total // count), total * portions[0] // sum(portions)))
    least = 1 if total - largest >= count - 1 else 0
    holding, rest = [largest] + [least] * (count - 1), total - largest - least * (count - 1)
    while rest > 0:
        movable = [i for i in range(1, count) if holding[i] < largest] or [i for i in range(1, count) if holding[i] < most]
        pool, budget = sum([portions[i] for i in movable]), rest
        for i in movable:
            more = min(most - holding[i], max(1, budget * portions[i] // pool), rest)
            holding[i] = holding[i] + more
            rest = rest - more
    return np.array(holding)


def bell_draw(key, extent, scale, bound, pieces=(), kind=jnp.bfloat16):
    entries = jax.random.normal(key, extent, jnp.float32) * scale
    if len(pieces) > 0:
        entries = shard_levels(key, extent, pieces, -0.22, 0.18) * entries
    return jnp.clip(entries, min=-bound, max=bound).astype(kind)


def setup_inputs(seed: int = 0) -> dict:
    key_of = jax.random.split(jax.random.key(seed), 12)
    queries = draw_queries(jax.random.fold_in(key_of[11], 71), 0)
    key_rows = draw_key_rows(jax.random.fold_in(key_of[11], 71), 0)
    value_rows = bell_draw(key_of[2], (3, TOKENS, KVH * HD), 1.0, 6.0, ((1, 16), (2, 8)))
    residual = bell_draw(key_of[3], (3, TOKENS, D), 0.5, 6.0, ((1, 128),))
    w_out = bell_draw(key_of[4], (HEADS * HD, D), 0.2, 3.0, ((0, 8),))
    norm_gain = jnp.clip(1.0 + 0.18 * jax.random.normal(key_of[5], (D,), jnp.float32), 0.1, 1.9)
    w_gate = bell_draw(key_of[6], (2 * E, D, FH), D ** -0.5, 0.09375, ((0, 128),))
    w_up = bell_draw(key_of[7], (2 * E, D, FH), D ** -0.5, 0.09375, ((0, 128),))
    w_down = bell_draw(key_of[8], (2 * E, FH, D), FH ** -0.5, 0.21875, ((0, 128),))
    routes_keys = jax.random.split(jax.random.fold_in(key_of[9], 1), TOKENS // TOK_DEV)
    routes_turns = jax.random.permutation(jax.random.fold_in(key_of[9], 3), TOKENS // TOK_DEV)
    routes = jax.vmap(lambda own, number: routed_block(jax.random.fold_in(key_of[9], 2), own, number, TOK_DEV, E, TOP, CAP, 2))(routes_keys, routes_turns).reshape((TOKENS, TOP))
    route_gain = jnp.clip(0.03 + 0.27 * jax.random.uniform(key_of[10], (TOKENS, TOP), jnp.float32) ** shard_levels(key_of[10], (TOKENS, TOP), ((0, 128),), -0.2, 0.2), 0.03, 0.3)
    return dict(queries=queries, key_rows=key_rows, value_rows=value_rows, residual=residual, w_out=w_out, norm_gain=norm_gain, w_gate=w_gate, w_up=w_up, w_down=w_down, routes=routes, route_gain=route_gain)


EPS = 1e-06

def attention(queries, key_rows, value_rows):
    groups = HEADS // KVH
    score_scale = 1.0 / math.sqrt(HD)
    highest = lax.Precision.HIGHEST
    q_float = queries.astype(jnp.float32).reshape(3, IMAGES, LENGTH, KVH, groups, HD).transpose(1, 0, 2, 3, 4, 5)
    k_float = key_rows.astype(jnp.float32).reshape(3, IMAGES, LENGTH, KVH, HD).transpose(1, 0, 2, 3, 4)
    v_float = value_rows.astype(jnp.float32).reshape(3, IMAGES, LENGTH, KVH, HD).transpose(1, 0, 2, 3, 4)

    def one_image(block):
        q_img, k_img, v_img = block
        scores = jnp.einsum('qkgd,nkd->kgqn', q_img[0], k_img[0], precision=highest) * score_scale
        weights = jax.nn.softmax(scores, axis=-1)
        main_out = jnp.einsum('kgqn,nkd->qkgd', weights, v_img[0], precision=highest)
        outs = [main_out]
        for probe in (1, 2):
            slopes = (jnp.einsum('qkgd,nkd->kgqn', q_img[probe], k_img[0], precision=highest) + jnp.einsum('qkgd,nkd->kgqn', q_img[0], k_img[probe], precision=highest)) * score_scale
            weighted = weights * slopes
            row_total = lax.optimization_barrier(jnp.sum(weighted, axis=-1)).transpose(2, 0, 1)
            tangent = jnp.einsum('kgqn,nkd->qkgd', weighted, v_img[0], precision=highest) + jnp.einsum('kgqn,nkd->qkgd', weights, v_img[probe], precision=highest) - row_total[..., None] * main_out
            outs.append(tangent)
        return jnp.stack(outs)
    mixed = lax.map(one_image, (q_float, k_float, v_float))
    mixed = mixed.transpose(1, 0, 2, 3, 4, 5)
    return mixed.reshape(3, TOKENS, HEADS * HD).astype(jnp.bfloat16)

def experts(normed, w_gate, w_up, w_down, routes, route_gain):
    limit = TOKENS // TOK_DEV * CAP
    positions = jnp.arange(limit)

    def step(running, block_index):
        expert = block_index // 2
        hit = routes == expert
        weight = lax.optimization_barrier(jnp.sum(jnp.where(hit, route_gain, 0.0), axis=1))
        chosen = jnp.any(hit, axis=1)
        chosen_count = jnp.sum(chosen.astype(jnp.int32))
        picked = jnp.nonzero(chosen, size=limit, fill_value=0)[0].astype(jnp.int32)
        row_weight = weight[picked] * (positions < chosen_count).astype(jnp.float32)
        tok_rows = normed[:, picked].reshape(3 * limit, D)
        gate_pre = jnp.dot(tok_rows, w_gate[block_index], preferred_element_type=jnp.float32).reshape(3, limit, FH)
        up_pre = jnp.dot(tok_rows, w_up[block_index], preferred_element_type=jnp.float32).reshape(3, limit, FH)
        sigma = jax.nn.sigmoid(gate_pre[0])
        activ = gate_pre[0] * sigma
        slope = sigma * (1.0 + gate_pre[0] * (1.0 - sigma))
        main_hidden = activ * up_pre[0]
        tangent_hidden = slope[None] * gate_pre[1:] * up_pre[0][None] + activ[None] * up_pre[1:]
        hidden = jnp.concatenate([main_hidden[None], tangent_hidden], axis=0).astype(jnp.bfloat16)
        part_out = jnp.dot(hidden.reshape(3 * limit, FH), w_down[block_index], preferred_element_type=jnp.float32).astype(jnp.bfloat16)
        part_out = lax.optimization_barrier(part_out).astype(jnp.float32).reshape(3, limit, D)
        return (running.at[:, picked].add(part_out * row_weight[None, :, None]), None)
    running, _ = lax.scan(step, jnp.zeros((3, TOKENS, D), jnp.float32), jnp.arange(2 * E))
    return running

def reference(queries, key_rows, value_rows, residual, w_out, norm_gain, w_gate, w_up, w_down, routes, route_gain):
    attended = attention(queries, key_rows, value_rows)
    projected = jnp.dot(attended.reshape(3 * TOKENS, HEADS * HD), w_out, preferred_element_type=jnp.float32).reshape(3, TOKENS, D)
    summed = residual.astype(jnp.float32) + projected
    main_sum = summed[0]
    recip = lax.rsqrt(lax.optimization_barrier(jnp.mean(main_sum * main_sum, axis=-1, keepdims=True)) + EPS)
    main_norm = main_sum * recip * norm_gain
    inner = lax.optimization_barrier(jnp.mean(main_sum[None] * summed[1:], axis=-1, keepdims=True))
    tangent_norm = (summed[1:] * recip[None] - main_sum[None] * (recip * recip * recip)[None] * inner) * norm_gain
    normed = jnp.concatenate([main_norm[None], tangent_norm], axis=0).astype(jnp.bfloat16)
    combined = summed + experts(normed, w_gate, w_up, w_down, routes, route_gain)
    layer_out = combined.astype(jnp.bfloat16)
    probe_products = lax.optimization_barrier(jnp.mean(residual[1:].astype(jnp.float32) * combined[1:], axis=-1))
    return (layer_out, probe_products)
```

```python
import math

import jax
import jax.numpy as jnp
from jax import lax
from jax.experimental import pallas as pl
from jax.experimental.pallas import tpu as pltpu
from jax.sharding import PartitionSpec as P

HD = 128
EPS = 1e-06
MESH = pl.DeviceIdType.MESH
BF = jnp.bfloat16
F32 = jnp.float32

SEQ = 16
KEYS = 128
TOK = 16
D = 4096
LANES = 256
FOLD = D // LANES
CHIPS = 64
SLOTS = 3
VECS = 3 * SLOTS
FH = 768
HALF = 32
ROWS = HALF * VECS
FT = 256
NT = 512


def dot(a, b):
    return jnp.dot(a, b, preferred_element_type=F32)


def dot_nt(a, b):
    return lax.dot_general(a, b, (((1,), (1,)), ((), ())), preferred_element_type=F32)


def attend_kernel(
    q_ref,
    k_ref,
    v_ref,
    res_ref,
    gain_ref,
    wo_ref,
    wg_ref,
    wu_ref,
    wd_ref,
    summed_ref,
    normed_ref,
    sg_ref,
    su_ref,
    sd_ref,
    kb,
    vb,
    qs,
    qc,
    scores,
    slopes,
    att,
    wo,
    sib_send,
    sib_recv,
    own,
    y_send,
    y_recv,
    stage,
    local_sem,
    w_send,
    w_recv,
    k_send,
    k_recv,
    v_send,
    v_recv,
    s_send,
    s_recv,
    ys_send,
    ys_recv,
):
    seq = lax.axis_index("seq")
    ex = lax.axis_index("exp")
    z, x = lax.div(seq, 4), lax.rem(seq, 4)
    y, core = lax.div(ex, 2), lax.rem(ex, 2)
    sibling = (seq, y * 2 + (1 - core))
    scale = 1.0 / math.sqrt(HD)

    def z_peer(d):
        return (lax.rem(z + d, 4) * 4 + x, ex)

    def x_peer(d):
        return (z * 4 + lax.rem(x + d, 4), ex)

    def y_peer(d):
        return (seq, lax.rem(y + d, 4) * 2 + core)

    wo_copy = pltpu.make_async_copy(wo_ref, wo, local_sem)
    wo_copy.start()

    barrier = pltpu.get_barrier_semaphore()
    pl.semaphore_signal(barrier, inc=1, device_id=sibling, device_id_type=MESH)
    for d in (1, 2, 3):
        for peer in (z_peer(d), x_peer(d), y_peer(d)):
            pl.semaphore_signal(barrier, inc=1, device_id=peer, device_id_type=MESH)
    kb[seq] = k_ref[...]
    vb[seq] = v_ref[...]
    pl.semaphore_wait(barrier, 10)

    def remote(src, dst, ssem, rsem, peer):
        return pltpu.make_async_remote_copy(
            src_ref=src, dst_ref=dst, send_sem=ssem, recv_sem=rsem, device_id=peer, device_id_type=MESH
        )

    def k_copy(origin, number, peer):
        return remote(kb.at[origin], kb.at[origin], k_send.at[number], k_recv.at[origin], peer)

    def v_copy(origin, number, peer):
        return remote(vb.at[origin], vb.at[origin], v_send.at[number], v_recv.at[origin], peer)

    order = (1, 3, 2)
    for d in order:
        k_copy(seq, d - 1, z_peer(d)).start()
        v_copy(seq, d - 1, x_peer(d)).start()
    for d in order:
        k_copy(seq, 3 + d - 1, x_peer(d)).start()
        v_copy(seq, 3 + d - 1, z_peer(d)).start()
    weight_copies = [
        remote(wg_ref, sg_ref, w_send.at[0], w_recv.at[0], sibling),
        remote(wu_ref, su_ref, w_send.at[1], w_recv.at[1], sibling),
        remote(wd_ref, sd_ref, w_send.at[2], w_recv.at[2], sibling),
    ]
    for copy in weight_copies:
        copy.start()

    for h in range(4):
        for s in range(3):
            qs[s, h * 128 : (h + 1) * 128, :] = q_ref[s, :, h * 128 : (h + 1) * 128]
    for t in (1, 2):
        qc[t - 1, :, :HD] = qs[t]
        qc[t - 1, :, HD:] = qs[0]

    for d in order:
        from_z = lax.rem(z + d, 4) * 4 + x
        from_x = z * 4 + lax.rem(x + d, 4)
        k_copy(from_z, 0, z_peer(d)).wait_recv()
        for e in order:
            k_copy(from_z, 3 * (d + 1) + e - 1, x_peer(e)).start()
        v_copy(from_x, 0, x_peer(d)).wait_recv()
        for e in order:
            v_copy(from_x, 3 * (d + 1) + e - 1, z_peer(e)).start()

    for dz in (0,) + order:
        c = lax.rem(z + dz, 4)
        for e in (1, 2, 3):
            k_copy(c * 4 + lax.rem(x + e, 4), 0, x_peer(e)).wait_recv()
        kc = kb[pl.ds(c * 4, 4)]
        k0 = kc[:, 0].reshape(512, HD)
        scores[c] = dot_nt(qs[0], k0) * scale
        for t in (1, 2):
            kt = kc[:, t].reshape(512, HD)
            slopes[t - 1, c] = dot_nt(qc[t - 1], jnp.concatenate([k0, kt], axis=1)) * scale

    for d in order:
        for e in (0, 1, 2, 3):
            origin = lax.rem(z + d, 4) * 4 + lax.rem(x + e, 4)
            v_copy(origin, 0, z_peer(d)).wait_recv()

    def head(h, carry):
        rows = pl.ds(pl.multiple_of(h * 128, 128), 128)
        top = jnp.max(scores[0, rows, :], axis=1, keepdims=True)
        for c in (1, 2, 3):
            top = jnp.maximum(top, jnp.max(scores[c, rows, :], axis=1, keepdims=True))
        total = jnp.zeros((128, 1), F32)
        r1 = jnp.zeros((128, 1), F32)
        r2 = jnp.zeros((128, 1), F32)
        acc = jnp.zeros((128, 3 * HD), F32)
        mixed = jnp.zeros((256, HD), F32)
        for c in range(4):
            p = jnp.exp(scores[c, rows, :] - top).astype(BF)
            pf = p.astype(F32)
            w1 = (pf * slopes[0, c, rows, :]).astype(BF)
            w2 = (pf * slopes[1, c, rows, :]).astype(BF)
            total += jnp.sum(pf, axis=1, keepdims=True)
            r1 += jnp.sum(w1.astype(F32), axis=1, keepdims=True)
            r2 += jnp.sum(w2.astype(F32), axis=1, keepdims=True)
            v0 = vb[4 * c : 4 * c + 4, 0].reshape(512, HD)
            v1 = vb[4 * c : 4 * c + 4, 1].reshape(512, HD)
            v2 = vb[4 * c : 4 * c + 4, 2].reshape(512, HD)
            acc += dot(p, jnp.concatenate([v0, v1, v2], axis=1))
            mixed += dot(jnp.concatenate([w1, w2], axis=0), v0)
        inv = 1.0 / total
        main = acc[:, :HD] * inv
        t1 = (mixed[:128] + acc[:, HD : 2 * HD]) * inv - (r1 * inv) * main
        t2 = (mixed[128:] + acc[:, 2 * HD :]) * inv - (r2 * inv) * main
        att[0, :, rows] = main.astype(BF)
        att[1, :, rows] = t1.astype(BF)
        att[2, :, rows] = t2.astype(BF)
        return carry

    lax.fori_loop(0, 4, head, 0)

    wo_copy.wait()

    def block_rows(parity):
        parts = []
        for d in range(4):
            j = lax.rem(y + d, 4) * 2 + parity
            rows = pl.ds(pl.multiple_of(j * TOK, TOK), TOK)
            for s in range(3):
                parts.append(att[s, rows, :])
        return jnp.concatenate(parts, axis=0)

    sib_rows = block_rows(1 - core)
    sib_copies = []
    for n in range(4):
        sib_send[n] = dot(sib_rows, wo[:, n * 1024 : (n + 1) * 1024]).astype(BF)
        copy = remote(sib_send.at[n], sib_recv.at[n], s_send.at[n], s_recv.at[n], sibling)
        copy.start()
        sib_copies.append(copy)
    own_rows = block_rows(core)
    y_copies = []
    for n in range(4):
        lanes = slice(n * 1024, (n + 1) * 1024)
        product = dot(own_rows, wo[:, lanes])
        sib_copies[n].wait_recv()
        both = product + sib_recv[n].astype(F32)
        own[:, lanes] = both[:48]
        for d in order:
            y_send[n, d - 1] = both[48 * d : 48 * (d + 1)].astype(BF)
            copy = remote(
                y_send.at[n, d - 1], y_recv.at[n, d - 1], ys_send.at[n, d - 1], ys_recv.at[n, d - 1], y_peer(d)
            )
            copy.start()
            y_copies.append(copy)
    for n in range(4):
        for d in (1, 2, 3):
            y_copies[n * 3 + order.index(d)].wait_recv()
        lanes = slice(n * 1024, (n + 1) * 1024)
        part = own[:, lanes]
        for d in (1, 2, 3):
            part += y_recv[n, d - 1].astype(F32)
        for s in range(3):
            summed_ref[s, :, lanes] = part[16 * s : 16 * (s + 1)] + res_ref[s, :, lanes].astype(F32)

    main_sum = summed_ref[0]
    recip = lax.rsqrt(jnp.mean(main_sum * main_sum, axis=-1, keepdims=True) + EPS)
    normed_ref[TOK] = jnp.zeros((3, FOLD, LANES), BF)
    for s in range(3):
        if s == 0:
            rows = main_sum * recip * gain_ref[...]
        else:
            inner = jnp.mean(main_sum * summed_ref[s], axis=-1, keepdims=True)
            rows = (summed_ref[s] * recip - main_sum * (recip * recip * recip * inner)) * gain_ref[...]
        for c in range(FOLD):
            for half in (0, 128):
                first = c * LANES + half
                stage[half // 128, pl.ds(c, TOK, stride=FOLD), :] = rows[:, first : first + 128]
        for half in (0, 1):
            normed_ref[:TOK, s, :, half * 128 : half * 128 + 128] = (
                stage[half].reshape(TOK, FOLD, 128).astype(BF)
            )

    for d in order:
        k_copy(seq, d - 1, z_peer(d)).wait_send()
        v_copy(seq, d - 1, x_peer(d)).wait_send()
    for number in range(3, 15):
        k_copy(seq, number, x_peer(1)).wait_send()
        v_copy(seq, number, z_peer(1)).wait_send()
    for copy in sib_copies + y_copies:
        copy.wait_send()
    for copy in weight_copies:
        copy.wait()


def attend(q, k, v, residual, gain, w_out, w_gate, w_up, w_down):
    vmem = pl.BlockSpec(memory_space=pltpu.VMEM)
    anywhere = pl.BlockSpec(memory_space=pl.ANY)
    dma = pltpu.SemaphoreType.DMA
    return pl.pallas_call(
        attend_kernel,
        out_shape=(
            jax.ShapeDtypeStruct((3, TOK, D), F32),
            jax.ShapeDtypeStruct((TOK + 1, 3, FOLD, LANES), BF),
            jax.ShapeDtypeStruct(w_gate.shape, BF),
            jax.ShapeDtypeStruct(w_up.shape, BF),
            jax.ShapeDtypeStruct(w_down.shape, BF),
        ),
        in_specs=[vmem] * 5 + [anywhere] * 4,
        out_specs=(vmem, vmem, anywhere, anywhere, anywhere),
        scratch_shapes=[
            pltpu.VMEM((SEQ, 3, KEYS, HD), BF),
            pltpu.VMEM((SEQ, 3, KEYS, HD), BF),
            pltpu.VMEM((3, 512, HD), BF),
            pltpu.VMEM((2, 512, 2 * HD), BF),
            pltpu.VMEM((4, 512, 512), F32),
            pltpu.VMEM((2, 4, 512, 512), F32),
            pltpu.VMEM((3, KEYS, 512), BF),
            pltpu.VMEM((512, D), BF),
            pltpu.VMEM((4, 192, 1024), BF),
            pltpu.VMEM((4, 192, 1024), BF),
            pltpu.VMEM((48, D), F32),
            pltpu.VMEM((4, 3, 48, 1024), BF),
            pltpu.VMEM((4, 3, 48, 1024), BF),
            pltpu.VMEM((2, TOK * FOLD, 128), F32),
            dma,
            dma((3,)),
            dma((3,)),
            dma((15,)),
            dma((SEQ,)),
            dma((15,)),
            dma((SEQ,)),
            dma((4,)),
            dma((4,)),
            dma((4, 3)),
            dma((4, 3)),
        ],
        compiler_params=pltpu.CompilerParams(
            collective_id=0, has_side_effects=True, vmem_limit_bytes=50 * 2**20
        ),
        name="attend",
    )(q, k, v, residual, gain, w_out, w_gate, w_up, w_down)


def expert_kernel(
    tok_ref,
    pos_ref,
    gain_ref,
    normed_ref,
    summed_ref,
    res_ref,
    wg_ref,
    wu_ref,
    wd_ref,
    sg_ref,
    su_ref,
    sd_ref,
    out_ref,
    probe_ref,
    send,
    recv,
    back,
    rows_in,
    hidden,
    stage,
    wgu,
    wdn,
    total,
    send_sem,
    recv_sem,
    bsend_sem,
    brecv_sem,
    gu_sem,
    dn_sem,
):
    seq = lax.axis_index("seq")
    ex = lax.axis_index("exp")
    z, x = lax.div(seq, 4), lax.rem(seq, 4)
    y, core = lax.div(ex, 2), lax.rem(ex, 2)

    def peer(i, sign):
        iz = lax.div(i, 16)
        dz = lax.rem(iz, 2) * 2 + lax.div(iz, 2)
        dx = lax.rem(lax.div(i, 4), 4)
        dy = lax.rem(i, 4)
        if sign < 0:
            dz, dx, dy = 4 - dz, 4 - dx, 4 - dy
        return (lax.rem(z + dz, 4) * 4 + lax.rem(x + dx, 4), lax.rem(y + dy, 4) * 2 + core)

    def out_copy(i):
        return pltpu.make_async_remote_copy(
            src_ref=send.at[i],
            dst_ref=recv.at[i],
            send_sem=send_sem.at[i],
            recv_sem=recv_sem.at[i],
            device_id=peer(i, 1),
            device_id_type=MESH,
        )

    def back_copy(i):
        return pltpu.make_async_remote_copy(
            src_ref=recv.at[i],
            dst_ref=back.at[i],
            send_sem=bsend_sem.at[i],
            recv_sem=brecv_sem.at[i],
            device_id=peer(i, -1),
            device_id_type=MESH,
        )

    def gu_start(t, slot):
        lanes = pl.ds(pl.multiple_of(lax.rem(t, 3) * FT, FT), FT)

        def go(gate, up):
            pltpu.make_async_copy(gate.at[0, :, lanes], wgu.at[slot, 0], gu_sem.at[slot, 0]).start()
            pltpu.make_async_copy(up.at[0, :, lanes], wgu.at[slot, 1], gu_sem.at[slot, 1]).start()

        @pl.when(t < 3)
        def _():
            go(wg_ref, wu_ref)

        @pl.when(t >= 3)
        def _():
            go(sg_ref, su_ref)

    def gu_wait(slot):
        pltpu.make_async_copy(wg_ref.at[0, :, :FT], wgu.at[slot, 0], gu_sem.at[slot, 0]).wait()
        pltpu.make_async_copy(wu_ref.at[0, :, :FT], wgu.at[slot, 1], gu_sem.at[slot, 1]).wait()

    def dn_start(n, slot):
        lanes = pl.ds(pl.multiple_of(n * NT, NT), NT)
        pltpu.make_async_copy(wd_ref.at[0, :, lanes], wdn.at[slot, 0], dn_sem.at[slot, 0]).start()
        pltpu.make_async_copy(sd_ref.at[0, :, lanes], wdn.at[slot, 1], dn_sem.at[slot, 1]).start()

    def dn_wait(slot):
        pltpu.make_async_copy(wd_ref.at[0, :, :NT], wdn.at[slot, 0], dn_sem.at[slot, 0]).wait()
        pltpu.make_async_copy(sd_ref.at[0, :, :NT], wdn.at[slot, 1], dn_sem.at[slot, 1]).wait()

    barrier = pltpu.get_barrier_semaphore()

    def greet(i, carry):
        pl.semaphore_signal(barrier, inc=1, device_id=peer(i, 1), device_id_type=MESH)
        return carry

    lax.fori_loop(1, CHIPS, greet, 0)
    gu_start(0, 0)

    for slot in range(SLOTS):
        token = tok_ref[slot]
        for s in range(3):
            recv[0, s * SLOTS + slot] = normed_ref[token, s]
    pl.semaphore_wait(barrier, CHIPS - 1)

    def dispatch(i, carry):
        for slot in range(SLOTS):
            token = tok_ref[i * SLOTS + slot]
            for s in range(3):
                send[i, s * SLOTS + slot] = normed_ref[token, s]
        out_copy(i).start()
        return carry

    lax.fori_loop(1, CHIPS, dispatch, 0)

    def chunk(g, carry):
        def arrive(i, carry):
            out_copy(i).wait_recv()
            return carry

        lax.fori_loop(jnp.where(g == 0, 1, HALF), (g + 1) * HALF, arrive, 0)

        def unfold(m, carry):
            v, part = lax.div(m, 2), lax.rem(m, 2)
            tiles = recv[pl.ds(g * HALF + part * 16, 16), v].astype(F32).reshape(16 * FOLD, LANES)
            for half in (0, 1):
                stage[half, : 16 * FOLD] = tiles[:, half * 128 : half * 128 + 128]
            row = pl.multiple_of(v * HALF + part * 16, 16)
            for c in range(FOLD):
                for half in (0, 1):
                    first = c * LANES + half * 128
                    rows_in[pl.ds(row, 16), first : first + 128] = stage[
                        half, pl.ds(c, 16, stride=FOLD), :
                    ].astype(BF)
            return carry

        lax.fori_loop(0, 2 * VECS, unfold, 0)

        def gate_up(t, carry):
            slot = lax.rem(t, 2)

            @pl.when(t < 5)
            def _():
                gu_start(t + 1, 1 - slot)

            @pl.when(t == 5)
            def _():
                dn_start(0, 0)

            gu_wait(slot)
            g_all = dot(rows_in[...], wgu[slot, 0])
            u_all = dot(rows_in[...], wgu[slot, 1])
            n = SLOTS * HALF
            g0, u0 = g_all[:n], u_all[:n]
            sigma = 1.0 / (1.0 + jnp.exp(-g0))
            active = g0 * sigma
            slope = sigma * (1.0 + g0 * (1.0 - sigma)) * u0
            lanes = pl.ds(pl.multiple_of(t * FT, FT), FT)
            hidden[:n, lanes] = (active * u0).astype(BF)
            hidden[n : 2 * n, lanes] = (slope * g_all[n : 2 * n] + active * u_all[n : 2 * n]).astype(BF)
            hidden[2 * n :, lanes] = (slope * g_all[2 * n :] + active * u_all[2 * n :]).astype(BF)
            return carry

        lax.fori_loop(0, 6, gate_up, 0)

        def down(n, carry):
            slot = lax.rem(n, 2)

            @pl.when(n < 7)
            def _():
                dn_start(n + 1, 1 - slot)

            @pl.when((n == 7) & (g == 0))
            def _():
                gu_start(0, 0)

            dn_wait(slot)
            part = dot(hidden[:, :FH], wdn[slot, 0]) + dot(hidden[:, FH:], wdn[slot, 1])
            for q in range(NT // LANES):
                for half in (0, 1):
                    first = q * LANES + half * 128
                    stage[half, pl.ds(n * (NT // LANES) + q, ROWS, stride=FOLD), :] = part[
                        :, first : first + 128
                    ]
            return carry

        lax.fori_loop(0, D // NT, down, 0)

        def fold(v, carry):
            for part in (0, 1):
                row = pl.multiple_of((v * HALF + part * 16) * FOLD, 256)
                for half in (0, 1):
                    recv[pl.ds(g * HALF + part * 16, 16), v, :, half * 128 : half * 128 + 128] = (
                        stage[half, pl.ds(row, 16 * FOLD), :].reshape(16, FOLD, 128).astype(BF)
                    )
            return carry

        lax.fori_loop(0, VECS, fold, 0)

        def give_back(i, carry):
            back_copy(i).start()
            return carry

        lax.fori_loop(jnp.where(g == 0, 1, HALF), (g + 1) * HALF, give_back, 0)
        return carry

    lax.fori_loop(0, 2, chunk, 0)
    back[0] = recv[0]

    def collect(i, carry):
        out_copy(i).wait_send()
        back_copy(i).wait()
        return carry

    lax.fori_loop(1, CHIPS, collect, 0)

    def combine(tok, carry):
        sums = [jnp.zeros((FOLD, LANES), F32) for _ in range(3)]
        for r in range(8):
            where = pos_ref[tok * 8 + r]
            chip, slot = lax.div(where, SLOTS), lax.rem(where, SLOTS)
            weight = gain_ref[tok * 8 + r]
            for s in range(3):
                sums[s] += weight * back[chip, s * SLOTS + slot].astype(F32)
        row = pl.ds(pl.multiple_of(tok * FOLD, FOLD), FOLD)
        for s in range(3):
            for half in (0, 1):
                total[s, half, row, :] = sums[s][:, half * 128 : half * 128 + 128]
        return carry

    lax.fori_loop(0, TOK, combine, 0)
    probes = [jnp.zeros((TOK, 128), F32) for _ in range(2)]
    for c in range(FOLD):
        for half in (0, 1):
            first = c * LANES + half * 128
            lanes = slice(first, first + 128)
            for s in range(3):
                value = summed_ref[s, :, lanes] + total[s, half, pl.ds(c, TOK, stride=FOLD), :]
                out_ref[s, :, lanes] = value.astype(BF)
                if s:
                    probes[s - 1] += value * res_ref[s, :, lanes].astype(F32)
    for t in range(2):
        mean = jnp.sum(probes[t], axis=1, keepdims=True) * (1.0 / D)
        probe_ref[t] = jnp.broadcast_to(mean, (TOK, 128))


def experts(tok, pos, gains, normed, summed, residual, wg, wu, wd, sg, su, sd):
    smem = pl.BlockSpec(memory_space=pltpu.SMEM)
    vmem = pl.BlockSpec(memory_space=pltpu.VMEM)
    anywhere = pl.BlockSpec(memory_space=pl.ANY)
    dma = pltpu.SemaphoreType.DMA
    tiles = (CHIPS, VECS, FOLD, LANES)
    return pl.pallas_call(
        expert_kernel,
        out_shape=(
            jax.ShapeDtypeStruct((3, TOK, D), BF),
            jax.ShapeDtypeStruct((2, TOK, 128), F32),
        ),
        in_specs=[smem] * 3 + [vmem] * 3 + [anywhere] * 6,
        out_specs=(vmem, vmem),
        scratch_shapes=[
            pltpu.VMEM(tiles, BF),
            pltpu.VMEM(tiles, BF),
            pltpu.VMEM(tiles, BF),
            pltpu.VMEM((ROWS, D), BF),
            pltpu.VMEM((ROWS, 2 * FH), BF),
            pltpu.VMEM((2, ROWS * FOLD, 128), F32),
            pltpu.VMEM((2, 2, D, FT), BF),
            pltpu.VMEM((2, 2, FH, NT), BF),
            pltpu.VMEM((3, 2, TOK * FOLD, 128), F32),
            dma((CHIPS,)),
            dma((CHIPS,)),
            dma((CHIPS,)),
            dma((CHIPS,)),
            dma((2, 2)),
            dma((2, 2)),
        ],
        compiler_params=pltpu.CompilerParams(
            collective_id=1, has_side_effects=True, vmem_limit_bytes=56 * 2**20
        ),
        name="experts",
    )(tok, pos, gains, normed, summed, residual, wg, wu, wd, sg, su, sd)


def plan(routes):
    seq, ex = lax.axis_index("seq"), lax.axis_index("exp")
    z, x, y = seq // 4, seq % 4, ex // 2
    flat = routes.reshape(-1)
    count = flat.shape[0]
    order = jnp.arange(count)
    earlier = (flat[:, None] == flat[None, :]) & (order[None, :] < order[:, None])
    slot = jnp.sum(earlier.astype(jnp.int32), axis=1)
    dz = (flat // 16 - z) % 4
    dx = (flat // 4 % 4 - x) % 4
    dy = (flat % 4 - y) % 4
    number = (dz % 2 * 2 + dz // 2) * 16 + dx * 4 + dy
    pos = number * SLOTS + slot
    hit = (jnp.arange(CHIPS * SLOTS)[:, None] == pos[None, :]).astype(jnp.int32)
    tok = TOK + jnp.sum(hit * (order // 8 - TOK)[None, :], axis=1)
    return tok.astype(jnp.int32), pos.astype(jnp.int32)


def shards(
    queries,
    key_rows,
    value_rows,
    residual,
    w_out,
    norm_gain,
    w_gate,
    w_up,
    w_down,
    routes,
    route_gain,
):
    tok, pos = plan(routes)
    summed, normed, sg, su, sd = attend(
        queries, key_rows, value_rows, residual, norm_gain[None, :], w_out, w_gate, w_up, w_down
    )
    layer_out, probes = experts(
        tok, pos, route_gain.reshape(-1), normed, summed, residual, w_gate, w_up, w_down, sg, su, sd
    )
    return layer_out, probes[:, :, 0]


def solution(mesh):
    return jax.shard_map(
        shards,
        mesh=mesh,
        in_specs=(
            P(None, "seq", "exp"),
            P(None, "seq", "exp"),
            P(None, "seq", "exp"),
            P(None, ("seq", "exp"), None),
            P("exp", None),
            P(),
            P(("seq", "exp"), None, None),
            P(("seq", "exp"), None, None),
            P(("seq", "exp"), None, None),
            P(("seq", "exp"), None),
            P(("seq", "exp"), None),
        ),
        out_specs=(P(None, ("seq", "exp"), None), P(None, ("seq", "exp"))),
        check_vma=False,
    )
```

```python
import math

import jax
import jax.numpy as jnp
from jax import lax
from jax.experimental import pallas as pl
from jax.experimental.pallas import tpu as pltpu
from jax.sharding import PartitionSpec as P

HD = 128
EPS = 1e-06
MESH = pl.DeviceIdType.MESH
BF = jnp.bfloat16
F32 = jnp.float32

SEQ = 16
KEYS = 128
TOK = 16
D = 4096
LANES = 256
FOLD = D // LANES
CHIPS = 64
SLOTS = 3
VECS = 3 * SLOTS
FH = 768
HALF = 32
ROWS = HALF * VECS
FT = 256
WINDOW = 24
NT = 512


def dot(a, b):
    return jnp.dot(a, b, preferred_element_type=F32)


def dot_nt(a, b):
    return lax.dot_general(a, b, (((1,), (1,)), ((), ())), preferred_element_type=F32)


def layer_kernel(
    tok_ref,
    pos_ref,
    gains_ref,
    q_hbm,
    k_hbm,
    v_hbm,
    res_hbm,
    gain_hbm,
    wo_hbm,
    wg_ref,
    wu_ref,
    wd_ref,
    out_ref,
    probe_ref,
    sg_ref,
    su_ref,
    sd_ref,
    q_ref,
    res_ref,
    gain_ref,
    summed_ref,
    normed_ref,
    kb,
    vb,
    sib_send,
    sib_recv,
    own,
    y_send,
    y_recv,
    send,
    recv,
    back,
    total,
    in_sem,
    w_send,
    w_recv,
    k_send,
    k_recv,
    v_send,
    v_recv,
    s_send,
    s_recv,
    ys_send,
    ys_recv,
    send_sem,
    recv_sem,
    bsend_sem,
    brecv_sem,
    gu_sem,
    dn_sem,
):
    seq = lax.axis_index("seq")
    ex = lax.axis_index("exp")
    z, x = lax.div(seq, 4), lax.rem(seq, 4)
    y, core = lax.div(ex, 2), lax.rem(ex, 2)
    sibling = (seq, y * 2 + (1 - core))
    scale = 1.0 / math.sqrt(HD)
    order = (1, 3, 2)

    def z_peer(d):
        return (lax.rem(z + d, 4) * 4 + x, ex)

    def x_peer(d):
        return (z * 4 + lax.rem(x + d, 4), ex)

    def y_peer(d):
        return (seq, lax.rem(y + d, 4) * 2 + core)

    def peer(i, sign):
        iz = lax.div(i, 16)
        dz = lax.rem(iz, 2) * 2 + lax.div(iz, 2)
        dx = lax.rem(lax.div(i, 4), 4)
        dy = lax.rem(i, 4)
        if sign < 0:
            dz, dx, dy = 4 - dz, 4 - dx, 4 - dy
        return (lax.rem(z + dz, 4) * 4 + lax.rem(x + dx, 4), lax.rem(y + dy, 4) * 2 + core)

    def remote(src, dst, ssem, rsem, peer):
        return pltpu.make_async_remote_copy(
            src_ref=src, dst_ref=dst, send_sem=ssem, recv_sem=rsem, device_id=peer, device_id_type=MESH
        )

    barrier = pltpu.get_barrier_semaphore()
    pl.semaphore_signal(barrier, inc=1, device_id=sibling, device_id_type=MESH)

    def greet(i, carry):
        pl.semaphore_signal(barrier, inc=1, device_id=peer(i, 1), device_id_type=MESH)
        return carry

    lax.fori_loop(1, CHIPS, greet, 0)
    k_in = pltpu.make_async_copy(k_hbm, kb.at[seq], in_sem.at[0])
    v_in = pltpu.make_async_copy(v_hbm, vb.at[seq], in_sem.at[1])
    q_in = pltpu.make_async_copy(q_hbm, q_ref, in_sem.at[2])
    res_in = pltpu.make_async_copy(res_hbm, res_ref, in_sem.at[3])
    gain_in = pltpu.make_async_copy(gain_hbm, gain_ref, in_sem.at[4])
    for copy in (k_in, v_in, q_in, res_in, gain_in):
        copy.start()
    k_in.wait()
    v_in.wait()
    pl.semaphore_wait(barrier, CHIPS)

    weight_copies = [
        remote(wg_ref, sg_ref, w_send.at[0], w_recv.at[0], sibling),
        remote(wu_ref, su_ref, w_send.at[1], w_recv.at[1], sibling),
        remote(wd_ref, sd_ref, w_send.at[2], w_recv.at[2], sibling),
    ]

    def k_copy(origin, number, peer):
        return remote(kb.at[origin], kb.at[origin], k_send.at[number], k_recv.at[origin], peer)

    def v_copy(origin, number, peer):
        return remote(vb.at[origin], vb.at[origin], v_send.at[number], v_recv.at[origin], peer)

    for d in order:
        k_copy(seq, d - 1, z_peer(d)).start()
        v_copy(seq, d - 1, x_peer(d)).start()
    for d in order:
        k_copy(seq, 3 + d - 1, x_peer(d)).start()
        v_copy(seq, 3 + d - 1, z_peer(d)).start()
    for copy in weight_copies:
        copy.start()

    def attend(qs, qc, scores, slopes, att, wo):
        wo_copy = pltpu.make_async_copy(wo_hbm, wo, in_sem.at[5])
        wo_copy.start()
        q_in.wait()
        for h in range(4):
            for s in range(3):
                qs[s, h * 128 : (h + 1) * 128, :] = q_ref[s, :, h * 128 : (h + 1) * 128]
        for t in (1, 2):
            qc[t - 1, :, :HD] = qs[t]
            qc[t - 1, :, HD:] = qs[0]

        for d in order:
            from_z = lax.rem(z + d, 4) * 4 + x
            from_x = z * 4 + lax.rem(x + d, 4)
            k_copy(from_z, 0, z_peer(d)).wait_recv()
            for e in order:
                k_copy(from_z, 3 * (d + 1) + e - 1, x_peer(e)).start()
            v_copy(from_x, 0, x_peer(d)).wait_recv()
            for e in order:
                v_copy(from_x, 3 * (d + 1) + e - 1, z_peer(e)).start()

        for dz in (0,) + order:
            c = lax.rem(z + dz, 4)
            for e in (1, 2, 3):
                k_copy(c * 4 + lax.rem(x + e, 4), 0, x_peer(e)).wait_recv()
            kc = kb[pl.ds(c * 4, 4)]
            k0 = kc[:, 0].reshape(512, HD)
            scores[c] = dot_nt(qs[0], k0) * scale
            for t in (1, 2):
                kt = kc[:, t].reshape(512, HD)
                slopes[t - 1, c] = dot_nt(qc[t - 1], jnp.concatenate([k0, kt], axis=1)) * scale

        for d in order:
            for e in (0, 1, 2, 3):
                origin = lax.rem(z + d, 4) * 4 + lax.rem(x + e, 4)
                v_copy(origin, 0, z_peer(d)).wait_recv()

        def head(h, carry):
            rows = pl.ds(pl.multiple_of(h * 128, 128), 128)
            top = jnp.max(scores[0, rows, :], axis=1, keepdims=True)
            for c in (1, 2, 3):
                top = jnp.maximum(top, jnp.max(scores[c, rows, :], axis=1, keepdims=True))
            norm = jnp.zeros((128, 1), F32)
            r1 = jnp.zeros((128, 1), F32)
            r2 = jnp.zeros((128, 1), F32)
            acc = jnp.zeros((128, 3 * HD), F32)
            mixed = jnp.zeros((256, HD), F32)
            for c in range(4):
                p = jnp.exp(scores[c, rows, :] - top).astype(BF)
                pf = p.astype(F32)
                w1 = (pf * slopes[0, c, rows, :]).astype(BF)
                w2 = (pf * slopes[1, c, rows, :]).astype(BF)
                norm += jnp.sum(pf, axis=1, keepdims=True)
                r1 += jnp.sum(w1.astype(F32), axis=1, keepdims=True)
                r2 += jnp.sum(w2.astype(F32), axis=1, keepdims=True)
                v0 = vb[4 * c : 4 * c + 4, 0].reshape(512, HD)
                v1 = vb[4 * c : 4 * c + 4, 1].reshape(512, HD)
                v2 = vb[4 * c : 4 * c + 4, 2].reshape(512, HD)
                acc += dot(p, jnp.concatenate([v0, v1, v2], axis=1))
                mixed += dot(jnp.concatenate([w1, w2], axis=0), v0)
            inv = 1.0 / norm
            main = acc[:, :HD] * inv
            t1 = (mixed[:128] + acc[:, HD : 2 * HD]) * inv - (r1 * inv) * main
            t2 = (mixed[128:] + acc[:, 2 * HD :]) * inv - (r2 * inv) * main
            att[0, :, rows] = main.astype(BF)
            att[1, :, rows] = t1.astype(BF)
            att[2, :, rows] = t2.astype(BF)
            return carry

        lax.fori_loop(0, 4, head, 0)

        wo_copy.wait()

        def block_rows(parity):
            parts = []
            for d in range(4):
                j = lax.rem(y + d, 4) * 2 + parity
                rows = pl.ds(pl.multiple_of(j * TOK, TOK), TOK)
                for s in range(3):
                    parts.append(att[s, rows, :])
            return jnp.concatenate(parts, axis=0)

        sib_rows = block_rows(1 - core)
        sib_copies = []
        for n in range(4):
            sib_send[n] = dot(sib_rows, wo[:, n * 1024 : (n + 1) * 1024]).astype(BF)
            copy = remote(sib_send.at[n], sib_recv.at[n], s_send.at[n], s_recv.at[n], sibling)
            copy.start()
            sib_copies.append(copy)
        own_rows = block_rows(core)
        y_copies = []
        for n in range(4):
            lanes = slice(n * 1024, (n + 1) * 1024)
            product = dot(own_rows, wo[:, lanes])
            sib_copies[n].wait_recv()
            both = product + sib_recv[n].astype(F32)
            own[:, lanes] = both[:48]
            for d in order:
                y_send[n, d - 1] = both[48 * d : 48 * (d + 1)].astype(BF)
                copy = remote(
                    y_send.at[n, d - 1], y_recv.at[n, d - 1], ys_send.at[n, d - 1], ys_recv.at[n, d - 1], y_peer(d)
                )
                copy.start()
                y_copies.append(copy)
        res_in.wait()
        for n in range(4):
            for d in (1, 2, 3):
                y_copies[n * 3 + order.index(d)].wait_recv()
            lanes = slice(n * 1024, (n + 1) * 1024)
            part = own[:, lanes]
            for d in (1, 2, 3):
                part += y_recv[n, d - 1].astype(F32)
            for s in range(3):
                summed_ref[s, :, lanes] = part[16 * s : 16 * (s + 1)] + res_ref[s, :, lanes].astype(F32)
        for d in order:
            k_copy(seq, d - 1, z_peer(d)).wait_send()
            v_copy(seq, d - 1, x_peer(d)).wait_send()
        for number in range(3, 15):
            k_copy(seq, number, x_peer(1)).wait_send()
            v_copy(seq, number, z_peer(1)).wait_send()
        for copy in sib_copies + y_copies:
            copy.wait_send()

    pl.run_scoped(
        attend,
        pltpu.VMEM((3, 512, HD), BF),
        pltpu.VMEM((2, 512, 2 * HD), BF),
        pltpu.VMEM((4, 512, 512), F32),
        pltpu.VMEM((2, 4, 512, 512), F32),
        pltpu.VMEM((3, KEYS, 512), BF),
        pltpu.VMEM((512, D), BF),
    )

    def out_copy(i):
        return remote(send.at[i], recv.at[i], send_sem.at[i], recv_sem.at[i], peer(i, 1))

    def back_copy(i):
        return remote(recv.at[i], back.at[i], bsend_sem.at[i], brecv_sem.at[i], peer(i, -1))

    def moe(rows_in, hidden, stage, wgu, wdn):
        def gu_start(t, slot):
            lanes = pl.ds(pl.multiple_of(lax.rem(t, 3) * FT, FT), FT)

            def go(gate, up):
                pltpu.make_async_copy(gate.at[0, :, lanes], wgu.at[slot, 0], gu_sem.at[slot, 0]).start()
                pltpu.make_async_copy(up.at[0, :, lanes], wgu.at[slot, 1], gu_sem.at[slot, 1]).start()

            @pl.when(t < 3)
            def _():
                go(wg_ref, wu_ref)

            @pl.when(t >= 3)
            def _():
                go(sg_ref, su_ref)

        def gu_wait(slot):
            pltpu.make_async_copy(wg_ref.at[0, :, :FT], wgu.at[slot, 0], gu_sem.at[slot, 0]).wait()
            pltpu.make_async_copy(wu_ref.at[0, :, :FT], wgu.at[slot, 1], gu_sem.at[slot, 1]).wait()

        def dn_start(n, slot):
            lanes = pl.ds(pl.multiple_of(n * NT, NT), NT)
            pltpu.make_async_copy(wd_ref.at[0, :, lanes], wdn.at[slot, 0], dn_sem.at[slot, 0]).start()
            pltpu.make_async_copy(sd_ref.at[0, :, lanes], wdn.at[slot, 1], dn_sem.at[slot, 1]).start()

        def dn_wait(slot):
            pltpu.make_async_copy(wd_ref.at[0, :, :NT], wdn.at[slot, 0], dn_sem.at[slot, 0]).wait()
            pltpu.make_async_copy(sd_ref.at[0, :, :NT], wdn.at[slot, 1], dn_sem.at[slot, 1]).wait()

        gu_start(0, 0)

        gain_in.wait()
        main_sum = summed_ref[0]
        recip = lax.rsqrt(jnp.mean(main_sum * main_sum, axis=-1, keepdims=True) + EPS)
        normed_ref[TOK] = jnp.zeros((3, FOLD, LANES), BF)
        for s in range(3):
            if s == 0:
                rows = main_sum * recip * gain_ref[...]
            else:
                inner = jnp.mean(main_sum * summed_ref[s], axis=-1, keepdims=True)
                rows = (summed_ref[s] * recip - main_sum * (recip * recip * recip * inner)) * gain_ref[...]
            for c in range(FOLD):
                for half in (0, 1):
                    first = c * LANES + half * 128
                    stage[half, pl.ds(c, TOK, stride=FOLD), :] = rows[:, first : first + 128]
            for half in (0, 1):
                normed_ref[:TOK, s, :, half * 128 : half * 128 + 128] = (
                    stage[half, : TOK * FOLD].reshape(TOK, FOLD, 128).astype(BF)
                )

        def dispatch(i, carry):
            for slot in range(SLOTS):
                token = tok_ref[i * SLOTS + slot]
                for s in range(3):
                    send[i, s * SLOTS + slot] = normed_ref[token, s]

            @pl.when(i > WINDOW)
            def _():
                out_copy(i - WINDOW).wait_send()

            out_copy(i).start()
            return carry

        lax.fori_loop(1, CHIPS, dispatch, 0)

        for slot in range(SLOTS):
            token = tok_ref[slot]
            for s in range(3):
                recv[0, s * SLOTS + slot] = normed_ref[token, s]
        for copy in weight_copies:
            copy.wait()

        def chunk(g, carry):
            def arrive(i, carry):
                out_copy(i).wait_recv()
                return carry

            lax.fori_loop(jnp.where(g == 0, 1, HALF), (g + 1) * HALF, arrive, 0)

            def unfold(m, carry):
                v, part = lax.div(m, 2), lax.rem(m, 2)
                tiles = recv[pl.ds(g * HALF + part * 16, 16), v].astype(F32).reshape(16 * FOLD, LANES)
                for half in (0, 1):
                    stage[half, : 16 * FOLD] = tiles[:, half * 128 : half * 128 + 128]
                row = pl.multiple_of(v * HALF + part * 16, 16)
                for c in range(FOLD):
                    for half in (0, 1):
                        first = c * LANES + half * 128
                        rows_in[pl.ds(row, 16), first : first + 128] = stage[
                            half, pl.ds(c, 16, stride=FOLD), :
                        ].astype(BF)
                return carry

            lax.fori_loop(0, 2 * VECS, unfold, 0)

            def gate_up(t, carry):
                slot = lax.rem(t, 2)

                @pl.when(t < 5)
                def _():
                    gu_start(t + 1, 1 - slot)

                @pl.when(t == 5)
                def _():
                    dn_start(0, 0)

                gu_wait(slot)
                g_all = dot(rows_in[...], wgu[slot, 0])
                u_all = dot(rows_in[...], wgu[slot, 1])
                n = SLOTS * HALF
                g0, u0 = g_all[:n], u_all[:n]
                sigma = 1.0 / (1.0 + jnp.exp(-g0))
                active = g0 * sigma
                slope = sigma * (1.0 + g0 * (1.0 - sigma)) * u0
                lanes = pl.ds(pl.multiple_of(t * FT, FT), FT)
                hidden[:n, lanes] = (active * u0).astype(BF)
                hidden[n : 2 * n, lanes] = (slope * g_all[n : 2 * n] + active * u_all[n : 2 * n]).astype(BF)
                hidden[2 * n :, lanes] = (slope * g_all[2 * n :] + active * u_all[2 * n :]).astype(BF)
                return carry

            lax.fori_loop(0, 6, gate_up, 0)

            def down(n, carry):
                slot = lax.rem(n, 2)

                @pl.when(n < D // NT - 1)
                def _():
                    dn_start(n + 1, 1 - slot)

                @pl.when((n == D // NT - 1) & (g == 0))
                def _():
                    gu_start(0, 0)

                dn_wait(slot)
                part = dot(hidden[:, :FH], wdn[slot, 0]) + dot(hidden[:, FH:], wdn[slot, 1])
                for q in range(NT // LANES):
                    for half in (0, 1):
                        first = q * LANES + half * 128
                        stage[half, pl.ds(n * (NT // LANES) + q, ROWS, stride=FOLD), :] = part[
                            :, first : first + 128
                        ]
                return carry

            lax.fori_loop(0, D // NT, down, 0)

            def fold(v, carry):
                for part in (0, 1):
                    row = pl.multiple_of((v * HALF + part * 16) * FOLD, 256)
                    for half in (0, 1):
                        recv[pl.ds(g * HALF + part * 16, 16), v, :, half * 128 : half * 128 + 128] = (
                            stage[half, pl.ds(row, 16 * FOLD), :].reshape(16, FOLD, 128).astype(BF)
                        )
                return carry

            lax.fori_loop(0, VECS, fold, 0)

            def give_back(i, carry):
                back_copy(i).start()
                return carry

            lax.fori_loop(jnp.where(g == 0, 1, HALF), (g + 1) * HALF, give_back, 0)
            return carry

        lax.fori_loop(0, 2, chunk, 0)

    pl.run_scoped(
        moe,
        pltpu.VMEM((ROWS, D), BF),
        pltpu.VMEM((ROWS, 2 * FH), BF),
        pltpu.VMEM((2, ROWS * FOLD, 128), F32),
        pltpu.VMEM((2, 2, D, FT), BF),
        pltpu.VMEM((2, 2, FH, NT), BF),
    )
    back[0] = recv[0]

    def collect(i, carry):
        @pl.when(i >= CHIPS - WINDOW)
        def _():
            out_copy(i).wait_send()

        back_copy(i).wait()
        return carry

    lax.fori_loop(1, CHIPS, collect, 0)

    def combine(tok, carry):
        sums = [jnp.zeros((FOLD, LANES), F32) for _ in range(3)]
        for r in range(8):
            where = pos_ref[r * TOK + tok]
            chip, slot = lax.div(where, SLOTS), lax.rem(where, SLOTS)
            weight = gains_ref[r, tok]
            for s in range(3):
                sums[s] += weight * back[chip, s * SLOTS + slot].astype(F32)
        row = pl.ds(pl.multiple_of(tok * FOLD, FOLD), FOLD)
        for s in range(3):
            for half in (0, 1):
                total[s, half, row, :] = sums[s][:, half * 128 : half * 128 + 128]
        return carry

    lax.fori_loop(0, TOK, combine, 0)
    probes = [jnp.zeros((TOK, 128), F32) for _ in range(2)]
    for c in range(FOLD):
        for half in (0, 1):
            first = c * LANES + half * 128
            lanes = slice(first, first + 128)
            for s in range(3):
                value = summed_ref[s, :, lanes] + total[s, half, pl.ds(c, TOK, stride=FOLD), :]
                out_ref[s, :, lanes] = value.astype(BF)
                if s:
                    probes[s - 1] += value * res_ref[s, :, lanes].astype(F32)
    diagonal = lax.broadcasted_iota(jnp.int32, (TOK, 128), 0) == lax.broadcasted_iota(jnp.int32, (TOK, 128), 1)
    for t in range(2):
        mean = jnp.sum(probes[t], axis=1, keepdims=True) * (1.0 / D)
        flat = jnp.sum(jnp.where(diagonal, mean, 0.0), axis=0, keepdims=True)
        probe_ref[t : t + 1, :] = flat[:, :TOK]


def layer(tok, pos, gains, q, k, v, residual, gain, w_out, w_gate, w_up, w_down):
    smem = pl.BlockSpec(memory_space=pltpu.SMEM)
    vmem = pl.BlockSpec(memory_space=pltpu.VMEM)
    hbm = pl.BlockSpec(memory_space=pltpu.HBM)
    dma = pltpu.SemaphoreType.DMA
    tiles = (CHIPS, VECS, FOLD, LANES)
    outs = pl.pallas_call(
        layer_kernel,
        out_shape=(
            jax.ShapeDtypeStruct((3, TOK, D), BF),
            jax.ShapeDtypeStruct((2, TOK), F32),
            jax.ShapeDtypeStruct(w_gate.shape, BF),
            jax.ShapeDtypeStruct(w_up.shape, BF),
            jax.ShapeDtypeStruct(w_down.shape, BF),
        ),
        in_specs=[smem] * 3 + [hbm] * 9,
        out_specs=(vmem, vmem, hbm, hbm, hbm),
        scratch_shapes=[
            pltpu.VMEM((3, KEYS, 512), BF),
            pltpu.VMEM((3, TOK, D), BF),
            pltpu.VMEM((1, D), F32),
            pltpu.VMEM((3, TOK, D), F32),
            pltpu.VMEM((TOK + 1, 3, FOLD, LANES), BF),
            pltpu.VMEM((SEQ, 3, KEYS, HD), BF),
            pltpu.VMEM((SEQ, 3, KEYS, HD), BF),
            pltpu.VMEM((4, 192, 1024), BF),
            pltpu.VMEM((4, 192, 1024), BF),
            pltpu.VMEM((48, D), F32),
            pltpu.VMEM((4, 3, 48, 1024), BF),
            pltpu.VMEM((4, 3, 48, 1024), BF),
            pltpu.VMEM(tiles, BF),
            pltpu.VMEM(tiles, BF),
            pltpu.VMEM(tiles, BF),
            pltpu.VMEM((3, 2, TOK * FOLD, 128), F32),
            dma((6,)),
            dma((3,)),
            dma((3,)),
            dma((15,)),
            dma((SEQ,)),
            dma((15,)),
            dma((SEQ,)),
            dma((4,)),
            dma((4,)),
            dma((4, 3)),
            dma((4, 3)),
            dma((CHIPS,)),
            dma((CHIPS,)),
            dma((CHIPS,)),
            dma((CHIPS,)),
            dma((2, 2)),
            dma((2, 2)),
        ],
        compiler_params=pltpu.CompilerParams(
            collective_id=0, has_side_effects=True, vmem_limit_bytes=58 * 2**20
        ),
        name="layer",
    )(tok, pos, gains, q, k, v, residual, gain, w_out, w_gate, w_up, w_down)
    return outs[0], outs[1]


def plan(routes):
    seq, ex = lax.axis_index("seq"), lax.axis_index("exp")
    z, x, y = seq // 4, seq % 4, ex // 2
    flat = routes.T.reshape(-1)
    count = flat.shape[0]
    order = jnp.arange(count)
    earlier = (flat[:, None] == flat[None, :]) & (order[None, :] < order[:, None])
    slot = jnp.sum(earlier.astype(jnp.int32), axis=1)
    dz = (flat // 16 - z) % 4
    dx = (flat // 4 % 4 - x) % 4
    dy = (flat % 4 - y) % 4
    number = (dz % 2 * 2 + dz // 2) * 16 + dx * 4 + dy
    pos = number * SLOTS + slot
    hit = (jnp.arange(CHIPS * SLOTS)[:, None] == pos[None, :]).astype(jnp.int32)
    tok = TOK + jnp.sum(hit * (order % TOK - TOK)[None, :], axis=1)
    return tok.astype(jnp.int32), pos.astype(jnp.int32)


def shards(
    queries,
    key_rows,
    value_rows,
    residual,
    w_out,
    norm_gain,
    w_gate,
    w_up,
    w_down,
    routes,
    route_gain,
):
    tok, pos = plan(routes)
    return layer(
        tok,
        pos,
        route_gain.T,
        queries,
        key_rows,
        value_rows,
        residual,
        norm_gain[None, :],
        w_out,
        w_gate,
        w_up,
        w_down,
    )


def solution(mesh):
    return jax.shard_map(
        shards,
        mesh=mesh,
        in_specs=(
            P(None, "seq", "exp"),
            P(None, "seq", "exp"),
            P(None, "seq", "exp"),
            P(None, ("seq", "exp"), None),
            P("exp", None),
            P(),
            P(("seq", "exp"), None, None),
            P(("seq", "exp"), None, None),
            P(("seq", "exp"), None, None),
            P(("seq", "exp"), None),
            P(("seq", "exp"), None),
        ),
        out_specs=(P(None, ("seq", "exp"), None), P(None, ("seq", "exp"))),
        check_vma=False,
    )
```

```python
import math

import jax
import jax.numpy as jnp
from jax import lax
from jax.experimental import pallas as pl
from jax.experimental.pallas import tpu as pltpu
from jax.sharding import PartitionSpec as P

HD = 128
EPS = 1e-06
MESH = pl.DeviceIdType.MESH
BF = jnp.bfloat16
F32 = jnp.float32

SEQ = 16
KEYS = 128
TOK = 16
D = 4096
LANES = 256
FOLD = D // LANES
CHIPS = 64
SLOTS = 3
VECS = 3 * SLOTS
FH = 768
HALF = 32
ROWS = HALF * VECS
FT = 256
WINDOW = 24
NT = 512


def dot(a, b):
    return jnp.dot(a, b, preferred_element_type=F32)


def dot_nt(a, b):
    return lax.dot_general(a, b, (((1,), (1,)), ((), ())), preferred_element_type=F32)


def layer_kernel(
    tok_ref,
    pos_ref,
    gains_ref,
    q_hbm,
    k_hbm,
    v_hbm,
    res_hbm,
    gain_hbm,
    wo_hbm,
    wg_ref,
    wu_ref,
    wd_ref,
    out_ref,
    probe_ref,
    sg_ref,
    su_ref,
    sd_ref,
    q_ref,
    res_ref,
    gain_ref,
    summed_ref,
    normed_ref,
    kb,
    vb,
    sib_send,
    sib_recv,
    own,
    y_send,
    y_recv,
    send,
    recv,
    back,
    total,
    in_sem,
    w_send,
    w_recv,
    k_send,
    k_recv,
    v_send,
    v_recv,
    s_send,
    s_recv,
    ys_send,
    ys_recv,
    send_sem,
    recv_sem,
    bsend_sem,
    brecv_sem,
    gu_sem,
    dn_sem,
):
    seq = lax.axis_index("seq")
    ex = lax.axis_index("exp")
    z, x = lax.div(seq, 4), lax.rem(seq, 4)
    y, core = lax.div(ex, 2), lax.rem(ex, 2)
    sibling = (seq, y * 2 + (1 - core))
    scale = 1.0 / math.sqrt(HD)
    order = (1, 3, 2)

    def z_peer(d):
        return (lax.rem(z + d, 4) * 4 + x, ex)

    def x_peer(d):
        return (z * 4 + lax.rem(x + d, 4), ex)

    def y_peer(d):
        return (seq, lax.rem(y + d, 4) * 2 + core)

    def peer(i, sign):
        iz = lax.div(i, 16)
        dz = lax.rem(iz, 2) * 2 + lax.div(iz, 2)
        dx = lax.rem(lax.div(i, 4), 4)
        dy = lax.rem(i, 4)
        if sign < 0:
            dz, dx, dy = 4 - dz, 4 - dx, 4 - dy
        return (lax.rem(z + dz, 4) * 4 + lax.rem(x + dx, 4), lax.rem(y + dy, 4) * 2 + core)

    def remote(src, dst, ssem, rsem, peer):
        return pltpu.make_async_remote_copy(
            src_ref=src, dst_ref=dst, send_sem=ssem, recv_sem=rsem, device_id=peer, device_id_type=MESH
        )

    barrier = pltpu.get_barrier_semaphore()
    pl.semaphore_signal(barrier, inc=1, device_id=sibling, device_id_type=MESH)

    def greet(i, carry):
        pl.semaphore_signal(barrier, inc=1, device_id=peer(i, 1), device_id_type=MESH)
        return carry

    lax.fori_loop(1, CHIPS, greet, 0)
    k_in = pltpu.make_async_copy(k_hbm, kb.at[seq], in_sem.at[0])
    v_in = pltpu.make_async_copy(v_hbm, vb.at[seq], in_sem.at[1])
    q_in = pltpu.make_async_copy(q_hbm, q_ref, in_sem.at[2])
    res_in = pltpu.make_async_copy(res_hbm, res_ref, in_sem.at[3])
    gain_in = pltpu.make_async_copy(gain_hbm, gain_ref, in_sem.at[4])
    for copy in (k_in, v_in, q_in, res_in, gain_in):
        copy.start()
    k_in.wait()
    v_in.wait()
    pl.semaphore_wait(barrier, CHIPS)

    def weight_copy(which, part):
        source = (wg_ref, wu_ref, wd_ref)[which]
        place = (sg_ref, su_ref, sd_ref)[which]
        count = (D, D, FH)[which] // 4
        rows = pl.ds(pl.multiple_of(part * count, count), count)
        number = which * 4 + part
        return remote(source.at[0, rows, :], place.at[0, rows, :], w_send.at[number], w_recv.at[number], sibling)

    def k_copy(origin, number, peer):
        return remote(kb.at[origin], kb.at[origin], k_send.at[number], k_recv.at[origin], peer)

    def v_copy(origin, number, peer):
        return remote(vb.at[origin], vb.at[origin], v_send.at[number], v_recv.at[origin], peer)

    for d in order:
        k_copy(seq, d - 1, z_peer(d)).start()
        v_copy(seq, d - 1, x_peer(d)).start()
    for d in order:
        k_copy(seq, 3 + d - 1, x_peer(d)).start()
        v_copy(seq, 3 + d - 1, z_peer(d)).start()
    weight_copy(0, 0).start()
    weight_copy(0, 1).start()

    def attend(qs, qc, scores, slopes, att, wo):
        wo_copy = pltpu.make_async_copy(wo_hbm, wo, in_sem.at[5])
        wo_copy.start(priority=1)
        q_in.wait()
        for h in range(4):
            for s in range(3):
                qs[s, h * 128 : (h + 1) * 128, :] = q_ref[s, :, h * 128 : (h + 1) * 128]
        for t in (1, 2):
            qc[t - 1, :, :HD] = qs[t]
            qc[t - 1, :, HD:] = qs[0]

        for d in order:
            from_z = lax.rem(z + d, 4) * 4 + x
            from_x = z * 4 + lax.rem(x + d, 4)
            k_copy(from_z, 0, z_peer(d)).wait_recv()
            for e in order:
                k_copy(from_z, 3 * (d + 1) + e - 1, x_peer(e)).start()
            v_copy(from_x, 0, x_peer(d)).wait_recv()
            for e in order:
                v_copy(from_x, 3 * (d + 1) + e - 1, z_peer(e)).start()
            if d != 2:
                weight_copy(0, 2 + order.index(d)).start()

        for dz in (0,) + order:
            c = lax.rem(z + dz, 4)
            for e in (1, 2, 3):
                k_copy(c * 4 + lax.rem(x + e, 4), 0, x_peer(e)).wait_recv()
            weight_copy(1, dz).start()
            kc = kb[pl.ds(c * 4, 4)]
            k0 = kc[:, 0].reshape(512, HD)
            scores[c] = dot_nt(qs[0], k0) * scale
            for t in (1, 2):
                kt = kc[:, t].reshape(512, HD)
                slopes[t - 1, c] = dot_nt(qc[t - 1], jnp.concatenate([k0, kt], axis=1)) * scale

        for d in order:
            for e in (0, 1, 2, 3):
                origin = lax.rem(z + d, 4) * 4 + lax.rem(x + e, 4)
                v_copy(origin, 0, z_peer(d)).wait_recv()

        def head(h, carry):
            weight_copy(2, h).start()
            rows = pl.ds(pl.multiple_of(h * 128, 128), 128)
            top = jnp.max(scores[0, rows, :], axis=1, keepdims=True)
            for c in (1, 2, 3):
                top = jnp.maximum(top, jnp.max(scores[c, rows, :], axis=1, keepdims=True))
            norm = jnp.zeros((128, 1), F32)
            r1 = jnp.zeros((128, 1), F32)
            r2 = jnp.zeros((128, 1), F32)
            acc = jnp.zeros((128, 3 * HD), F32)
            mixed = jnp.zeros((256, HD), F32)
            for c in range(4):
                p = jnp.exp(scores[c, rows, :] - top).astype(BF)
                pf = p.astype(F32)
                w1 = (pf * slopes[0, c, rows, :]).astype(BF)
                w2 = (pf * slopes[1, c, rows, :]).astype(BF)
                norm += jnp.sum(pf, axis=1, keepdims=True)
                r1 += jnp.sum(w1.astype(F32), axis=1, keepdims=True)
                r2 += jnp.sum(w2.astype(F32), axis=1, keepdims=True)
                v0 = vb[4 * c : 4 * c + 4, 0].reshape(512, HD)
                v1 = vb[4 * c : 4 * c + 4, 1].reshape(512, HD)
                v2 = vb[4 * c : 4 * c + 4, 2].reshape(512, HD)
                acc += dot(p, jnp.concatenate([v0, v1, v2], axis=1))
                mixed += dot(jnp.concatenate([w1, w2], axis=0), v0)
            inv = 1.0 / norm
            main = acc[:, :HD] * inv
            t1 = (mixed[:128] + acc[:, HD : 2 * HD]) * inv - (r1 * inv) * main
            t2 = (mixed[128:] + acc[:, 2 * HD :]) * inv - (r2 * inv) * main
            att[0, :, rows] = main.astype(BF)
            att[1, :, rows] = t1.astype(BF)
            att[2, :, rows] = t2.astype(BF)
            return carry

        lax.fori_loop(0, 4, head, 0)

        wo_copy.wait()

        def block_rows(parity):
            parts = []
            for d in range(4):
                j = lax.rem(y + d, 4) * 2 + parity
                rows = pl.ds(pl.multiple_of(j * TOK, TOK), TOK)
                for s in range(3):
                    parts.append(att[s, rows, :])
            return jnp.concatenate(parts, axis=0)

        sib_rows = block_rows(1 - core)
        sib_copies = []
        for n in range(4):
            sib_send[n] = dot(sib_rows, wo[:, n * 1024 : (n + 1) * 1024]).astype(BF)
            copy = remote(sib_send.at[n], sib_recv.at[n], s_send.at[n], s_recv.at[n], sibling)
            copy.start()
            sib_copies.append(copy)
        own_rows = block_rows(core)
        y_copies = []
        for n in range(4):
            lanes = slice(n * 1024, (n + 1) * 1024)
            product = dot(own_rows, wo[:, lanes])
            sib_copies[n].wait_recv()
            both = product + sib_recv[n].astype(F32)
            own[:, lanes] = both[:48]
            for d in order:
                y_send[n, d - 1] = both[48 * d : 48 * (d + 1)].astype(BF)
                copy = remote(
                    y_send.at[n, d - 1], y_recv.at[n, d - 1], ys_send.at[n, d - 1], ys_recv.at[n, d - 1], y_peer(d)
                )
                copy.start()
                y_copies.append(copy)
        res_in.wait()
        for n in range(4):
            for d in (1, 2, 3):
                y_copies[n * 3 + order.index(d)].wait_recv()
            lanes = slice(n * 1024, (n + 1) * 1024)
            part = own[:, lanes]
            for d in (1, 2, 3):
                part += y_recv[n, d - 1].astype(F32)
            for s in range(3):
                summed_ref[s, :, lanes] = part[16 * s : 16 * (s + 1)] + res_ref[s, :, lanes].astype(F32)
        for d in order:
            k_copy(seq, d - 1, z_peer(d)).wait_send()
            v_copy(seq, d - 1, x_peer(d)).wait_send()
        for number in range(3, 15):
            k_copy(seq, number, x_peer(1)).wait_send()
            v_copy(seq, number, z_peer(1)).wait_send()
        for copy in sib_copies + y_copies:
            copy.wait_send()

    pl.run_scoped(
        attend,
        pltpu.VMEM((3, 512, HD), BF),
        pltpu.VMEM((2, 512, 2 * HD), BF),
        pltpu.VMEM((4, 512, 512), F32),
        pltpu.VMEM((2, 4, 512, 512), F32),
        pltpu.VMEM((3, KEYS, 512), BF),
        pltpu.VMEM((512, D), BF),
    )

    def out_copy(i):
        return remote(send.at[i], recv.at[i], send_sem.at[i], recv_sem.at[i], peer(i, 1))

    def back_copy(i):
        return remote(recv.at[i], back.at[i], bsend_sem.at[i], brecv_sem.at[i], peer(i, -1))

    def moe(rows_in, hidden, stage, wgu, wdn):
        def gu_copy(source, which, lanes, slot):
            place = wgu.at[slot, :, which * FT : (which + 1) * FT]
            return pltpu.make_async_copy(source.at[0, :, lanes], place, gu_sem.at[slot, which])

        def dn_copy(source, which, lanes, slot):
            place = wdn.at[slot, which * FH : (which + 1) * FH, :]
            return pltpu.make_async_copy(source.at[0, :, lanes], place, dn_sem.at[slot, which])

        def gu_start(t, slot):
            lanes = pl.ds(pl.multiple_of(lax.rem(t, 3) * FT, FT), FT)

            def go(gate, up):
                gu_copy(gate, 0, lanes, slot).start(priority=1)
                gu_copy(up, 1, lanes, slot).start(priority=1)

            @pl.when(t < 3)
            def _():
                go(wg_ref, wu_ref)

            @pl.when(t >= 3)
            def _():
                go(sg_ref, su_ref)

        def gu_wait(slot):
            gu_copy(wg_ref, 0, slice(0, FT), slot).wait()
            gu_copy(wu_ref, 1, slice(0, FT), slot).wait()

        def dn_start(n, slot):
            lanes = pl.ds(pl.multiple_of(n * NT, NT), NT)
            dn_copy(wd_ref, 0, lanes, slot).start(priority=1)
            dn_copy(sd_ref, 1, lanes, slot).start(priority=1)

        def dn_wait(slot):
            dn_copy(wd_ref, 0, slice(0, NT), slot).wait()
            dn_copy(sd_ref, 1, slice(0, NT), slot).wait()

        gu_start(0, 0)

        gain_in.wait()
        main_sum = summed_ref[0]
        recip = lax.rsqrt(jnp.mean(main_sum * main_sum, axis=-1, keepdims=True) + EPS)
        normed_ref[TOK] = jnp.zeros((3, FOLD, LANES), BF)
        for s in range(3):
            if s == 0:
                rows = main_sum * recip * gain_ref[...]
            else:
                inner = jnp.mean(main_sum * summed_ref[s], axis=-1, keepdims=True)
                rows = (summed_ref[s] * recip - main_sum * (recip * recip * recip * inner)) * gain_ref[...]
            for c in range(FOLD):
                for half in (0, 1):
                    first = c * LANES + half * 128
                    stage[half, pl.ds(c, TOK, stride=FOLD), :] = rows[:, first : first + 128]
            for half in (0, 1):
                normed_ref[:TOK, s, :, half * 128 : half * 128 + 128] = (
                    stage[half, : TOK * FOLD].reshape(TOK, FOLD, 128).astype(BF)
                )

        def dispatch(i, carry):
            for slot in range(SLOTS):
                token = tok_ref[i * SLOTS + slot]
                for s in range(3):
                    send[i, s * SLOTS + slot] = normed_ref[token, s]

            @pl.when(i > WINDOW)
            def _():
                out_copy(i - WINDOW).wait_send()

            out_copy(i).start()
            return carry

        lax.fori_loop(1, CHIPS, dispatch, 0)

        for slot in range(SLOTS):
            token = tok_ref[slot]
            for s in range(3):
                recv[0, s * SLOTS + slot] = normed_ref[token, s]
        for which in range(3):
            for part in range(4):
                weight_copy(which, part).wait()

        def chunk(g, carry):
            def arrive(i, carry):
                out_copy(i).wait_recv()
                return carry

            lax.fori_loop(jnp.where(g == 0, 1, HALF), (g + 1) * HALF, arrive, 0)

            def unfold(m, carry):
                v, part = lax.div(m, 2), lax.rem(m, 2)
                tiles = recv[pl.ds(g * HALF + part * 16, 16), v].astype(F32).reshape(16 * FOLD, LANES)
                for half in (0, 1):
                    stage[half, : 16 * FOLD] = tiles[:, half * 128 : half * 128 + 128]
                row = pl.multiple_of(v * HALF + part * 16, 16)
                for c in range(FOLD):
                    for half in (0, 1):
                        first = c * LANES + half * 128
                        rows_in[pl.ds(row, 16), first : first + 128] = stage[
                            half, pl.ds(c, 16, stride=FOLD), :
                        ].astype(BF)
                return carry

            lax.fori_loop(0, 2 * VECS, unfold, 0)

            def gate_up(t, carry):
                slot = lax.rem(t, 2)

                @pl.when(t < 5)
                def _():
                    gu_start(t + 1, 1 - slot)

                @pl.when(t == 5)
                def _():
                    dn_start(0, 0)

                gu_wait(slot)
                both = dot(rows_in[...], wgu[slot])
                g_all, u_all = both[:, :FT], both[:, FT:]
                n = SLOTS * HALF
                g0, u0 = g_all[:n], u_all[:n]
                sigma = 1.0 / (1.0 + jnp.exp(-g0))
                active = g0 * sigma
                slope = sigma * (1.0 + g0 * (1.0 - sigma)) * u0
                lanes = pl.ds(pl.multiple_of(t * FT, FT), FT)
                hidden[:n, lanes] = (active * u0).astype(BF)
                hidden[n : 2 * n, lanes] = (slope * g_all[n : 2 * n] + active * u_all[n : 2 * n]).astype(BF)
                hidden[2 * n :, lanes] = (slope * g_all[2 * n :] + active * u_all[2 * n :]).astype(BF)
                return carry

            lax.fori_loop(0, 6, gate_up, 0)

            def down(n, carry):
                slot = lax.rem(n, 2)

                @pl.when(n < D // NT - 1)
                def _():
                    dn_start(n + 1, 1 - slot)

                @pl.when((n == D // NT - 1) & (g == 0))
                def _():
                    gu_start(0, 0)

                dn_wait(slot)
                part = dot(hidden[...], wdn[slot])
                for q in range(NT // LANES):
                    for half in (0, 1):
                        first = q * LANES + half * 128
                        stage[half, pl.ds(n * (NT // LANES) + q, ROWS, stride=FOLD), :] = part[
                            :, first : first + 128
                        ]
                return carry

            lax.fori_loop(0, D // NT, down, 0)

            def fold(v, carry):
                for part in (0, 1):
                    row = pl.multiple_of((v * HALF + part * 16) * FOLD, 256)
                    for half in (0, 1):
                        recv[pl.ds(g * HALF + part * 16, 16), v, :, half * 128 : half * 128 + 128] = (
                            stage[half, pl.ds(row, 16 * FOLD), :].reshape(16, FOLD, 128).astype(BF)
                        )
                return carry

            lax.fori_loop(0, VECS, fold, 0)

            def give_back(i, carry):
                back_copy(i).start()
                return carry

            lax.fori_loop(jnp.where(g == 0, 1, HALF), (g + 1) * HALF, give_back, 0)
            return carry

        lax.fori_loop(0, 2, chunk, 0)

    pl.run_scoped(
        moe,
        pltpu.VMEM((ROWS, D), BF),
        pltpu.VMEM((ROWS, 2 * FH), BF),
        pltpu.VMEM((2, ROWS * FOLD, 128), F32),
        pltpu.VMEM((2, D, 2 * FT), BF),
        pltpu.VMEM((2, 2 * FH, NT), BF),
    )
    back[0] = recv[0]

    def collect(i, carry):
        @pl.when(i >= CHIPS - WINDOW)
        def _():
            out_copy(i).wait_send()

        back_copy(i).wait()
        return carry

    lax.fori_loop(1, CHIPS, collect, 0)

    def combine(tok, carry):
        sums = [jnp.zeros((FOLD, LANES), F32) for _ in range(3)]
        for r in range(8):
            where = pos_ref[r * TOK + tok]
            chip, slot = lax.div(where, SLOTS), lax.rem(where, SLOTS)
            weight = gains_ref[r, tok]
            for s in range(3):
                sums[s] += weight * back[chip, s * SLOTS + slot].astype(F32)
        row = pl.ds(pl.multiple_of(tok * FOLD, FOLD), FOLD)
        for s in range(3):
            for half in (0, 1):
                total[s, half, row, :] = sums[s][:, half * 128 : half * 128 + 128]
        return carry

    lax.fori_loop(0, TOK, combine, 0)
    probes = [jnp.zeros((TOK, 128), F32) for _ in range(2)]
    for c in range(FOLD):
        for half in (0, 1):
            first = c * LANES + half * 128
            lanes = slice(first, first + 128)
            for s in range(3):
                value = summed_ref[s, :, lanes] + total[s, half, pl.ds(c, TOK, stride=FOLD), :]
                out_ref[s, :, lanes] = value.astype(BF)
                if s:
                    probes[s - 1] += value * res_ref[s, :, lanes].astype(F32)
    diagonal = lax.broadcasted_iota(jnp.int32, (TOK, 128), 0) == lax.broadcasted_iota(jnp.int32, (TOK, 128), 1)
    for t in range(2):
        mean = jnp.sum(probes[t], axis=1, keepdims=True) * (1.0 / D)
        flat = jnp.sum(jnp.where(diagonal, mean, 0.0), axis=0, keepdims=True)
        probe_ref[t : t + 1, :] = flat[:, :TOK]


def layer(tok, pos, gains, q, k, v, residual, gain, w_out, w_gate, w_up, w_down):
    smem = pl.BlockSpec(memory_space=pltpu.SMEM)
    vmem = pl.BlockSpec(memory_space=pltpu.VMEM)
    hbm = pl.BlockSpec(memory_space=pltpu.HBM)
    dma = pltpu.SemaphoreType.DMA
    tiles = (CHIPS, VECS, FOLD, LANES)
    outs = pl.pallas_call(
        layer_kernel,
        out_shape=(
            jax.ShapeDtypeStruct((3, TOK, D), BF),
            jax.ShapeDtypeStruct((2, TOK), F32),
            jax.ShapeDtypeStruct(w_gate.shape, BF),
            jax.ShapeDtypeStruct(w_up.shape, BF),
            jax.ShapeDtypeStruct(w_down.shape, BF),
        ),
        in_specs=[smem] * 3 + [hbm] * 9,
        out_specs=(vmem, vmem, hbm, hbm, hbm),
        scratch_shapes=[
            pltpu.VMEM((3, KEYS, 512), BF),
            pltpu.VMEM((3, TOK, D), BF),
            pltpu.VMEM((1, D), F32),
            pltpu.VMEM((3, TOK, D), F32),
            pltpu.VMEM((TOK + 1, 3, FOLD, LANES), BF),
            pltpu.VMEM((SEQ, 3, KEYS, HD), BF),
            pltpu.VMEM((SEQ, 3, KEYS, HD), BF),
            pltpu.VMEM((4, 192, 1024), BF),
            pltpu.VMEM((4, 192, 1024), BF),
            pltpu.VMEM((48, D), F32),
            pltpu.VMEM((4, 3, 48, 1024), BF),
            pltpu.VMEM((4, 3, 48, 1024), BF),
            pltpu.VMEM(tiles, BF),
            pltpu.VMEM(tiles, BF),
            pltpu.VMEM(tiles, BF),
            pltpu.VMEM((3, 2, TOK * FOLD, 128), F32),
            dma((6,)),
            dma((12,)),
            dma((12,)),
            dma((15,)),
            dma((SEQ,)),
            dma((15,)),
            dma((SEQ,)),
            dma((4,)),
            dma((4,)),
            dma((4, 3)),
            dma((4, 3)),
            dma((CHIPS,)),
            dma((CHIPS,)),
            dma((CHIPS,)),
            dma((CHIPS,)),
            dma((2, 2)),
            dma((2, 2)),
        ],
        compiler_params=pltpu.CompilerParams(
            collective_id=0, has_side_effects=True, vmem_limit_bytes=58 * 2**20
        ),
        name="layer",
    )(tok, pos, gains, q, k, v, residual, gain, w_out, w_gate, w_up, w_down)
    return outs[0], outs[1]


def plan(routes):
    seq, ex = lax.axis_index("seq"), lax.axis_index("exp")
    z, x, y = seq // 4, seq % 4, ex // 2
    flat = routes.T.reshape(-1)
    count = flat.shape[0]
    order = jnp.arange(count)
    earlier = (flat[:, None] == flat[None, :]) & (order[None, :] < order[:, None])
    slot = jnp.sum(earlier.astype(jnp.int32), axis=1)
    dz = (flat // 16 - z) % 4
    dx = (flat // 4 % 4 - x) % 4
    dy = (flat % 4 - y) % 4
    number = (dz % 2 * 2 + dz // 2) * 16 + dx * 4 + dy
    pos = number * SLOTS + slot
    hit = (jnp.arange(CHIPS * SLOTS)[:, None] == pos[None, :]).astype(jnp.int32)
    tok = TOK + jnp.sum(hit * (order % TOK - TOK)[None, :], axis=1)
    return tok.astype(jnp.int32), pos.astype(jnp.int32)


def shards(
    queries,
    key_rows,
    value_rows,
    residual,
    w_out,
    norm_gain,
    w_gate,
    w_up,
    w_down,
    routes,
    route_gain,
):
    tok, pos = plan(routes)
    return layer(
        tok,
        pos,
        route_gain.T,
        queries,
        key_rows,
        value_rows,
        residual,
        norm_gain[None, :],
        w_out,
        w_gate,
        w_up,
        w_down,
    )


def solution(mesh):
    return jax.shard_map(
        shards,
        mesh=mesh,
        in_specs=(
            P(None, "seq", "exp"),
            P(None, "seq", "exp"),
            P(None, "seq", "exp"),
            P(None, ("seq", "exp"), None),
            P("exp", None),
            P(),
            P(("seq", "exp"), None, None),
            P(("seq", "exp"), None, None),
            P(("seq", "exp"), None, None),
            P(("seq", "exp"), None),
            P(("seq", "exp"), None),
        ),
        out_specs=(P(None, ("seq", "exp"), None), P(None, ("seq", "exp"))),
        check_vma=False,
    )
```

```python
import math

import jax
import jax.numpy as jnp
from jax import lax
from jax.experimental import pallas as pl
from jax.experimental.pallas import tpu as pltpu
from jax.sharding import PartitionSpec as P

HD = 128
EPS = 1e-06
MESH = pl.DeviceIdType.MESH
BF = jnp.bfloat16
F32 = jnp.float32

SEQ = 16
KEYS = 128
TOK = 16
D = 4096
LANES = 256
FOLD = D // LANES
CHIPS = 64
SLOTS = 3
VECS = 3 * SLOTS
FH = 768
ROWS = CHIPS * VECS
FT = 256
NT = 512


def dot(a, b):
    return jnp.dot(a, b, preferred_element_type=F32)


def dot_nt(a, b):
    return lax.dot_general(a, b, (((1,), (1,)), ((), ())), preferred_element_type=F32)


def place():
    seq, ex = lax.axis_index("seq"), lax.axis_index("exp")
    return lax.div(seq, 4), lax.rem(seq, 4), lax.div(ex, 2), lax.rem(ex, 2)


def peer(i, sign):
    z, x, y, core = place()
    dy = lax.rem(i, 4)
    dz = lax.rem(lax.div(i, 16) + dy, 4)
    dx = lax.rem(lax.rem(lax.div(i, 4), 4) + dy, 4)
    if sign < 0:
        dz, dx, dy = 4 - dz, 4 - dx, 4 - dy
    return (lax.rem(z + dz, 4) * 4 + lax.rem(x + dx, 4), lax.rem(y + dy, 4) * 2 + core)


def remote(src, dst, ssem, rsem, device):
    return pltpu.make_async_remote_copy(
        src_ref=src, dst_ref=dst, send_sem=ssem, recv_sem=rsem, device_id=device, device_id_type=MESH
    )


def greet(i, carry):
    barrier = pltpu.get_barrier_semaphore()
    pl.semaphore_signal(barrier, inc=1, device_id=peer(i, 1), device_id_type=MESH)
    return carry


def attend_kernel(
    tok_ref,
    q_hbm,
    k_hbm,
    v_hbm,
    res_hbm,
    gain_hbm,
    wo_hbm,
    wg_ref,
    wu_ref,
    wd_ref,
    summed_ref,
    recv,
    sg_ref,
    su_ref,
    sd_ref,
    q_ref,
    res_ref,
    gain_ref,
    normed_ref,
    stage,
    kb,
    vb,
    sib_send,
    sib_recv,
    own,
    y_send,
    y_recv,
    send,
    in_sem,
    w_send,
    w_recv,
    k_send,
    k_recv,
    v_send,
    v_recv,
    s_send,
    s_recv,
    ys_send,
    ys_recv,
    send_sem,
    recv_sem,
):
    seq = lax.axis_index("seq")
    ex = lax.axis_index("exp")
    z, x = lax.div(seq, 4), lax.rem(seq, 4)
    y, core = lax.div(ex, 2), lax.rem(ex, 2)
    sibling = (seq, y * 2 + (1 - core))
    scale = 1.0 / math.sqrt(HD)
    order = (1, 3, 2)

    def z_peer(d):
        return (lax.rem(z + d, 4) * 4 + x, ex)

    def x_peer(d):
        return (z * 4 + lax.rem(x + d, 4), ex)

    def y_peer(d):
        return (seq, lax.rem(y + d, 4) * 2 + core)

    barrier = pltpu.get_barrier_semaphore()
    pl.semaphore_signal(barrier, inc=1, device_id=sibling, device_id_type=MESH)

    lax.fori_loop(1, CHIPS, greet, 0)
    k_in = pltpu.make_async_copy(k_hbm, kb.at[seq], in_sem.at[0])
    v_in = pltpu.make_async_copy(v_hbm, vb.at[seq], in_sem.at[1])
    q_in = pltpu.make_async_copy(q_hbm, q_ref, in_sem.at[2])
    res_in = pltpu.make_async_copy(res_hbm, res_ref, in_sem.at[3])
    gain_in = pltpu.make_async_copy(gain_hbm, gain_ref, in_sem.at[4])
    for copy in (k_in, v_in, q_in, res_in, gain_in):
        copy.start()
    k_in.wait()
    v_in.wait()
    pl.semaphore_wait(barrier, CHIPS)

    def weight_copy(which, part):
        source = (wg_ref, wu_ref, wd_ref)[which]
        place = (sg_ref, su_ref, sd_ref)[which]
        count = (D, D, FH)[which] // 4
        rows = pl.ds(pl.multiple_of(part * count, count), count)
        number = which * 4 + part
        return remote(source.at[0, rows, :], place.at[0, rows, :], w_send.at[number], w_recv.at[number], sibling)

    def k_copy(origin, number, peer):
        return remote(kb.at[origin], kb.at[origin], k_send.at[number], k_recv.at[origin], peer)

    def v_copy(origin, number, peer):
        return remote(vb.at[origin], vb.at[origin], v_send.at[number], v_recv.at[origin], peer)

    for d in order:
        k_copy(seq, d - 1, z_peer(d)).start()
        v_copy(seq, d - 1, x_peer(d)).start()
    for d in order:
        k_copy(seq, 3 + d - 1, x_peer(d)).start()
        v_copy(seq, 3 + d - 1, z_peer(d)).start()
    for part in range(4):
        weight_copy(0, part).start()

    def attend(qs, qc, scores, slopes, att, wo):
        wo_copy = pltpu.make_async_copy(wo_hbm, wo, in_sem.at[5])
        wo_copy.start(priority=1)
        q_in.wait()
        for h in range(4):
            for s in range(3):
                qs[s, h * 128 : (h + 1) * 128, :] = q_ref[s, :, h * 128 : (h + 1) * 128]
        for t in (1, 2):
            qc[t - 1, :, :HD] = qs[t]
            qc[t - 1, :, HD:] = qs[0]

        for d in order:
            from_z = lax.rem(z + d, 4) * 4 + x
            from_x = z * 4 + lax.rem(x + d, 4)
            k_copy(from_z, 0, z_peer(d)).wait_recv()
            for e in order:
                k_copy(from_z, 3 * (d + 1) + e - 1, x_peer(e)).start()
            v_copy(from_x, 0, x_peer(d)).wait_recv()
            for e in order:
                v_copy(from_x, 3 * (d + 1) + e - 1, z_peer(e)).start()

        for part in range(4):
            weight_copy(1, part).start()

        for dz in (0,) + order:
            c = lax.rem(z + dz, 4)
            for e in (1, 2, 3):
                k_copy(c * 4 + lax.rem(x + e, 4), 0, x_peer(e)).wait_recv()
            kc = kb[pl.ds(c * 4, 4)]
            k0 = kc[:, 0].reshape(512, HD)
            scores[c] = dot_nt(qs[0], k0) * scale
            for t in (1, 2):
                kt = kc[:, t].reshape(512, HD)
                slopes[t - 1, c] = dot_nt(qc[t - 1], jnp.concatenate([k0, kt], axis=1)) * scale

        for d in order:
            for e in (0, 1, 2, 3):
                origin = lax.rem(z + d, 4) * 4 + lax.rem(x + e, 4)
                v_copy(origin, 0, z_peer(d)).wait_recv()

        def head(h, carry):
            rows = pl.ds(pl.multiple_of(h * 128, 128), 128)
            top = jnp.max(scores[0, rows, :], axis=1, keepdims=True)
            for c in (1, 2, 3):
                top = jnp.maximum(top, jnp.max(scores[c, rows, :], axis=1, keepdims=True))
            norm = jnp.zeros((128, 1), F32)
            r1 = jnp.zeros((128, 1), F32)
            r2 = jnp.zeros((128, 1), F32)
            acc = jnp.zeros((128, 3 * HD), F32)
            mixed = jnp.zeros((256, HD), F32)
            for c in range(4):
                p = jnp.exp(scores[c, rows, :] - top).astype(BF)
                pf = p.astype(F32)
                w1 = (pf * slopes[0, c, rows, :]).astype(BF)
                w2 = (pf * slopes[1, c, rows, :]).astype(BF)
                norm += jnp.sum(pf, axis=1, keepdims=True)
                r1 += jnp.sum(w1.astype(F32), axis=1, keepdims=True)
                r2 += jnp.sum(w2.astype(F32), axis=1, keepdims=True)
                v0 = vb[4 * c : 4 * c + 4, 0].reshape(512, HD)
                v1 = vb[4 * c : 4 * c + 4, 1].reshape(512, HD)
                v2 = vb[4 * c : 4 * c + 4, 2].reshape(512, HD)
                acc += dot(p, jnp.concatenate([v0, v1, v2], axis=1))
                mixed += dot(jnp.concatenate([w1, w2], axis=0), v0)
            inv = 1.0 / norm
            main = acc[:, :HD] * inv
            t1 = (mixed[:128] + acc[:, HD : 2 * HD]) * inv - (r1 * inv) * main
            t2 = (mixed[128:] + acc[:, 2 * HD :]) * inv - (r2 * inv) * main
            att[0, :, rows] = main.astype(BF)
            att[1, :, rows] = t1.astype(BF)
            att[2, :, rows] = t2.astype(BF)
            return carry

        lax.fori_loop(0, 4, head, 0)

        wo_copy.wait()

        def block_rows(parity):
            parts = []
            for d in range(4):
                j = lax.rem(y + d, 4) * 2 + parity
                rows = pl.ds(pl.multiple_of(j * TOK, TOK), TOK)
                for s in range(3):
                    parts.append(att[s, rows, :])
            return jnp.concatenate(parts, axis=0)

        sib_rows = block_rows(1 - core)
        sib_copies = []
        for n in range(4):
            sib_send[n] = dot(sib_rows, wo[:, n * 1024 : (n + 1) * 1024]).astype(BF)
            copy = remote(sib_send.at[n], sib_recv.at[n], s_send.at[n], s_recv.at[n], sibling)
            copy.start()
            sib_copies.append(copy)
        own_rows = block_rows(core)
        y_copies = []
        for n in range(4):
            lanes = slice(n * 1024, (n + 1) * 1024)
            product = dot(own_rows, wo[:, lanes])
            sib_copies[n].wait_recv()
            both = product + sib_recv[n].astype(F32)
            own[:, lanes] = both[:48]
            for d in order:
                y_send[n, d - 1] = both[48 * d : 48 * (d + 1)].astype(BF)
                copy = remote(
                    y_send.at[n, d - 1], y_recv.at[n, d - 1], ys_send.at[n, d - 1], ys_recv.at[n, d - 1], y_peer(d)
                )
                copy.start()
                y_copies.append(copy)
        for part in range(4):
            weight_copy(2, part).start()
        res_in.wait()
        for n in range(4):
            for d in (1, 2, 3):
                y_copies[n * 3 + order.index(d)].wait_recv()
            lanes = slice(n * 1024, (n + 1) * 1024)
            part = own[:, lanes]
            for d in (1, 2, 3):
                part += y_recv[n, d - 1].astype(F32)
            for s in range(3):
                summed_ref[s, :, lanes] = part[16 * s : 16 * (s + 1)] + res_ref[s, :, lanes].astype(F32)
        for d in order:
            k_copy(seq, d - 1, z_peer(d)).wait_send()
            v_copy(seq, d - 1, x_peer(d)).wait_send()
        for number in range(3, 15):
            k_copy(seq, number, x_peer(1)).wait_send()
            v_copy(seq, number, z_peer(1)).wait_send()
        for copy in sib_copies + y_copies:
            copy.wait_send()

    pl.run_scoped(
        attend,
        pltpu.VMEM((3, 512, HD), BF),
        pltpu.VMEM((2, 512, 2 * HD), BF),
        pltpu.VMEM((4, 512, 512), F32),
        pltpu.VMEM((2, 4, 512, 512), F32),
        pltpu.VMEM((3, KEYS, 512), BF),
        pltpu.VMEM((512, D), BF),
    )

    gain_in.wait()
    main_sum = summed_ref[0]
    recip = lax.rsqrt(jnp.mean(main_sum * main_sum, axis=-1, keepdims=True) + EPS)
    normed_ref[TOK] = jnp.zeros((3, FOLD, LANES), BF)
    for s in range(3):
        if s == 0:
            rows = main_sum * recip * gain_ref[...]
        else:
            inner = jnp.mean(main_sum * summed_ref[s], axis=-1, keepdims=True)
            rows = (summed_ref[s] * recip - main_sum * (recip * recip * recip * inner)) * gain_ref[...]
        for c in range(FOLD):
            for half in (0, 1):
                first = c * LANES + half * 128
                stage[half, pl.ds(c, TOK, stride=FOLD), :] = rows[:, first : first + 128]
        for half in (0, 1):
            normed_ref[:TOK, s, :, half * 128 : half * 128 + 128] = (
                stage[half, : TOK * FOLD].reshape(TOK, FOLD, 128).astype(BF)
            )

    def out_copy(i):
        return remote(send.at[i], recv.at[i], send_sem.at[i], recv_sem.at[i], peer(i, 1))

    def fill(i):
        for slot in range(SLOTS):
            token = tok_ref[i * SLOTS + slot]
            for s in range(3):
                send[i, s * SLOTS + slot] = normed_ref[token, s]

    def dispatch(i, carry):
        fill(i)
        out_copy(i).start()
        return carry

    lax.fori_loop(1, CHIPS, dispatch, 0)

    fill(0)
    stay = pltpu.make_async_copy(send.at[0], recv.at[0], in_sem.at[6])
    stay.start()
    for which in range(3):
        for part in range(4):
            weight_copy(which, part).wait()
    stay.wait()

    def collect(i, carry):
        out_copy(i).wait()
        return carry

    lax.fori_loop(1, CHIPS, collect, 0)


def attend(tok, q, k, v, residual, gain, w_out, w_gate, w_up, w_down):
    smem = pl.BlockSpec(memory_space=pltpu.SMEM)
    vmem = pl.BlockSpec(memory_space=pltpu.VMEM)
    hbm = pl.BlockSpec(memory_space=pltpu.HBM)
    dma = pltpu.SemaphoreType.DMA
    tiles = (CHIPS, VECS, FOLD, LANES)
    return pl.pallas_call(
        attend_kernel,
        out_shape=(
            jax.ShapeDtypeStruct((3, TOK, D), F32),
            jax.ShapeDtypeStruct(tiles, BF),
            jax.ShapeDtypeStruct(w_gate.shape, BF),
            jax.ShapeDtypeStruct(w_up.shape, BF),
            jax.ShapeDtypeStruct(w_down.shape, BF),
        ),
        in_specs=[smem] + [hbm] * 9,
        out_specs=(vmem, hbm, hbm, hbm, hbm),
        scratch_shapes=[
            pltpu.VMEM((3, KEYS, 512), BF),
            pltpu.VMEM((3, TOK, D), BF),
            pltpu.VMEM((1, D), F32),
            pltpu.VMEM((TOK + 1, 3, FOLD, LANES), BF),
            pltpu.VMEM((2, TOK * FOLD, 128), F32),
            pltpu.VMEM((SEQ, 3, KEYS, HD), BF),
            pltpu.VMEM((SEQ, 3, KEYS, HD), BF),
            pltpu.VMEM((4, 192, 1024), BF),
            pltpu.VMEM((4, 192, 1024), BF),
            pltpu.VMEM((48, D), F32),
            pltpu.VMEM((4, 3, 48, 1024), BF),
            pltpu.VMEM((4, 3, 48, 1024), BF),
            pltpu.VMEM(tiles, BF),
            dma((7,)),
            dma((12,)),
            dma((12,)),
            dma((15,)),
            dma((SEQ,)),
            dma((15,)),
            dma((SEQ,)),
            dma((4,)),
            dma((4,)),
            dma((4, 3)),
            dma((4, 3)),
            dma((CHIPS,)),
            dma((CHIPS,)),
        ],
        compiler_params=pltpu.CompilerParams(
            collective_id=0, has_side_effects=True, vmem_limit_bytes=56 * 2**20
        ),
        name="attend",
    )(tok, q, k, v, residual, gain, w_out, w_gate, w_up, w_down)


def expert_kernel(
    recv_hbm, wg_ref, wu_ref, wd_ref, sg_ref, su_ref, sd_ref, done_ref, recv, rows_in, hidden, stage, wgu, wdn, in_sem, gu_sem, dn_sem
):
    recv_in = pltpu.make_async_copy(recv_hbm, recv, in_sem)
    recv_in.start()

    def gu_copy(source, which, lanes, slot):
        place = wgu.at[slot, :, which * FT : (which + 1) * FT]
        return pltpu.make_async_copy(source.at[0, :, lanes], place, gu_sem.at[slot, which])

    def dn_copy(source, which, lanes, slot):
        place = wdn.at[slot, which * FH : (which + 1) * FH, :]
        return pltpu.make_async_copy(source.at[0, :, lanes], place, dn_sem.at[slot, which])

    def gu_start(t, slot):
        lanes = pl.ds(pl.multiple_of(lax.rem(t, 3) * FT, FT), FT)

        def go(gate, up):
            gu_copy(gate, 0, lanes, slot).start(priority=1)
            gu_copy(up, 1, lanes, slot).start(priority=1)

        @pl.when(t < 3)
        def _():
            go(wg_ref, wu_ref)

        @pl.when(t >= 3)
        def _():
            go(sg_ref, su_ref)

    def gu_wait(slot):
        gu_copy(wg_ref, 0, slice(0, FT), slot).wait()
        gu_copy(wu_ref, 1, slice(0, FT), slot).wait()

    def dn_start(n, slot):
        lanes = pl.ds(pl.multiple_of(n * NT, NT), NT)
        dn_copy(wd_ref, 0, lanes, slot).start(priority=1)
        dn_copy(sd_ref, 1, lanes, slot).start(priority=1)

    def dn_wait(slot):
        dn_copy(wd_ref, 0, slice(0, NT), slot).wait()
        dn_copy(sd_ref, 1, slice(0, NT), slot).wait()

    gu_start(0, 0)
    recv_in.wait()

    def unfold(m, carry):
        v, part = lax.div(m, 4), lax.rem(m, 4)
        tiles = recv[pl.ds(part * 16, 16), v].astype(F32).reshape(16 * FOLD, LANES)
        for half in (0, 1):
            stage[half, : 16 * FOLD] = tiles[:, half * 128 : half * 128 + 128]
        row = pl.multiple_of(v * CHIPS + part * 16, 16)
        for c in range(FOLD):
            for half in (0, 1):
                first = c * LANES + half * 128
                rows_in[pl.ds(row, 16), first : first + 128] = stage[
                    half, pl.ds(c, 16, stride=FOLD), :
                ].astype(BF)
        return carry

    lax.fori_loop(0, 4 * VECS, unfold, 0)

    def gate_up(t, carry):
        slot = lax.rem(t, 2)

        @pl.when(t < 5)
        def _():
            gu_start(t + 1, 1 - slot)

        @pl.when(t == 5)
        def _():
            dn_start(0, 0)

        gu_wait(slot)
        both = dot(rows_in[...], wgu[slot])
        g_all, u_all = both[:, :FT], both[:, FT:]
        n = SLOTS * CHIPS
        g0, u0 = g_all[:n], u_all[:n]
        sigma = 1.0 / (1.0 + jnp.exp(-g0))
        active = g0 * sigma
        slope = sigma * (1.0 + g0 * (1.0 - sigma)) * u0
        lanes = pl.ds(pl.multiple_of(t * FT, FT), FT)
        hidden[:n, lanes] = (active * u0).astype(BF)
        hidden[n : 2 * n, lanes] = (slope * g_all[n : 2 * n] + active * u_all[n : 2 * n]).astype(BF)
        hidden[2 * n :, lanes] = (slope * g_all[2 * n :] + active * u_all[2 * n :]).astype(BF)
        return carry

    lax.fori_loop(0, 6, gate_up, 0)

    def down(n, carry):
        slot = lax.rem(n, 2)

        @pl.when(n < D // NT - 1)
        def _():
            dn_start(n + 1, 1 - slot)

        dn_wait(slot)
        part = dot(hidden[...], wdn[slot])
        for q in range(NT // LANES):
            for half in (0, 1):
                first = q * LANES + half * 128
                stage[half, pl.ds(n * (NT // LANES) + q, ROWS, stride=FOLD), :] = part[
                    :, first : first + 128
                ]
        return carry

    lax.fori_loop(0, D // NT, down, 0)

    def fold(v, carry):
        for part in range(4):
            row = pl.multiple_of((v * CHIPS + part * 16) * FOLD, 256)
            for half in (0, 1):
                done_ref[part * 16 : part * 16 + 16, v, :, half * 128 : half * 128 + 128] = (
                    stage[half, pl.ds(row, 16 * FOLD), :].reshape(16, FOLD, 128).astype(BF)
                )
        return carry

    lax.fori_loop(0, VECS, fold, 0)


def experts(recv, wg, wu, wd, sg, su, sd):
    vmem = pl.BlockSpec(memory_space=pltpu.VMEM)
    hbm = pl.BlockSpec(memory_space=pltpu.HBM)
    dma = pltpu.SemaphoreType.DMA
    tiles = (CHIPS, VECS, FOLD, LANES)
    return pl.pallas_call(
        expert_kernel,
        out_shape=jax.ShapeDtypeStruct(tiles, BF),
        in_specs=[hbm] * 7,
        out_specs=vmem,
        scratch_shapes=[
            pltpu.VMEM(tiles, BF),
            pltpu.VMEM((ROWS, D), BF),
            pltpu.VMEM((ROWS, 2 * FH), BF),
            pltpu.VMEM((2, ROWS * FOLD, 128), F32),
            pltpu.VMEM((2, D, 2 * FT), BF),
            pltpu.VMEM((2, 2 * FH, NT), BF),
            dma,
            dma((2, 2)),
            dma((2, 2)),
        ],
        compiler_params=pltpu.CompilerParams(vmem_limit_bytes=56 * 2**20),
        name="experts",
    )(recv, wg, wu, wd, sg, su, sd)


def combine_kernel(
    pos_ref, gains_ref, done_ref, summed_ref, res_ref, out_ref, probe_ref, back, total, own_sem, bsend_sem, brecv_sem
):
    barrier = pltpu.get_barrier_semaphore()
    lax.fori_loop(1, CHIPS, greet, 0)
    stay = pltpu.make_async_copy(done_ref.at[0], back.at[0], own_sem)
    stay.start()
    pl.semaphore_wait(barrier, CHIPS - 1)

    def back_copy(i):
        return remote(done_ref.at[i], back.at[i], bsend_sem.at[i], brecv_sem.at[i], peer(i, -1))

    def give_back(i, carry):
        back_copy(i).start()
        return carry

    lax.fori_loop(1, CHIPS, give_back, 0)
    stay.wait()

    def collect(i, carry):
        back_copy(i).wait()
        return carry

    lax.fori_loop(1, CHIPS, collect, 0)

    def combine(tok, carry):
        sums = [jnp.zeros((FOLD, LANES), F32) for _ in range(3)]
        for r in range(8):
            where = pos_ref[r * TOK + tok]
            chip, slot = lax.div(where, SLOTS), lax.rem(where, SLOTS)
            weight = gains_ref[r, tok]
            for s in range(3):
                sums[s] += weight * back[chip, s * SLOTS + slot].astype(F32)
        row = pl.ds(pl.multiple_of(tok * FOLD, FOLD), FOLD)
        for s in range(3):
            for half in (0, 1):
                total[s, half, row, :] = sums[s][:, half * 128 : half * 128 + 128]
        return carry

    lax.fori_loop(0, TOK, combine, 0)
    probes = [jnp.zeros((TOK, 128), F32) for _ in range(2)]
    for c in range(FOLD):
        for half in (0, 1):
            first = c * LANES + half * 128
            lanes = slice(first, first + 128)
            for s in range(3):
                value = summed_ref[s, :, lanes] + total[s, half, pl.ds(c, TOK, stride=FOLD), :]
                out_ref[s, :, lanes] = value.astype(BF)
                if s:
                    probes[s - 1] += value * res_ref[s, :, lanes].astype(F32)
    diagonal = lax.broadcasted_iota(jnp.int32, (TOK, 128), 0) == lax.broadcasted_iota(jnp.int32, (TOK, 128), 1)
    for t in range(2):
        mean = jnp.sum(probes[t], axis=1, keepdims=True) * (1.0 / D)
        flat = jnp.sum(jnp.where(diagonal, mean, 0.0), axis=0, keepdims=True)
        probe_ref[t : t + 1, :] = flat[:, :TOK]


def give_back(pos, gains, done, summed, residual):
    smem = pl.BlockSpec(memory_space=pltpu.SMEM)
    vmem = pl.BlockSpec(memory_space=pltpu.VMEM)
    dma = pltpu.SemaphoreType.DMA
    return pl.pallas_call(
        combine_kernel,
        out_shape=(
            jax.ShapeDtypeStruct((3, TOK, D), BF),
            jax.ShapeDtypeStruct((2, TOK), F32),
        ),
        in_specs=[smem] * 2 + [vmem] * 3,
        out_specs=(vmem, vmem),
        scratch_shapes=[
            pltpu.VMEM((CHIPS, VECS, FOLD, LANES), BF),
            pltpu.VMEM((3, 2, TOK * FOLD, 128), F32),
            dma,
            dma((CHIPS,)),
            dma((CHIPS,)),
        ],
        compiler_params=pltpu.CompilerParams(
            collective_id=1, has_side_effects=True, vmem_limit_bytes=40 * 2**20
        ),
        name="give_back",
    )(pos, gains, done, summed, residual)


def plan(routes):
    seq, ex = lax.axis_index("seq"), lax.axis_index("exp")
    z, x, y = seq // 4, seq % 4, ex // 2
    flat = routes.T.reshape(-1)
    count = flat.shape[0]
    order = jnp.arange(count)
    earlier = (flat[:, None] == flat[None, :]) & (order[None, :] < order[:, None])
    slot = jnp.sum(earlier.astype(jnp.int32), axis=1)
    dz = (flat // 16 - z) % 4
    dx = (flat // 4 % 4 - x) % 4
    dy = (flat % 4 - y) % 4
    number = (dz - dy) % 4 * 16 + (dx - dy) % 4 * 4 + dy
    pos = number * SLOTS + slot
    hit = (jnp.arange(CHIPS * SLOTS)[:, None] == pos[None, :]).astype(jnp.int32)
    tok = TOK + jnp.sum(hit * (order % TOK - TOK)[None, :], axis=1)
    return tok.astype(jnp.int32), pos.astype(jnp.int32)


def shards(
    queries,
    key_rows,
    value_rows,
    residual,
    w_out,
    norm_gain,
    w_gate,
    w_up,
    w_down,
    routes,
    route_gain,
):
    tok, pos = plan(routes)
    summed, recv, sg, su, sd = attend(
        tok, queries, key_rows, value_rows, residual, norm_gain[None, :], w_out, w_gate, w_up, w_down
    )
    done = experts(recv, w_gate, w_up, w_down, sg, su, sd)
    return give_back(pos, route_gain.T, done, summed, residual)


def solution(mesh):
    return jax.shard_map(
        shards,
        mesh=mesh,
        in_specs=(
            P(None, "seq", "exp"),
            P(None, "seq", "exp"),
            P(None, "seq", "exp"),
            P(None, ("seq", "exp"), None),
            P("exp", None),
            P(),
            P(("seq", "exp"), None, None),
            P(("seq", "exp"), None, None),
            P(("seq", "exp"), None, None),
            P(("seq", "exp"), None),
            P(("seq", "exp"), None),
        ),
        out_specs=(P(None, ("seq", "exp"), None), P(None, ("seq", "exp"))),
        check_vma=False,
    )
```

```python
import math

import jax
import jax.numpy as jnp
from jax import lax
from jax.experimental import pallas as pl
from jax.experimental.pallas import tpu as pltpu
from jax.sharding import PartitionSpec as P

HD = 128
EPS = 1e-06
MESH = pl.DeviceIdType.MESH
BF = jnp.bfloat16
F32 = jnp.float32

SEQ = 16
KEYS = 128
TOK = 16
D = 4096
LANES = 256
FOLD = D // LANES
CHIPS = 64
SLOTS = 3
VECS = 3 * SLOTS
FH = 768
HALF = 32
ROWS = HALF * VECS
FT = 256
WINDOW = 24
NT = 512


def dot(a, b):
    return jnp.dot(a, b, preferred_element_type=F32)


def dot_nt(a, b):
    return lax.dot_general(a, b, (((1,), (1,)), ((), ())), preferred_element_type=F32)


def layer_kernel(
    tok_ref,
    pos_ref,
    gains_ref,
    q_hbm,
    k_hbm,
    v_hbm,
    res_hbm,
    gain_hbm,
    wo_hbm,
    wg_ref,
    wu_ref,
    wd_ref,
    out_ref,
    probe_ref,
    sg_ref,
    su_ref,
    sd_ref,
    q_ref,
    res_ref,
    gain_ref,
    summed_ref,
    normed_ref,
    kb,
    vb,
    sib_send,
    sib_recv,
    own,
    y_send,
    y_recv,
    send,
    recv,
    back,
    total,
    in_sem,
    w_send,
    w_recv,
    k_send,
    k_recv,
    v_send,
    v_recv,
    s_send,
    s_recv,
    ys_send,
    ys_recv,
    send_sem,
    recv_sem,
    bsend_sem,
    brecv_sem,
    gu_sem,
    dn_sem,
):
    seq = lax.axis_index("seq")
    ex = lax.axis_index("exp")
    z, x = lax.div(seq, 4), lax.rem(seq, 4)
    y, core = lax.div(ex, 2), lax.rem(ex, 2)
    sibling = (seq, y * 2 + (1 - core))
    scale = 1.0 / math.sqrt(HD)
    order = (1, 3, 2)

    def z_peer(d):
        return (lax.rem(z + d, 4) * 4 + x, ex)

    def x_peer(d):
        return (z * 4 + lax.rem(x + d, 4), ex)

    def y_peer(d):
        return (seq, lax.rem(y + d, 4) * 2 + core)

    def peer(i, sign):
        dy = lax.rem(i, 4)
        dz = lax.rem(lax.div(i, 16) + dy, 4)
        dx = lax.rem(lax.rem(lax.div(i, 4), 4) + dy, 4)
        if sign < 0:
            dz, dx, dy = 4 - dz, 4 - dx, 4 - dy
        return (lax.rem(z + dz, 4) * 4 + lax.rem(x + dx, 4), lax.rem(y + dy, 4) * 2 + core)

    def remote(src, dst, ssem, rsem, peer):
        return pltpu.make_async_remote_copy(
            src_ref=src, dst_ref=dst, send_sem=ssem, recv_sem=rsem, device_id=peer, device_id_type=MESH
        )

    barrier = pltpu.get_barrier_semaphore()
    pl.semaphore_signal(barrier, inc=1, device_id=sibling, device_id_type=MESH)

    def greet(i, carry):
        pl.semaphore_signal(barrier, inc=1, device_id=peer(i, 1), device_id_type=MESH)
        return carry

    lax.fori_loop(1, CHIPS, greet, 0)
    k_in = pltpu.make_async_copy(k_hbm, kb.at[seq], in_sem.at[0])
    v_in = pltpu.make_async_copy(v_hbm, vb.at[seq], in_sem.at[1])
    q_in = pltpu.make_async_copy(q_hbm, q_ref, in_sem.at[2])
    res_in = pltpu.make_async_copy(res_hbm, res_ref, in_sem.at[3])
    gain_in = pltpu.make_async_copy(gain_hbm, gain_ref, in_sem.at[4])
    for copy in (k_in, v_in, q_in, res_in, gain_in):
        copy.start()
    k_in.wait()
    v_in.wait()
    pl.semaphore_wait(barrier, CHIPS)

    def weight_copy(which, part):
        source = (wg_ref, wu_ref, wd_ref)[which]
        place = (sg_ref, su_ref, sd_ref)[which]
        count = (D, D, FH)[which] // 4
        rows = pl.ds(pl.multiple_of(part * count, count), count)
        number = which * 4 + part
        return remote(source.at[0, rows, :], place.at[0, rows, :], w_send.at[number], w_recv.at[number], sibling)

    def k_copy(origin, number, peer):
        return remote(kb.at[origin], kb.at[origin], k_send.at[number], k_recv.at[origin], peer)

    def v_copy(origin, number, peer):
        return remote(vb.at[origin], vb.at[origin], v_send.at[number], v_recv.at[origin], peer)

    for d in order:
        k_copy(seq, d - 1, z_peer(d)).start()
        v_copy(seq, d - 1, x_peer(d)).start()
    for d in order:
        k_copy(seq, 3 + d - 1, x_peer(d)).start()
        v_copy(seq, 3 + d - 1, z_peer(d)).start()
    for part in range(4):
        weight_copy(0, part).start()

    def attend(qs, qc, scores, slopes, att, wo):
        wo_copy = pltpu.make_async_copy(wo_hbm, wo, in_sem.at[5])
        wo_copy.start(priority=1)
        q_in.wait()
        for h in range(4):
            for s in range(3):
                qs[s, h * 128 : (h + 1) * 128, :] = q_ref[s, :, h * 128 : (h + 1) * 128]
        for t in (1, 2):
            qc[t - 1, :, :HD] = qs[t]
            qc[t - 1, :, HD:] = qs[0]

        for d in order:
            from_z = lax.rem(z + d, 4) * 4 + x
            from_x = z * 4 + lax.rem(x + d, 4)
            k_copy(from_z, 0, z_peer(d)).wait_recv()
            for e in order:
                k_copy(from_z, 3 * (d + 1) + e - 1, x_peer(e)).start()
            v_copy(from_x, 0, x_peer(d)).wait_recv()
            for e in order:
                v_copy(from_x, 3 * (d + 1) + e - 1, z_peer(e)).start()

        for part in range(4):
            weight_copy(1, part).start()

        for dz in (0,) + order:
            c = lax.rem(z + dz, 4)
            for e in (1, 2, 3):
                k_copy(c * 4 + lax.rem(x + e, 4), 0, x_peer(e)).wait_recv()
            kc = kb[pl.ds(c * 4, 4)]
            k0 = kc[:, 0].reshape(512, HD)
            scores[c] = dot_nt(qs[0], k0) * scale
            for t in (1, 2):
                kt = kc[:, t].reshape(512, HD)
                slopes[t - 1, c] = dot_nt(qc[t - 1], jnp.concatenate([k0, kt], axis=1)) * scale

        for d in order:
            for e in (0, 1, 2, 3):
                origin = lax.rem(z + d, 4) * 4 + lax.rem(x + e, 4)
                v_copy(origin, 0, z_peer(d)).wait_recv()

        def head(h, carry):
            rows = pl.ds(pl.multiple_of(h * 128, 128), 128)
            top = jnp.max(scores[0, rows, :], axis=1, keepdims=True)
            for c in (1, 2, 3):
                top = jnp.maximum(top, jnp.max(scores[c, rows, :], axis=1, keepdims=True))
            norm = jnp.zeros((128, 1), F32)
            r1 = jnp.zeros((128, 1), F32)
            r2 = jnp.zeros((128, 1), F32)
            acc = jnp.zeros((128, 3 * HD), F32)
            mixed = jnp.zeros((256, HD), F32)
            for c in range(4):
                p = jnp.exp(scores[c, rows, :] - top).astype(BF)
                pf = p.astype(F32)
                w1 = (pf * slopes[0, c, rows, :]).astype(BF)
                w2 = (pf * slopes[1, c, rows, :]).astype(BF)
                norm += jnp.sum(pf, axis=1, keepdims=True)
                r1 += jnp.sum(w1.astype(F32), axis=1, keepdims=True)
                r2 += jnp.sum(w2.astype(F32), axis=1, keepdims=True)
                v0 = vb[4 * c : 4 * c + 4, 0].reshape(512, HD)
                v1 = vb[4 * c : 4 * c + 4, 1].reshape(512, HD)
                v2 = vb[4 * c : 4 * c + 4, 2].reshape(512, HD)
                acc += dot(p, jnp.concatenate([v0, v1, v2], axis=1))
                mixed += dot(jnp.concatenate([w1, w2], axis=0), v0)
            inv = 1.0 / norm
            main = acc[:, :HD] * inv
            t1 = (mixed[:128] + acc[:, HD : 2 * HD]) * inv - (r1 * inv) * main
            t2 = (mixed[128:] + acc[:, 2 * HD :]) * inv - (r2 * inv) * main
            att[0, :, rows] = main.astype(BF)
            att[1, :, rows] = t1.astype(BF)
            att[2, :, rows] = t2.astype(BF)
            return carry

        lax.fori_loop(0, 4, head, 0)

        wo_copy.wait()

        def block_rows(parity):
            parts = []
            for d in range(4):
                j = lax.rem(y + d, 4) * 2 + parity
                rows = pl.ds(pl.multiple_of(j * TOK, TOK), TOK)
                for s in range(3):
                    parts.append(att[s, rows, :])
            return jnp.concatenate(parts, axis=0)

        sib_rows = block_rows(1 - core)
        sib_copies = []
        for n in range(4):
            sib_send[n] = dot(sib_rows, wo[:, n * 1024 : (n + 1) * 1024]).astype(BF)
            copy = remote(sib_send.at[n], sib_recv.at[n], s_send.at[n], s_recv.at[n], sibling)
            copy.start()
            sib_copies.append(copy)
        own_rows = block_rows(core)
        y_copies = []
        for n in range(4):
            lanes = slice(n * 1024, (n + 1) * 1024)
            product = dot(own_rows, wo[:, lanes])
            sib_copies[n].wait_recv()
            both = product + sib_recv[n].astype(F32)
            own[:, lanes] = both[:48]
            for d in order:
                y_send[n, d - 1] = both[48 * d : 48 * (d + 1)].astype(BF)
                copy = remote(
                    y_send.at[n, d - 1], y_recv.at[n, d - 1], ys_send.at[n, d - 1], ys_recv.at[n, d - 1], y_peer(d)
                )
                copy.start()
                y_copies.append(copy)
        for part in range(4):
            weight_copy(2, part).start()
        res_in.wait()
        for n in range(4):
            for d in (1, 2, 3):
                y_copies[n * 3 + order.index(d)].wait_recv()
            lanes = slice(n * 1024, (n + 1) * 1024)
            part = own[:, lanes]
            for d in (1, 2, 3):
                part += y_recv[n, d - 1].astype(F32)
            for s in range(3):
                summed_ref[s, :, lanes] = part[16 * s : 16 * (s + 1)] + res_ref[s, :, lanes].astype(F32)
        for d in order:
            k_copy(seq, d - 1, z_peer(d)).wait_send()
            v_copy(seq, d - 1, x_peer(d)).wait_send()
        for number in range(3, 15):
            k_copy(seq, number, x_peer(1)).wait_send()
            v_copy(seq, number, z_peer(1)).wait_send()
        for copy in sib_copies + y_copies:
            copy.wait_send()

    pl.run_scoped(
        attend,
        pltpu.VMEM((3, 512, HD), BF),
        pltpu.VMEM((2, 512, 2 * HD), BF),
        pltpu.VMEM((4, 512, 512), F32),
        pltpu.VMEM((2, 4, 512, 512), F32),
        pltpu.VMEM((3, KEYS, 512), BF),
        pltpu.VMEM((512, D), BF),
    )

    def out_copy(i):
        return remote(send.at[i], recv.at[i], send_sem.at[i], recv_sem.at[i], peer(i, 1))

    def back_copy(i):
        return remote(recv.at[i], back.at[i], bsend_sem.at[i], brecv_sem.at[i], peer(i, -1))

    def moe(rows_in, hidden, stage, wgu, wdn):
        def gu_copy(source, which, lanes, slot):
            place = wgu.at[slot, :, which * FT : (which + 1) * FT]
            return pltpu.make_async_copy(source.at[0, :, lanes], place, gu_sem.at[slot, which])

        def dn_copy(source, which, lanes, slot):
            place = wdn.at[slot, which * FH : (which + 1) * FH, :]
            return pltpu.make_async_copy(source.at[0, :, lanes], place, dn_sem.at[slot, which])

        def gu_start(t, slot):
            lanes = pl.ds(pl.multiple_of(lax.rem(t, 3) * FT, FT), FT)

            def go(gate, up):
                gu_copy(gate, 0, lanes, slot).start(priority=1)
                gu_copy(up, 1, lanes, slot).start(priority=1)

            @pl.when(t < 3)
            def _():
                go(wg_ref, wu_ref)

            @pl.when(t >= 3)
            def _():
                go(sg_ref, su_ref)

        def gu_wait(slot):
            gu_copy(wg_ref, 0, slice(0, FT), slot).wait()
            gu_copy(wu_ref, 1, slice(0, FT), slot).wait()

        def dn_start(n, slot):
            lanes = pl.ds(pl.multiple_of(n * NT, NT), NT)
            dn_copy(wd_ref, 0, lanes, slot).start(priority=1)
            dn_copy(sd_ref, 1, lanes, slot).start(priority=1)

        def dn_wait(slot):
            dn_copy(wd_ref, 0, slice(0, NT), slot).wait()
            dn_copy(sd_ref, 1, slice(0, NT), slot).wait()

        gu_start(0, 0)

        gain_in.wait()
        main_sum = summed_ref[0]
        recip = lax.rsqrt(jnp.mean(main_sum * main_sum, axis=-1, keepdims=True) + EPS)
        normed_ref[TOK] = jnp.zeros((3, FOLD, LANES), BF)
        for s in range(3):
            if s == 0:
                rows = main_sum * recip * gain_ref[...]
            else:
                inner = jnp.mean(main_sum * summed_ref[s], axis=-1, keepdims=True)
                rows = (summed_ref[s] * recip - main_sum * (recip * recip * recip * inner)) * gain_ref[...]
            for c in range(FOLD):
                for half in (0, 1):
                    first = c * LANES + half * 128
                    stage[half, pl.ds(c, TOK, stride=FOLD), :] = rows[:, first : first + 128]
            for half in (0, 1):
                normed_ref[:TOK, s, :, half * 128 : half * 128 + 128] = (
                    stage[half, : TOK * FOLD].reshape(TOK, FOLD, 128).astype(BF)
                )

        def dispatch(i, carry):
            for slot in range(SLOTS):
                token = tok_ref[i * SLOTS + slot]
                for s in range(3):
                    send[i, s * SLOTS + slot] = normed_ref[token, s]

            @pl.when(i > WINDOW)
            def _():
                out_copy(i - WINDOW).wait_send()

            out_copy(i).start()
            return carry

        lax.fori_loop(1, CHIPS, dispatch, 0)

        for slot in range(SLOTS):
            token = tok_ref[slot]
            for s in range(3):
                recv[0, s * SLOTS + slot] = normed_ref[token, s]
        for which in range(3):
            for part in range(4):
                weight_copy(which, part).wait()

        def chunk(g, carry):
            def arrive(i, carry):
                out_copy(i).wait_recv()
                return carry

            lax.fori_loop(jnp.where(g == 0, 1, HALF), (g + 1) * HALF, arrive, 0)

            def unfold(m, carry):
                v, part = lax.div(m, 2), lax.rem(m, 2)
                tiles = recv[pl.ds(g * HALF + part * 16, 16), v].astype(F32).reshape(16 * FOLD, LANES)
                for half in (0, 1):
                    stage[half, : 16 * FOLD] = tiles[:, half * 128 : half * 128 + 128]
                row = pl.multiple_of(v * HALF + part * 16, 16)
                for c in range(FOLD):
                    for half in (0, 1):
                        first = c * LANES + half * 128
                        rows_in[pl.ds(row, 16), first : first + 128] = stage[
                            half, pl.ds(c, 16, stride=FOLD), :
                        ].astype(BF)
                return carry

            lax.fori_loop(0, 2 * VECS, unfold, 0)

            def gate_up(t, carry):
                slot = lax.rem(t, 2)

                @pl.when(t < 5)
                def _():
                    gu_start(t + 1, 1 - slot)

                @pl.when(t == 5)
                def _():
                    dn_start(0, 0)

                gu_wait(slot)
                both = dot(rows_in[...], wgu[slot])
                g_all, u_all = both[:, :FT], both[:, FT:]
                n = SLOTS * HALF
                g0, u0 = g_all[:n], u_all[:n]
                sigma = 1.0 / (1.0 + jnp.exp(-g0))
                active = g0 * sigma
                slope = sigma * (1.0 + g0 * (1.0 - sigma)) * u0
                lanes = pl.ds(pl.multiple_of(t * FT, FT), FT)
                hidden[:n, lanes] = (active * u0).astype(BF)
                hidden[n : 2 * n, lanes] = (slope * g_all[n : 2 * n] + active * u_all[n : 2 * n]).astype(BF)
                hidden[2 * n :, lanes] = (slope * g_all[2 * n :] + active * u_all[2 * n :]).astype(BF)
                return carry

            lax.fori_loop(0, 6, gate_up, 0)

            def down(n, carry):
                slot = lax.rem(n, 2)

                @pl.when(n < D // NT - 1)
                def _():
                    dn_start(n + 1, 1 - slot)

                @pl.when((n == D // NT - 1) & (g == 0))
                def _():
                    gu_start(0, 0)

                dn_wait(slot)
                part = dot(hidden[...], wdn[slot])
                for q in range(NT // LANES):
                    for half in (0, 1):
                        first = q * LANES + half * 128
                        stage[half, pl.ds(n * (NT // LANES) + q, ROWS, stride=FOLD), :] = part[
                            :, first : first + 128
                        ]
                return carry

            lax.fori_loop(0, D // NT, down, 0)

            def fold(v, carry):
                for part in (0, 1):
                    row = pl.multiple_of((v * HALF + part * 16) * FOLD, 256)
                    for half in (0, 1):
                        recv[pl.ds(g * HALF + part * 16, 16), v, :, half * 128 : half * 128 + 128] = (
                            stage[half, pl.ds(row, 16 * FOLD), :].reshape(16, FOLD, 128).astype(BF)
                        )
                return carry

            lax.fori_loop(0, VECS, fold, 0)

            def give_back(i, carry):
                back_copy(i).start()
                return carry

            lax.fori_loop(jnp.where(g == 0, 1, HALF), (g + 1) * HALF, give_back, 0)
            return carry

        lax.fori_loop(0, 2, chunk, 0)

    pl.run_scoped(
        moe,
        pltpu.VMEM((ROWS, D), BF),
        pltpu.VMEM((ROWS, 2 * FH), BF),
        pltpu.VMEM((2, ROWS * FOLD, 128), F32),
        pltpu.VMEM((2, D, 2 * FT), BF),
        pltpu.VMEM((2, 2 * FH, NT), BF),
    )
    back[0] = recv[0]

    def collect(i, carry):
        @pl.when(i >= CHIPS - WINDOW)
        def _():
            out_copy(i).wait_send()

        back_copy(i).wait()
        return carry

    lax.fori_loop(1, CHIPS, collect, 0)

    def combine(tok, carry):
        sums = [jnp.zeros((FOLD, LANES), F32) for _ in range(3)]
        for r in range(8):
            where = pos_ref[r * TOK + tok]
            chip, slot = lax.div(where, SLOTS), lax.rem(where, SLOTS)
            weight = gains_ref[r, tok]
            for s in range(3):
                sums[s] += weight * back[chip, s * SLOTS + slot].astype(F32)
        row = pl.ds(pl.multiple_of(tok * FOLD, FOLD), FOLD)
        for s in range(3):
            for half in (0, 1):
                total[s, half, row, :] = sums[s][:, half * 128 : half * 128 + 128]
        return carry

    lax.fori_loop(0, TOK, combine, 0)
    probes = [jnp.zeros((TOK, 128), F32) for _ in range(2)]
    for c in range(FOLD):
        for half in (0, 1):
            first = c * LANES + half * 128
            lanes = slice(first, first + 128)
            for s in range(3):
                value = summed_ref[s, :, lanes] + total[s, half, pl.ds(c, TOK, stride=FOLD), :]
                out_ref[s, :, lanes] = value.astype(BF)
                if s:
                    probes[s - 1] += value * res_ref[s, :, lanes].astype(F32)
    diagonal = lax.broadcasted_iota(jnp.int32, (TOK, 128), 0) == lax.broadcasted_iota(jnp.int32, (TOK, 128), 1)
    for t in range(2):
        mean = jnp.sum(probes[t], axis=1, keepdims=True) * (1.0 / D)
        flat = jnp.sum(jnp.where(diagonal, mean, 0.0), axis=0, keepdims=True)
        probe_ref[t : t + 1, :] = flat[:, :TOK]


def layer(tok, pos, gains, q, k, v, residual, gain, w_out, w_gate, w_up, w_down):
    smem = pl.BlockSpec(memory_space=pltpu.SMEM)
    vmem = pl.BlockSpec(memory_space=pltpu.VMEM)
    hbm = pl.BlockSpec(memory_space=pltpu.HBM)
    dma = pltpu.SemaphoreType.DMA
    tiles = (CHIPS, VECS, FOLD, LANES)
    outs = pl.pallas_call(
        layer_kernel,
        out_shape=(
            jax.ShapeDtypeStruct((3, TOK, D), BF),
            jax.ShapeDtypeStruct((2, TOK), F32),
            jax.ShapeDtypeStruct(w_gate.shape, BF),
            jax.ShapeDtypeStruct(w_up.shape, BF),
            jax.ShapeDtypeStruct(w_down.shape, BF),
        ),
        in_specs=[smem] * 3 + [hbm] * 9,
        out_specs=(vmem, vmem, hbm, hbm, hbm),
        scratch_shapes=[
            pltpu.VMEM((3, KEYS, 512), BF),
            pltpu.VMEM((3, TOK, D), BF),
            pltpu.VMEM((1, D), F32),
            pltpu.VMEM((3, TOK, D), F32),
            pltpu.VMEM((TOK + 1, 3, FOLD, LANES), BF),
            pltpu.VMEM((SEQ, 3, KEYS, HD), BF),
            pltpu.VMEM((SEQ, 3, KEYS, HD), BF),
            pltpu.VMEM((4, 192, 1024), BF),
            pltpu.VMEM((4, 192, 1024), BF),
            pltpu.VMEM((48, D), F32),
            pltpu.VMEM((4, 3, 48, 1024), BF),
            pltpu.VMEM((4, 3, 48, 1024), BF),
            pltpu.VMEM(tiles, BF),
            pltpu.VMEM(tiles, BF),
            pltpu.VMEM(tiles, BF),
            pltpu.VMEM((3, 2, TOK * FOLD, 128), F32),
            dma((6,)),
            dma((12,)),
            dma((12,)),
            dma((15,)),
            dma((SEQ,)),
            dma((15,)),
            dma((SEQ,)),
            dma((4,)),
            dma((4,)),
            dma((4, 3)),
            dma((4, 3)),
            dma((CHIPS,)),
            dma((CHIPS,)),
            dma((CHIPS,)),
            dma((CHIPS,)),
            dma((2, 2)),
            dma((2, 2)),
        ],
        compiler_params=pltpu.CompilerParams(
            collective_id=0, has_side_effects=True, vmem_limit_bytes=58 * 2**20
        ),
        name="layer",
    )(tok, pos, gains, q, k, v, residual, gain, w_out, w_gate, w_up, w_down)
    return outs[0], outs[1]


def plan(routes):
    seq, ex = lax.axis_index("seq"), lax.axis_index("exp")
    z, x, y = seq // 4, seq % 4, ex // 2
    flat = routes.T.reshape(-1)
    count = flat.shape[0]
    order = jnp.arange(count)
    earlier = (flat[:, None] == flat[None, :]) & (order[None, :] < order[:, None])
    slot = jnp.sum(earlier.astype(jnp.int32), axis=1)
    dz = (flat // 16 - z) % 4
    dx = (flat // 4 % 4 - x) % 4
    dy = (flat % 4 - y) % 4
    number = (dz - dy) % 4 * 16 + (dx - dy) % 4 * 4 + dy
    pos = number * SLOTS + slot
    hit = (jnp.arange(CHIPS * SLOTS)[:, None] == pos[None, :]).astype(jnp.int32)
    tok = TOK + jnp.sum(hit * (order % TOK - TOK)[None, :], axis=1)
    return tok.astype(jnp.int32), pos.astype(jnp.int32)


def shards(
    queries,
    key_rows,
    value_rows,
    residual,
    w_out,
    norm_gain,
    w_gate,
    w_up,
    w_down,
    routes,
    route_gain,
):
    tok, pos = plan(routes)
    return layer(
        tok,
        pos,
        route_gain.T,
        queries,
        key_rows,
        value_rows,
        residual,
        norm_gain[None, :],
        w_out,
        w_gate,
        w_up,
        w_down,
    )


def solution(mesh):
    return jax.shard_map(
        shards,
        mesh=mesh,
        in_specs=(
            P(None, "seq", "exp"),
            P(None, "seq", "exp"),
            P(None, "seq", "exp"),
            P(None, ("seq", "exp"), None),
            P("exp", None),
            P(),
            P(("seq", "exp"), None, None),
            P(("seq", "exp"), None, None),
            P(("seq", "exp"), None, None),
            P(("seq", "exp"), None),
            P(("seq", "exp"), None),
        ),
        out_specs=(P(None, ("seq", "exp"), None), P(None, ("seq", "exp"))),
        check_vma=False,
    )
```

```python
import math

import jax
import jax.numpy as jnp
from jax import lax
from jax.experimental import pallas as pl
from jax.experimental.pallas import tpu as pltpu
from jax.sharding import PartitionSpec as P

HD = 128
EPS = 1e-06
MESH = pl.DeviceIdType.MESH
BF = jnp.bfloat16
F32 = jnp.float32

SEQ = 16
KEYS = 128
TOK = 16
D = 4096
LANES = 256
FOLD = D // LANES
CHIPS = 64
SLOTS = 3
VECS = 3 * SLOTS
FH = 768
HALF = 32
ROWS = HALF * VECS
FT = 256
WINDOW = 24
NT = 512


def dot(a, b):
    return jnp.dot(a, b, preferred_element_type=F32)


def dot_nt(a, b):
    return lax.dot_general(a, b, (((1,), (1,)), ((), ())), preferred_element_type=F32)


def layer_kernel(
    tok_ref,
    pos_ref,
    gains_ref,
    q_hbm,
    k_hbm,
    v_hbm,
    res_hbm,
    gain_hbm,
    wo_hbm,
    wg_ref,
    wu_ref,
    wd_ref,
    out_ref,
    probe_ref,
    sg_ref,
    su_ref,
    sd_ref,
    q_ref,
    res_ref,
    gain_ref,
    summed_ref,
    normed_ref,
    kb,
    vb,
    sib_send,
    sib_recv,
    own,
    y_send,
    y_recv,
    send0,
    send12,
    recv,
    back,
    total,
    in_sem,
    w_send,
    w_recv,
    k_send,
    k_recv,
    v_send,
    v_recv,
    s_send,
    s_recv,
    ys_send,
    ys_recv,
    send_sem,
    recv_sem,
    bsend_sem,
    brecv_sem,
    gu_sem,
    dn_sem,
):
    seq = lax.axis_index("seq")
    ex = lax.axis_index("exp")
    z, x = lax.div(seq, 4), lax.rem(seq, 4)
    y, core = lax.div(ex, 2), lax.rem(ex, 2)
    sibling = (seq, y * 2 + (1 - core))
    scale = 1.0 / math.sqrt(HD)
    order = (1, 3, 2)

    def z_peer(d):
        return (lax.rem(z + d, 4) * 4 + x, ex)

    def x_peer(d):
        return (z * 4 + lax.rem(x + d, 4), ex)

    def y_peer(d):
        return (seq, lax.rem(y + d, 4) * 2 + core)

    def peer(i, sign):
        dy = lax.rem(i, 4)
        dz = lax.rem(lax.div(i, 16) + dy, 4)
        dx = lax.rem(lax.rem(lax.div(i, 4), 4) + dy, 4)
        if sign < 0:
            dz, dx, dy = 4 - dz, 4 - dx, 4 - dy
        return (lax.rem(z + dz, 4) * 4 + lax.rem(x + dx, 4), lax.rem(y + dy, 4) * 2 + core)

    def remote(src, dst, ssem, rsem, peer):
        return pltpu.make_async_remote_copy(
            src_ref=src, dst_ref=dst, send_sem=ssem, recv_sem=rsem, device_id=peer, device_id_type=MESH
        )

    barrier = pltpu.get_barrier_semaphore()
    pl.semaphore_signal(barrier, inc=1, device_id=sibling, device_id_type=MESH)

    def greet(i, carry):
        pl.semaphore_signal(barrier, inc=1, device_id=peer(i, 1), device_id_type=MESH)
        return carry

    lax.fori_loop(1, CHIPS, greet, 0)
    k_in = pltpu.make_async_copy(k_hbm, kb.at[seq], in_sem.at[0])
    v_in = pltpu.make_async_copy(v_hbm, vb.at[seq], in_sem.at[1])
    q_in = pltpu.make_async_copy(q_hbm, q_ref, in_sem.at[2])
    res_in = pltpu.make_async_copy(res_hbm, res_ref, in_sem.at[3])
    gain_in = pltpu.make_async_copy(gain_hbm, gain_ref, in_sem.at[4])
    for copy in (k_in, v_in, q_in, res_in, gain_in):
        copy.start()
    k_in.wait()
    v_in.wait()
    pl.semaphore_wait(barrier, CHIPS)

    def weight_copy(which, part):
        source = (wg_ref, wu_ref, wd_ref)[which]
        place = (sg_ref, su_ref, sd_ref)[which]
        count = (D, D, FH)[which] // 4
        rows = pl.ds(pl.multiple_of(part * count, count), count)
        number = which * 4 + part
        return remote(source.at[0, rows, :], place.at[0, rows, :], w_send.at[number], w_recv.at[number], sibling)

    def k_copy(origin, number, peer):
        return remote(kb.at[origin], kb.at[origin], k_send.at[number], k_recv.at[origin], peer)

    def v_copy(origin, number, peer):
        return remote(vb.at[origin], vb.at[origin], v_send.at[number], v_recv.at[origin], peer)

    for d in order:
        k_copy(seq, d - 1, z_peer(d)).start()
        v_copy(seq, d - 1, x_peer(d)).start()
    for d in order:
        k_copy(seq, 3 + d - 1, x_peer(d)).start()
        v_copy(seq, 3 + d - 1, z_peer(d)).start()
    for part in range(4):
        weight_copy(0, part).start()

    def y_copy(n, d, group):
        rows = slice(0, TOK) if group == 0 else slice(TOK, 3 * TOK)
        return remote(
            y_send.at[n, d - 1, rows, :],
            y_recv.at[n, d - 1, rows, :],
            ys_send.at[n, d - 1, group],
            ys_recv.at[n, d - 1, group],
            y_peer(d),
        )

    def y_sum(group):
        for n in range(4):
            for d in (1, 2, 3):
                y_copy(n, d, group).wait_recv()
            lanes = slice(n * 1024, (n + 1) * 1024)
            for s in (0,) if group == 0 else (1, 2):
                rows = slice(s * TOK, (s + 1) * TOK)
                part = own[rows, lanes] + res_ref[s, :, lanes].astype(F32)
                for d in (1, 2, 3):
                    part += y_recv[n, d - 1, rows, :].astype(F32)
                summed_ref[s, :, lanes] = part

    def attend(qs, qc, scores, slopes, att, wo):
        wo_copy = pltpu.make_async_copy(wo_hbm, wo, in_sem.at[5])
        wo_copy.start(priority=1)
        q_in.wait()
        for h in range(4):
            for s in range(3):
                qs[s, h * 128 : (h + 1) * 128, :] = q_ref[s, :, h * 128 : (h + 1) * 128]
        for t in (1, 2):
            qc[t - 1, :, :HD] = qs[t]
            qc[t - 1, :, HD:] = qs[0]

        for d in order:
            from_z = lax.rem(z + d, 4) * 4 + x
            from_x = z * 4 + lax.rem(x + d, 4)
            k_copy(from_z, 0, z_peer(d)).wait_recv()
            for e in order:
                k_copy(from_z, 3 * (d + 1) + e - 1, x_peer(e)).start()
            v_copy(from_x, 0, x_peer(d)).wait_recv()
            for e in order:
                v_copy(from_x, 3 * (d + 1) + e - 1, z_peer(e)).start()

        for part in range(4):
            weight_copy(1, part).start()

        for dz in (0,) + order:
            c = lax.rem(z + dz, 4)
            for e in (1, 2, 3):
                k_copy(c * 4 + lax.rem(x + e, 4), 0, x_peer(e)).wait_recv()
            kc = kb[pl.ds(c * 4, 4)]
            k0 = kc[:, 0].reshape(512, HD)
            scores[c] = dot_nt(qs[0], k0) * scale
            for t in (1, 2):
                kt = kc[:, t].reshape(512, HD)
                slopes[t - 1, c] = dot_nt(qc[t - 1], jnp.concatenate([k0, kt], axis=1)) * scale

        for d in order:
            for e in (0, 1, 2, 3):
                origin = lax.rem(z + d, 4) * 4 + lax.rem(x + e, 4)
                v_copy(origin, 0, z_peer(d)).wait_recv()

        def head(h, carry):
            rows = pl.ds(pl.multiple_of(h * 128, 128), 128)
            top = jnp.max(scores[0, rows, :], axis=1, keepdims=True)
            for c in (1, 2, 3):
                top = jnp.maximum(top, jnp.max(scores[c, rows, :], axis=1, keepdims=True))
            norm = jnp.zeros((128, 1), F32)
            r1 = jnp.zeros((128, 1), F32)
            r2 = jnp.zeros((128, 1), F32)
            acc = jnp.zeros((128, 3 * HD), F32)
            mixed = jnp.zeros((256, HD), F32)
            for c in range(4):
                p = jnp.exp(scores[c, rows, :] - top).astype(BF)
                pf = p.astype(F32)
                w1 = (pf * slopes[0, c, rows, :]).astype(BF)
                w2 = (pf * slopes[1, c, rows, :]).astype(BF)
                norm += jnp.sum(pf, axis=1, keepdims=True)
                r1 += jnp.sum(w1.astype(F32), axis=1, keepdims=True)
                r2 += jnp.sum(w2.astype(F32), axis=1, keepdims=True)
                v0 = vb[4 * c : 4 * c + 4, 0].reshape(512, HD)
                v1 = vb[4 * c : 4 * c + 4, 1].reshape(512, HD)
                v2 = vb[4 * c : 4 * c + 4, 2].reshape(512, HD)
                acc += dot(p, jnp.concatenate([v0, v1, v2], axis=1))
                mixed += dot(jnp.concatenate([w1, w2], axis=0), v0)
            inv = 1.0 / norm
            main = acc[:, :HD] * inv
            t1 = (mixed[:128] + acc[:, HD : 2 * HD]) * inv - (r1 * inv) * main
            t2 = (mixed[128:] + acc[:, 2 * HD :]) * inv - (r2 * inv) * main
            att[0, :, rows] = main.astype(BF)
            att[1, :, rows] = t1.astype(BF)
            att[2, :, rows] = t2.astype(BF)
            return carry

        lax.fori_loop(0, 4, head, 0)

        wo_copy.wait()

        def block_rows(parity):
            parts = []
            for d in range(4):
                j = lax.rem(y + d, 4) * 2 + parity
                rows = pl.ds(pl.multiple_of(j * TOK, TOK), TOK)
                for s in range(3):
                    parts.append(att[s, rows, :])
            return jnp.concatenate(parts, axis=0)

        sib_rows = block_rows(1 - core)
        sib_copies = []
        for n in range(4):
            sib_send[n] = dot(sib_rows, wo[:, n * 1024 : (n + 1) * 1024]).astype(BF)
            copy = remote(sib_send.at[n], sib_recv.at[n], s_send.at[n], s_recv.at[n], sibling)
            copy.start()
            sib_copies.append(copy)
        own_rows = block_rows(core)
        for n in range(4):
            lanes = slice(n * 1024, (n + 1) * 1024)
            product = dot(own_rows, wo[:, lanes])
            sib_copies[n].wait_recv()
            both = product + sib_recv[n].astype(F32)
            own[:, lanes] = both[:48]
            for d in order:
                y_send[n, d - 1] = both[48 * d : 48 * (d + 1)].astype(BF)
                y_copy(n, d, 0).start()
        for n in range(4):
            for d in order:
                y_copy(n, d, 1).start()
        for part in range(4):
            weight_copy(2, part).start()
        res_in.wait()
        y_sum(0)
        for d in order:
            k_copy(seq, d - 1, z_peer(d)).wait_send()
            v_copy(seq, d - 1, x_peer(d)).wait_send()
        for number in range(3, 15):
            k_copy(seq, number, x_peer(1)).wait_send()
            v_copy(seq, number, z_peer(1)).wait_send()
        for copy in sib_copies:
            copy.wait_send()

    pl.run_scoped(
        attend,
        pltpu.VMEM((3, 512, HD), BF),
        pltpu.VMEM((2, 512, 2 * HD), BF),
        pltpu.VMEM((4, 512, 512), F32),
        pltpu.VMEM((2, 4, 512, 512), F32),
        pltpu.VMEM((3, KEYS, 512), BF),
        pltpu.VMEM((512, D), BF),
    )

    def out_copy(i, group):
        if group == 0:
            return remote(send0.at[i], recv.at[i, 0:SLOTS], send_sem.at[i, 0], recv_sem.at[i, 0], peer(i, 1))
        return remote(send12.at[i], recv.at[i, SLOTS:VECS], send_sem.at[i, 1], recv_sem.at[i, 1], peer(i, 1))

    def back_copy(i):
        return remote(recv.at[i], back.at[i], bsend_sem.at[i], brecv_sem.at[i], peer(i, -1))

    def moe(rows_in, hidden, stage, wgu, wdn):
        def gu_copy(source, which, lanes, slot):
            place = wgu.at[slot, :, which * FT : (which + 1) * FT]
            return pltpu.make_async_copy(source.at[0, :, lanes], place, gu_sem.at[slot, which])

        def dn_copy(source, which, lanes, slot):
            place = wdn.at[slot, which * FH : (which + 1) * FH, :]
            return pltpu.make_async_copy(source.at[0, :, lanes], place, dn_sem.at[slot, which])

        def gu_start(t, slot):
            lanes = pl.ds(pl.multiple_of(lax.rem(t, 3) * FT, FT), FT)

            def go(gate, up):
                gu_copy(gate, 0, lanes, slot).start(priority=1)
                gu_copy(up, 1, lanes, slot).start(priority=1)

            @pl.when(t < 3)
            def _():
                go(wg_ref, wu_ref)

            @pl.when(t >= 3)
            def _():
                go(sg_ref, su_ref)

        def gu_wait(slot):
            gu_copy(wg_ref, 0, slice(0, FT), slot).wait()
            gu_copy(wu_ref, 1, slice(0, FT), slot).wait()

        def dn_start(n, slot):
            lanes = pl.ds(pl.multiple_of(n * NT, NT), NT)
            dn_copy(wd_ref, 0, lanes, slot).start(priority=1)
            dn_copy(sd_ref, 1, lanes, slot).start(priority=1)

        def dn_wait(slot):
            dn_copy(wd_ref, 0, slice(0, NT), slot).wait()
            dn_copy(sd_ref, 1, slice(0, NT), slot).wait()

        gu_start(0, 0)

        gain_in.wait()
        main_sum = summed_ref[0]
        recip = lax.rsqrt(jnp.mean(main_sum * main_sum, axis=-1, keepdims=True) + EPS)
        normed_ref[TOK] = jnp.zeros((3, FOLD, LANES), BF)

        def norm(s):
            main = summed_ref[0]
            if s == 0:
                rows = main * recip * gain_ref[...]
            else:
                inner = jnp.mean(main * summed_ref[s], axis=-1, keepdims=True)
                rows = (summed_ref[s] * recip - main * (recip * recip * recip * inner)) * gain_ref[...]
            for c in range(FOLD):
                for half in (0, 1):
                    first = c * LANES + half * 128
                    stage[half, pl.ds(c, TOK, stride=FOLD), :] = rows[:, first : first + 128]
            for half in (0, 1):
                normed_ref[:TOK, s, :, half * 128 : half * 128 + 128] = (
                    stage[half, : TOK * FOLD].reshape(TOK, FOLD, 128).astype(BF)
                )

        def dispatch0(i, carry):
            for slot in range(SLOTS):
                send0[i, slot] = normed_ref[tok_ref[i * SLOTS + slot], 0]
            out_copy(i, 0).start()
            return carry

        def dispatch12(i, carry):
            for slot in range(SLOTS):
                token = tok_ref[i * SLOTS + slot]
                for s in (1, 2):
                    send12[i, (s - 1) * SLOTS + slot] = normed_ref[token, s]

            @pl.when(i > WINDOW)
            def _():
                out_copy(i - WINDOW, 1).wait_send()

            out_copy(i, 1).start()
            return carry

        norm(0)
        lax.fori_loop(1, CHIPS, dispatch0, 0)
        y_sum(1)
        norm(1)
        norm(2)
        lax.fori_loop(1, CHIPS, dispatch12, 0)

        for slot in range(SLOTS):
            token = tok_ref[slot]
            for s in range(3):
                recv[0, s * SLOTS + slot] = normed_ref[token, s]
        for n in range(4):
            for d in order:
                for group in (0, 1):
                    y_copy(n, d, group).wait_send()
        for which in range(3):
            for part in range(4):
                weight_copy(which, part).wait()

        def chunk(g, carry):
            def arrive(i, carry):
                out_copy(i, 0).wait_recv()
                out_copy(i, 1).wait_recv()
                return carry

            lax.fori_loop(jnp.where(g == 0, 1, HALF), (g + 1) * HALF, arrive, 0)

            def unfold(m, carry):
                v, part = lax.div(m, 2), lax.rem(m, 2)
                tiles = recv[pl.ds(g * HALF + part * 16, 16), v].astype(F32).reshape(16 * FOLD, LANES)
                for half in (0, 1):
                    stage[half, : 16 * FOLD] = tiles[:, half * 128 : half * 128 + 128]
                row = pl.multiple_of(v * HALF + part * 16, 16)
                for c in range(FOLD):
                    for half in (0, 1):
                        first = c * LANES + half * 128
                        rows_in[pl.ds(row, 16), first : first + 128] = stage[
                            half, pl.ds(c, 16, stride=FOLD), :
                        ].astype(BF)
                return carry

            lax.fori_loop(0, 2 * VECS, unfold, 0)

            def gate_up(t, carry):
                slot = lax.rem(t, 2)

                @pl.when(t < 5)
                def _():
                    gu_start(t + 1, 1 - slot)

                @pl.when(t == 5)
                def _():
                    dn_start(0, 0)

                gu_wait(slot)
                both = dot(rows_in[...], wgu[slot])
                g_all, u_all = both[:, :FT], both[:, FT:]
                n = SLOTS * HALF
                g0, u0 = g_all[:n], u_all[:n]
                sigma = 1.0 / (1.0 + jnp.exp(-g0))
                active = g0 * sigma
                slope = sigma * (1.0 + g0 * (1.0 - sigma)) * u0
                lanes = pl.ds(pl.multiple_of(t * FT, FT), FT)
                hidden[:n, lanes] = (active * u0).astype(BF)
                hidden[n : 2 * n, lanes] = (slope * g_all[n : 2 * n] + active * u_all[n : 2 * n]).astype(BF)
                hidden[2 * n :, lanes] = (slope * g_all[2 * n :] + active * u_all[2 * n :]).astype(BF)
                return carry

            lax.fori_loop(0, 6, gate_up, 0)

            def down(n, carry):
                slot = lax.rem(n, 2)

                @pl.when(n < D // NT - 1)
                def _():
                    dn_start(n + 1, 1 - slot)

                @pl.when((n == D // NT - 1) & (g == 0))
                def _():
                    gu_start(0, 0)

                dn_wait(slot)
                part = dot(hidden[...], wdn[slot])
                for q in range(NT // LANES):
                    for half in (0, 1):
                        first = q * LANES + half * 128
                        stage[half, pl.ds(n * (NT // LANES) + q, ROWS, stride=FOLD), :] = part[
                            :, first : first + 128
                        ]
                return carry

            lax.fori_loop(0, D // NT, down, 0)

            def fold(v, carry):
                for part in (0, 1):
                    row = pl.multiple_of((v * HALF + part * 16) * FOLD, 256)
                    for half in (0, 1):
                        recv[pl.ds(g * HALF + part * 16, 16), v, :, half * 128 : half * 128 + 128] = (
                            stage[half, pl.ds(row, 16 * FOLD), :].reshape(16, FOLD, 128).astype(BF)
                        )
                return carry

            lax.fori_loop(0, VECS, fold, 0)

            def give_back(i, carry):
                back_copy(i).start()
                return carry

            lax.fori_loop(jnp.where(g == 0, 1, HALF), (g + 1) * HALF, give_back, 0)
            return carry

        lax.fori_loop(0, 2, chunk, 0)

    pl.run_scoped(
        moe,
        pltpu.VMEM((ROWS, D), BF),
        pltpu.VMEM((ROWS, 2 * FH), BF),
        pltpu.VMEM((2, ROWS * FOLD, 128), F32),
        pltpu.VMEM((2, D, 2 * FT), BF),
        pltpu.VMEM((2, 2 * FH, NT), BF),
    )
    back[0] = recv[0]

    def collect(i, carry):
        out_copy(i, 0).wait_send()

        @pl.when(i >= CHIPS - WINDOW)
        def _():
            out_copy(i, 1).wait_send()

        back_copy(i).wait()
        return carry

    lax.fori_loop(1, CHIPS, collect, 0)

    def combine(tok, carry):
        sums = [jnp.zeros((FOLD, LANES), F32) for _ in range(3)]
        for r in range(8):
            where = pos_ref[r, tok]
            chip, slot = lax.div(where, SLOTS), lax.rem(where, SLOTS)
            weight = gains_ref[r, tok]
            for s in range(3):
                sums[s] += weight * back[chip, s * SLOTS + slot].astype(F32)
        row = pl.ds(pl.multiple_of(tok * FOLD, FOLD), FOLD)
        for s in range(3):
            for half in (0, 1):
                total[s, half, row, :] = sums[s][:, half * 128 : half * 128 + 128]
        return carry

    lax.fori_loop(0, TOK, combine, 0)
    probes = [jnp.zeros((TOK, 128), F32) for _ in range(2)]
    for c in range(FOLD):
        for half in (0, 1):
            first = c * LANES + half * 128
            lanes = slice(first, first + 128)
            for s in range(3):
                value = summed_ref[s, :, lanes] + total[s, half, pl.ds(c, TOK, stride=FOLD), :]
                out_ref[s, :, lanes] = value.astype(BF)
                if s:
                    probes[s - 1] += value * res_ref[s, :, lanes].astype(F32)
    diagonal = lax.broadcasted_iota(jnp.int32, (TOK, 128), 0) == lax.broadcasted_iota(jnp.int32, (TOK, 128), 1)
    for t in range(2):
        mean = jnp.sum(probes[t], axis=1, keepdims=True) * (1.0 / D)
        flat = jnp.sum(jnp.where(diagonal, mean, 0.0), axis=0, keepdims=True)
        probe_ref[t : t + 1, :] = flat[:, :TOK]


def layer(tok, pos, gains, q, k, v, residual, gain, w_out, w_gate, w_up, w_down):
    smem = pl.BlockSpec(memory_space=pltpu.SMEM)
    vmem = pl.BlockSpec(memory_space=pltpu.VMEM)
    hbm = pl.BlockSpec(memory_space=pltpu.HBM)
    dma = pltpu.SemaphoreType.DMA
    tiles = (CHIPS, VECS, FOLD, LANES)
    outs = pl.pallas_call(
        layer_kernel,
        out_shape=(
            jax.ShapeDtypeStruct((3, TOK, D), BF),
            jax.ShapeDtypeStruct((2, TOK), F32),
            jax.ShapeDtypeStruct(w_gate.shape, BF),
            jax.ShapeDtypeStruct(w_up.shape, BF),
            jax.ShapeDtypeStruct(w_down.shape, BF),
        ),
        in_specs=[smem] * 3 + [hbm] * 9,
        out_specs=(vmem, vmem, hbm, hbm, hbm),
        scratch_shapes=[
            pltpu.VMEM((3, KEYS, 512), BF),
            pltpu.VMEM((3, TOK, D), BF),
            pltpu.VMEM((1, D), F32),
            pltpu.VMEM((3, TOK, D), F32),
            pltpu.VMEM((TOK + 1, 3, FOLD, LANES), BF),
            pltpu.VMEM((SEQ, 3, KEYS, HD), BF),
            pltpu.VMEM((SEQ, 3, KEYS, HD), BF),
            pltpu.VMEM((4, 192, 1024), BF),
            pltpu.VMEM((4, 192, 1024), BF),
            pltpu.VMEM((48, D), F32),
            pltpu.VMEM((4, 3, 48, 1024), BF),
            pltpu.VMEM((4, 3, 48, 1024), BF),
            pltpu.VMEM((CHIPS, SLOTS, FOLD, LANES), BF),
            pltpu.VMEM((CHIPS, 2 * SLOTS, FOLD, LANES), BF),
            pltpu.VMEM(tiles, BF),
            pltpu.VMEM(tiles, BF),
            pltpu.VMEM((3, 2, TOK * FOLD, 128), F32),
            dma((6,)),
            dma((12,)),
            dma((12,)),
            dma((15,)),
            dma((SEQ,)),
            dma((15,)),
            dma((SEQ,)),
            dma((4,)),
            dma((4,)),
            dma((4, 3, 2)),
            dma((4, 3, 2)),
            dma((CHIPS, 2)),
            dma((CHIPS, 2)),
            dma((CHIPS,)),
            dma((CHIPS,)),
            dma((2, 2)),
            dma((2, 2)),
        ],
        compiler_params=pltpu.CompilerParams(
            collective_id=0, has_side_effects=True, vmem_limit_bytes=50 * 2**20
        ),
        name="layer",
    )(tok, pos, gains, q, k, v, residual, gain, w_out, w_gate, w_up, w_down)
    return outs[0], outs[1]


def plan(routes):
    seq, ex = lax.axis_index("seq"), lax.axis_index("exp")
    z, x, y = seq // 4, seq % 4, ex // 2
    mine = routes.T
    order = jnp.arange(8)[:, None] * TOK + jnp.arange(TOK)[None, :]
    same = mine[:, :, None, None] == mine[None, None]
    earlier = same & (order[None, None] < order[:, :, None, None])
    slot = jnp.sum(earlier.astype(jnp.int32), axis=(2, 3))
    dz = (mine // 16 - z) % 4
    dx = (mine // 4 % 4 - x) % 4
    dy = (mine % 4 - y) % 4
    number = (dz - dy) % 4 * 16 + (dx - dy) % 4 * 4 + dy
    pos = number * SLOTS + slot
    hit = (jnp.arange(CHIPS * SLOTS)[:, None, None] == pos[None]).astype(jnp.int32)
    tok = TOK + jnp.sum(hit * (jnp.arange(TOK) - TOK)[None, None, :], axis=(1, 2))
    return tok.astype(jnp.int32), pos.astype(jnp.int32)


def shards(
    queries,
    key_rows,
    value_rows,
    residual,
    w_out,
    norm_gain,
    w_gate,
    w_up,
    w_down,
    routes,
    route_gain,
):
    tok, pos = plan(routes)
    return layer(
        tok,
        pos,
        route_gain.T,
        queries,
        key_rows,
        value_rows,
        residual,
        norm_gain[None, :],
        w_out,
        w_gate,
        w_up,
        w_down,
    )


def solution(mesh):
    return jax.shard_map(
        shards,
        mesh=mesh,
        in_specs=(
            P(None, "seq", "exp"),
            P(None, "seq", "exp"),
            P(None, "seq", "exp"),
            P(None, ("seq", "exp"), None),
            P("exp", None),
            P(),
            P(("seq", "exp"), None, None),
            P(("seq", "exp"), None, None),
            P(("seq", "exp"), None, None),
            P(("seq", "exp"), None),
            P(("seq", "exp"), None),
        ),
        out_specs=(P(None, ("seq", "exp"), None), P(None, ("seq", "exp"))),
        check_vma=False,
    )
```

```python
import math

import jax
import jax.numpy as jnp
from jax import lax
from jax.experimental import pallas as pl
from jax.experimental.pallas import tpu as pltpu
from jax.sharding import PartitionSpec as P

HD = 128
EPS = 1e-06
MESH = pl.DeviceIdType.MESH
BF = jnp.bfloat16
F32 = jnp.float32

SEQ = 16
KEYS = 128
TOK = 16
D = 4096
LANES = 256
FOLD = D // LANES
CHIPS = 64
SLOTS = 3
VECS = 3 * SLOTS
FH = 768
HALF = 32
ROWS = HALF * VECS
FT = 256
WINDOW = 24
NT = 512


def dot(a, b):
    return jnp.dot(a, b, preferred_element_type=F32)


def dot_nt(a, b):
    return lax.dot_general(a, b, (((1,), (1,)), ((), ())), preferred_element_type=F32)


def layer_kernel(
    tok_ref,
    pos_ref,
    gains_ref,
    q_hbm,
    k_hbm,
    v_hbm,
    res_hbm,
    gain_hbm,
    wo_hbm,
    wg_ref,
    wu_ref,
    wd_ref,
    out_ref,
    probe_ref,
    sg_ref,
    su_ref,
    sd_ref,
    q_ref,
    res_ref,
    gain_ref,
    summed_ref,
    normed_ref,
    kb,
    vb,
    sib_send,
    sib_recv,
    own,
    y_send,
    y_recv,
    send,
    recv,
    back,
    total,
    in_sem,
    w_send,
    w_recv,
    kv_send,
    kv_recv,
    s_send,
    s_recv,
    ys_send,
    ys_recv,
    send_sem,
    recv_sem,
    bsend_sem,
    brecv_sem,
    gu_sem,
    dn_sem,
):
    seq = lax.axis_index("seq")
    ex = lax.axis_index("exp")
    z, x = lax.div(seq, 4), lax.rem(seq, 4)
    y, core = lax.div(ex, 2), lax.rem(ex, 2)
    sibling = (seq, y * 2 + (1 - core))
    scale = 1.0 / math.sqrt(HD)
    order = (1, 3, 2)

    def z_peer(d):
        return (lax.rem(z + d, 4) * 4 + x, ex)

    def x_peer(d):
        return (z * 4 + lax.rem(x + d, 4), ex)

    def y_peer(d):
        return (seq, lax.rem(y + d, 4) * 2 + core)

    def peer(i, sign):
        dy = lax.rem(i, 4)
        dz = lax.rem(lax.div(i, 16) + dy, 4)
        dx = lax.rem(lax.rem(lax.div(i, 4), 4) + dy, 4)
        if sign < 0:
            dz, dx, dy = 4 - dz, 4 - dx, 4 - dy
        return (lax.rem(z + dz, 4) * 4 + lax.rem(x + dx, 4), lax.rem(y + dy, 4) * 2 + core)

    def remote(src, dst, ssem, rsem, peer):
        return pltpu.make_async_remote_copy(
            src_ref=src, dst_ref=dst, send_sem=ssem, recv_sem=rsem, device_id=peer, device_id_type=MESH
        )

    barrier = pltpu.get_barrier_semaphore()
    pl.semaphore_signal(barrier, inc=1, device_id=sibling, device_id_type=MESH)

    def greet(i, carry):
        pl.semaphore_signal(barrier, inc=1, device_id=peer(i, 1), device_id_type=MESH)
        return carry

    lax.fori_loop(1, CHIPS, greet, 0)
    k_in = pltpu.make_async_copy(k_hbm, kb.at[seq], in_sem.at[0])
    v_in = pltpu.make_async_copy(v_hbm, vb.at[seq], in_sem.at[1])
    q_in = pltpu.make_async_copy(q_hbm, q_ref, in_sem.at[2])
    res_in = pltpu.make_async_copy(res_hbm, res_ref, in_sem.at[3])
    gain_in = pltpu.make_async_copy(gain_hbm, gain_ref, in_sem.at[4])
    for copy in (k_in, v_in, q_in, res_in, gain_in):
        copy.start()
    k_in.wait()
    v_in.wait()
    pl.semaphore_wait(barrier, CHIPS)

    def weight_copy(which, part):
        source = (wg_ref, wu_ref, wd_ref)[which]
        place = (sg_ref, su_ref, sd_ref)[which]
        count = (D, D, FH)[which] // 4
        rows = pl.ds(pl.multiple_of(part * count, count), count)
        number = which * 4 + part
        return remote(source.at[0, rows, :], place.at[0, rows, :], w_send.at[number], w_recv.at[number], sibling)

    sides = (1, 3)
    kv_sent = []

    def origin(which, da, db):
        dz, dx = (da, db) if which == 0 else (db, da)
        return lax.rem(z + dz, 4) * 4 + lax.rem(x + dx, 4)

    def kv_copy(which, source, number, half, device):
        buf = (kb, vb)[which]
        if half is None:
            ref = buf.at[source]
        else:
            ref = buf.at[source, :, half * 64 : half * 64 + 64, :]
        arrival = kv_recv.at[which, source, 1 if half == 1 else 0]
        return remote(ref, ref, kv_send.at[number], arrival, device)

    def push(which, da, db, half, axis, d):
        first = (axis == 0) == (which == 0)
        copy = kv_copy(which, origin(which, da, db), len(kv_sent), half, z_peer(d) if first else x_peer(d))
        copy.start()
        kv_sent.append(copy)

    def arrived(which, da, db, half):
        kv_copy(which, origin(which, da, db), 0, half, z_peer(1)).wait_recv()

    for axis in (0, 1):
        for which in (0, 1):
            for d in sides:
                push(which, 0, 0, None, axis, d)
    for part in range(4):
        weight_copy(0, part).start()

    def attend(qs, qc, scores, slopes, att, wo):
        wo_copy = pltpu.make_async_copy(wo_hbm, wo, in_sem.at[5])
        wo_copy.start(priority=1)
        q_in.wait()
        for h in range(4):
            for s in range(3):
                qs[s, h * 128 : (h + 1) * 128, :] = q_ref[s, :, h * 128 : (h + 1) * 128]
        for t in (1, 2):
            qc[t - 1, :, :HD] = qs[t]
            qc[t - 1, :, HD:] = qs[0]

        def cross(which, da):
            for d in sides:
                arrived(which, da, d, None)
                push(which, da, d, 1 if d == 1 else 0, 1, 4 - d)

        def opposite(which, da, db):
            arrived(which, da, db, 0)
            arrived(which, da, db, 1)

        def score(dz):
            opposite(0, dz, 2)
            c = lax.rem(z + dz, 4)
            kc = kb[pl.ds(c * 4, 4)]
            k0 = kc[:, 0].reshape(512, HD)
            scores[c] = dot_nt(qs[0], k0) * scale
            for t in (1, 2):
                kt = kc[:, t].reshape(512, HD)
                slopes[t - 1, c] = dot_nt(qc[t - 1], jnp.concatenate([k0, kt], axis=1)) * scale

        for d in sides:
            for which in (0, 1):
                arrived(which, d, 0, None)
                push(which, d, 0, 1 if d == 1 else 0, 0, 4 - d)
                for e in sides:
                    push(which, d, 0, None, 1, e)
        for which in (0, 1):
            cross(which, 0)
        for which in (0, 1):
            opposite(which, 2, 0)
            for e in sides:
                push(which, 2, 0, None, 1, e)
        done = 0
        for da in (1, 3, 2):
            for which in (0, 1):
                cross(which, da)
            score(done)
            done = da
        score(done)
        for da in range(4):
            opposite(1, da, 2)

        def head(h, carry):
            rows = pl.ds(pl.multiple_of(h * 128, 128), 128)
            top = jnp.max(scores[0, rows, :], axis=1, keepdims=True)
            for c in (1, 2, 3):
                top = jnp.maximum(top, jnp.max(scores[c, rows, :], axis=1, keepdims=True))
            norm = jnp.zeros((128, 1), F32)
            r1 = jnp.zeros((128, 1), F32)
            r2 = jnp.zeros((128, 1), F32)
            acc = jnp.zeros((128, 3 * HD), F32)
            mixed = jnp.zeros((256, HD), F32)
            for c in range(4):
                p = jnp.exp(scores[c, rows, :] - top).astype(BF)
                pf = p.astype(F32)
                w1 = (pf * slopes[0, c, rows, :]).astype(BF)
                w2 = (pf * slopes[1, c, rows, :]).astype(BF)
                norm += jnp.sum(pf, axis=1, keepdims=True)
                r1 += jnp.sum(w1.astype(F32), axis=1, keepdims=True)
                r2 += jnp.sum(w2.astype(F32), axis=1, keepdims=True)
                v0 = vb[4 * c : 4 * c + 4, 0].reshape(512, HD)
                v1 = vb[4 * c : 4 * c + 4, 1].reshape(512, HD)
                v2 = vb[4 * c : 4 * c + 4, 2].reshape(512, HD)
                acc += dot(p, jnp.concatenate([v0, v1, v2], axis=1))
                mixed += dot(jnp.concatenate([w1, w2], axis=0), v0)
            inv = 1.0 / norm
            main = acc[:, :HD] * inv
            t1 = (mixed[:128] + acc[:, HD : 2 * HD]) * inv - (r1 * inv) * main
            t2 = (mixed[128:] + acc[:, 2 * HD :]) * inv - (r2 * inv) * main
            att[0, :, rows] = main.astype(BF)
            att[1, :, rows] = t1.astype(BF)
            att[2, :, rows] = t2.astype(BF)
            return carry

        lax.fori_loop(0, 4, head, 0)

        wo_copy.wait()

        def block_rows(parity):
            parts = []
            for d in range(4):
                j = lax.rem(y + d, 4) * 2 + parity
                rows = pl.ds(pl.multiple_of(j * TOK, TOK), TOK)
                for s in range(3):
                    parts.append(att[s, rows, :])
            return jnp.concatenate(parts, axis=0)

        sib_rows = block_rows(1 - core)
        sib_copies = []
        for n in range(4):
            sib_send[n] = dot(sib_rows, wo[:, n * 1024 : (n + 1) * 1024]).astype(BF)
            copy = remote(sib_send.at[n], sib_recv.at[n], s_send.at[n], s_recv.at[n], sibling)
            copy.start()
            sib_copies.append(copy)
        own_rows = block_rows(core)
        y_copies = []
        for n in range(4):
            lanes = slice(n * 1024, (n + 1) * 1024)
            product = dot(own_rows, wo[:, lanes])
            sib_copies[n].wait_recv()
            both = product + sib_recv[n].astype(F32)
            own[:, lanes] = both[:48]
            for d in order:
                y_send[n, d - 1] = both[48 * d : 48 * (d + 1)].astype(BF)
                copy = remote(
                    y_send.at[n, d - 1], y_recv.at[n, d - 1], ys_send.at[n, d - 1], ys_recv.at[n, d - 1], y_peer(d)
                )
                copy.start()
                y_copies.append(copy)
        for part in range(4):
            weight_copy(1, part).start()
        for part in range(4):
            weight_copy(2, part).start()
        res_in.wait()
        for n in range(4):
            for d in (1, 2, 3):
                y_copies[n * 3 + order.index(d)].wait_recv()
            lanes = slice(n * 1024, (n + 1) * 1024)
            part = own[:, lanes]
            for d in (1, 2, 3):
                part += y_recv[n, d - 1].astype(F32)
            for s in range(3):
                summed_ref[s, :, lanes] = part[16 * s : 16 * (s + 1)] + res_ref[s, :, lanes].astype(F32)
        for copy in kv_sent + sib_copies + y_copies:
            copy.wait_send()

    pl.run_scoped(
        attend,
        pltpu.VMEM((3, 512, HD), BF),
        pltpu.VMEM((2, 512, 2 * HD), BF),
        pltpu.VMEM((4, 512, 512), F32),
        pltpu.VMEM((2, 4, 512, 512), F32),
        pltpu.VMEM((3, KEYS, 512), BF),
        pltpu.VMEM((512, D), BF),
    )

    def out_copy(i):
        return remote(send.at[i], recv.at[i], send_sem.at[i], recv_sem.at[i], peer(i, 1))

    def back_copy(i):
        return remote(recv.at[i], back.at[i], bsend_sem.at[i], brecv_sem.at[i], peer(i, -1))

    def moe(rows_in, hidden, stage, wgu, wdn):
        def gu_copy(source, which, lanes, slot):
            place = wgu.at[slot, :, which * FT : (which + 1) * FT]
            return pltpu.make_async_copy(source.at[0, :, lanes], place, gu_sem.at[slot, which])

        def dn_copy(source, which, lanes, slot):
            place = wdn.at[slot, which * FH : (which + 1) * FH, :]
            return pltpu.make_async_copy(source.at[0, :, lanes], place, dn_sem.at[slot, which])

        def gu_start(t, slot):
            lanes = pl.ds(pl.multiple_of(lax.rem(t, 3) * FT, FT), FT)

            def go(gate, up):
                gu_copy(gate, 0, lanes, slot).start(priority=1)
                gu_copy(up, 1, lanes, slot).start(priority=1)

            @pl.when(t < 3)
            def _():
                go(wg_ref, wu_ref)

            @pl.when(t >= 3)
            def _():
                go(sg_ref, su_ref)

        def gu_wait(slot):
            gu_copy(wg_ref, 0, slice(0, FT), slot).wait()
            gu_copy(wu_ref, 1, slice(0, FT), slot).wait()

        def dn_start(n, slot):
            lanes = pl.ds(pl.multiple_of(n * NT, NT), NT)
            dn_copy(wd_ref, 0, lanes, slot).start(priority=1)
            dn_copy(sd_ref, 1, lanes, slot).start(priority=1)

        def dn_wait(slot):
            dn_copy(wd_ref, 0, slice(0, NT), slot).wait()
            dn_copy(sd_ref, 1, slice(0, NT), slot).wait()

        gu_start(0, 0)

        gain_in.wait()
        main_sum = summed_ref[0]
        recip = lax.rsqrt(jnp.mean(main_sum * main_sum, axis=-1, keepdims=True) + EPS)
        normed_ref[TOK] = jnp.zeros((3, FOLD, LANES), BF)
        for s in range(3):
            if s == 0:
                rows = main_sum * recip * gain_ref[...]
            else:
                inner = jnp.mean(main_sum * summed_ref[s], axis=-1, keepdims=True)
                rows = (summed_ref[s] * recip - main_sum * (recip * recip * recip * inner)) * gain_ref[...]
            for c in range(FOLD):
                for half in (0, 1):
                    first = c * LANES + half * 128
                    stage[half, pl.ds(c, TOK, stride=FOLD), :] = rows[:, first : first + 128]
            for half in (0, 1):
                normed_ref[:TOK, s, :, half * 128 : half * 128 + 128] = (
                    stage[half, : TOK * FOLD].reshape(TOK, FOLD, 128).astype(BF)
                )

        def dispatch(i, carry):
            for slot in range(SLOTS):
                token = tok_ref[i * SLOTS + slot]
                for s in range(3):
                    send[i, s * SLOTS + slot] = normed_ref[token, s]

            @pl.when(i > WINDOW)
            def _():
                out_copy(i - WINDOW).wait_send()

            out_copy(i).start()
            return carry

        lax.fori_loop(1, CHIPS, dispatch, 0)

        for slot in range(SLOTS):
            token = tok_ref[slot]
            for s in range(3):
                recv[0, s * SLOTS + slot] = normed_ref[token, s]
        for which in range(3):
            for part in range(4):
                weight_copy(which, part).wait()

        def chunk(g, carry):
            def arrive(i, carry):
                out_copy(i).wait_recv()
                return carry

            lax.fori_loop(jnp.where(g == 0, 1, HALF), (g + 1) * HALF, arrive, 0)

            def unfold(m, carry):
                v, part = lax.div(m, 2), lax.rem(m, 2)
                tiles = recv[pl.ds(g * HALF + part * 16, 16), v].astype(F32).reshape(16 * FOLD, LANES)
                for half in (0, 1):
                    stage[half, : 16 * FOLD] = tiles[:, half * 128 : half * 128 + 128]
                row = pl.multiple_of(v * HALF + part * 16, 16)
                for c in range(FOLD):
                    for half in (0, 1):
                        first = c * LANES + half * 128
                        rows_in[pl.ds(row, 16), first : first + 128] = stage[
                            half, pl.ds(c, 16, stride=FOLD), :
                        ].astype(BF)
                return carry

            lax.fori_loop(0, 2 * VECS, unfold, 0)

            def gate_up(t, carry):
                slot = lax.rem(t, 2)

                @pl.when(t < 5)
                def _():
                    gu_start(t + 1, 1 - slot)

                @pl.when(t == 5)
                def _():
                    dn_start(0, 0)

                gu_wait(slot)
                both = dot(rows_in[...], wgu[slot])
                g_all, u_all = both[:, :FT], both[:, FT:]
                n = SLOTS * HALF
                g0, u0 = g_all[:n], u_all[:n]
                sigma = 1.0 / (1.0 + jnp.exp(-g0))
                active = g0 * sigma
                slope = sigma * (1.0 + g0 * (1.0 - sigma)) * u0
                lanes = pl.ds(pl.multiple_of(t * FT, FT), FT)
                hidden[:n, lanes] = (active * u0).astype(BF)
                hidden[n : 2 * n, lanes] = (slope * g_all[n : 2 * n] + active * u_all[n : 2 * n]).astype(BF)
                hidden[2 * n :, lanes] = (slope * g_all[2 * n :] + active * u_all[2 * n :]).astype(BF)
                return carry

            lax.fori_loop(0, 6, gate_up, 0)

            def down(n, carry):
                slot = lax.rem(n, 2)

                @pl.when(n < D // NT - 1)
                def _():
                    dn_start(n + 1, 1 - slot)

                @pl.when((n == D // NT - 1) & (g == 0))
                def _():
                    gu_start(0, 0)

                dn_wait(slot)
                part = dot(hidden[...], wdn[slot])
                for q in range(NT // LANES):
                    for half in (0, 1):
                        first = q * LANES + half * 128
                        stage[half, pl.ds(n * (NT // LANES) + q, ROWS, stride=FOLD), :] = part[
                            :, first : first + 128
                        ]
                return carry

            lax.fori_loop(0, D // NT, down, 0)

            def fold(v, carry):
                for part in (0, 1):
                    row = pl.multiple_of((v * HALF + part * 16) * FOLD, 256)
                    for half in (0, 1):
                        recv[pl.ds(g * HALF + part * 16, 16), v, :, half * 128 : half * 128 + 128] = (
                            stage[half, pl.ds(row, 16 * FOLD), :].reshape(16, FOLD, 128).astype(BF)
                        )
                return carry

            lax.fori_loop(0, VECS, fold, 0)

            def give_back(i, carry):
                back_copy(i).start()
                return carry

            lax.fori_loop(jnp.where(g == 0, 1, HALF), (g + 1) * HALF, give_back, 0)
            return carry

        lax.fori_loop(0, 2, chunk, 0)

    pl.run_scoped(
        moe,
        pltpu.VMEM((ROWS, D), BF),
        pltpu.VMEM((ROWS, 2 * FH), BF),
        pltpu.VMEM((2, ROWS * FOLD, 128), F32),
        pltpu.VMEM((2, D, 2 * FT), BF),
        pltpu.VMEM((2, 2 * FH, NT), BF),
    )
    back[0] = recv[0]

    def collect(i, carry):
        @pl.when(i >= CHIPS - WINDOW)
        def _():
            out_copy(i).wait_send()

        back_copy(i).wait()
        return carry

    lax.fori_loop(1, CHIPS, collect, 0)

    def combine(tok, carry):
        sums = [jnp.zeros((FOLD, LANES), F32) for _ in range(3)]
        for r in range(8):
            where = pos_ref[r * TOK + tok]
            chip, slot = lax.div(where, SLOTS), lax.rem(where, SLOTS)
            weight = gains_ref[r, tok]
            for s in range(3):
                sums[s] += weight * back[chip, s * SLOTS + slot].astype(F32)
        row = pl.ds(pl.multiple_of(tok * FOLD, FOLD), FOLD)
        for s in range(3):
            for half in (0, 1):
                total[s, half, row, :] = sums[s][:, half * 128 : half * 128 + 128]
        return carry

    lax.fori_loop(0, TOK, combine, 0)
    probes = [jnp.zeros((TOK, 128), F32) for _ in range(2)]
    for c in range(FOLD):
        for half in (0, 1):
            first = c * LANES + half * 128
            lanes = slice(first, first + 128)
            for s in range(3):
                value = summed_ref[s, :, lanes] + total[s, half, pl.ds(c, TOK, stride=FOLD), :]
                out_ref[s, :, lanes] = value.astype(BF)
                if s:
                    probes[s - 1] += value * res_ref[s, :, lanes].astype(F32)
    diagonal = lax.broadcasted_iota(jnp.int32, (TOK, 128), 0) == lax.broadcasted_iota(jnp.int32, (TOK, 128), 1)
    for t in range(2):
        mean = jnp.sum(probes[t], axis=1, keepdims=True) * (1.0 / D)
        flat = jnp.sum(jnp.where(diagonal, mean, 0.0), axis=0, keepdims=True)
        probe_ref[t : t + 1, :] = flat[:, :TOK]


def layer(tok, pos, gains, q, k, v, residual, gain, w_out, w_gate, w_up, w_down):
    smem = pl.BlockSpec(memory_space=pltpu.SMEM)
    vmem = pl.BlockSpec(memory_space=pltpu.VMEM)
    hbm = pl.BlockSpec(memory_space=pltpu.HBM)
    dma = pltpu.SemaphoreType.DMA
    tiles = (CHIPS, VECS, FOLD, LANES)
    outs = pl.pallas_call(
        layer_kernel,
        out_shape=(
            jax.ShapeDtypeStruct((3, TOK, D), BF),
            jax.ShapeDtypeStruct((2, TOK), F32),
            jax.ShapeDtypeStruct(w_gate.shape, BF),
            jax.ShapeDtypeStruct(w_up.shape, BF),
            jax.ShapeDtypeStruct(w_down.shape, BF),
        ),
        in_specs=[smem] * 3 + [hbm] * 9,
        out_specs=(vmem, vmem, hbm, hbm, hbm),
        scratch_shapes=[
            pltpu.VMEM((3, KEYS, 512), BF),
            pltpu.VMEM((3, TOK, D), BF),
            pltpu.VMEM((1, D), F32),
            pltpu.VMEM((3, TOK, D), F32),
            pltpu.VMEM((TOK + 1, 3, FOLD, LANES), BF),
            pltpu.VMEM((SEQ, 3, KEYS, HD), BF),
            pltpu.VMEM((SEQ, 3, KEYS, HD), BF),
            pltpu.VMEM((4, 192, 1024), BF),
            pltpu.VMEM((4, 192, 1024), BF),
            pltpu.VMEM((48, D), F32),
            pltpu.VMEM((4, 3, 48, 1024), BF),
            pltpu.VMEM((4, 3, 48, 1024), BF),
            pltpu.VMEM(tiles, BF),
            pltpu.VMEM(tiles, BF),
            pltpu.VMEM(tiles, BF),
            pltpu.VMEM((3, 2, TOK * FOLD, 128), F32),
            dma((6,)),
            dma((12,)),
            dma((12,)),
            dma((40,)),
            dma((2, SEQ, 2)),
            dma((4,)),
            dma((4,)),
            dma((4, 3)),
            dma((4, 3)),
            dma((CHIPS,)),
            dma((CHIPS,)),
            dma((CHIPS,)),
            dma((CHIPS,)),
            dma((2, 2)),
            dma((2, 2)),
        ],
        compiler_params=pltpu.CompilerParams(
            collective_id=0, has_side_effects=True, vmem_limit_bytes=58 * 2**20
        ),
        name="layer",
    )(tok, pos, gains, q, k, v, residual, gain, w_out, w_gate, w_up, w_down)
    return outs[0], outs[1]


def plan(routes):
    seq, ex = lax.axis_index("seq"), lax.axis_index("exp")
    z, x, y = seq // 4, seq % 4, ex // 2
    flat = routes.T.reshape(-1)
    count = flat.shape[0]
    order = jnp.arange(count)
    earlier = (flat[:, None] == flat[None, :]) & (order[None, :] < order[:, None])
    slot = jnp.sum(earlier.astype(jnp.int32), axis=1)
    dz = (flat // 16 - z) % 4
    dx = (flat // 4 % 4 - x) % 4
    dy = (flat % 4 - y) % 4
    number = (dz - dy) % 4 * 16 + (dx - dy) % 4 * 4 + dy
    pos = number * SLOTS + slot
    hit = (jnp.arange(CHIPS * SLOTS)[:, None] == pos[None, :]).astype(jnp.int32)
    tok = TOK + jnp.sum(hit * (order % TOK - TOK)[None, :], axis=1)
    return tok.astype(jnp.int32), pos.astype(jnp.int32)


def shards(
    queries,
    key_rows,
    value_rows,
    residual,
    w_out,
    norm_gain,
    w_gate,
    w_up,
    w_down,
    routes,
    route_gain,
):
    tok, pos = plan(routes)
    return layer(
        tok,
        pos,
        route_gain.T,
        queries,
        key_rows,
        value_rows,
        residual,
        norm_gain[None, :],
        w_out,
        w_gate,
        w_up,
        w_down,
    )


def solution(mesh):
    return jax.shard_map(
        shards,
        mesh=mesh,
        in_specs=(
            P(None, "seq", "exp"),
            P(None, "seq", "exp"),
            P(None, "seq", "exp"),
            P(None, ("seq", "exp"), None),
            P("exp", None),
            P(),
            P(("seq", "exp"), None, None),
            P(("seq", "exp"), None, None),
            P(("seq", "exp"), None, None),
            P(("seq", "exp"), None),
            P(("seq", "exp"), None),
        ),
        out_specs=(P(None, ("seq", "exp"), None), P(None, ("seq", "exp"))),
        check_vma=False,
    )
```

```python
import math

import jax
import jax.numpy as jnp
from jax import lax
from jax.experimental import pallas as pl
from jax.experimental.pallas import tpu as pltpu
from jax.sharding import PartitionSpec as P

HD = 128
EPS = 1e-06
MESH = pl.DeviceIdType.MESH
BF = jnp.bfloat16
F32 = jnp.float32

SEQ = 16
KEYS = 128
TOK = 16
D = 4096
LANES = 256
FOLD = D // LANES
CHIPS = 64
SLOTS = 3
VECS = 3 * SLOTS
FH = 768
HALF = 32
ROWS = HALF * VECS
FT = 256
WINDOW = 24
NT = 512


def dot(a, b):
    return jnp.dot(a, b, preferred_element_type=F32)


def dot_nt(a, b):
    return lax.dot_general(a, b, (((1,), (1,)), ((), ())), preferred_element_type=F32)


def layer_kernel(
    tok_ref,
    pos_ref,
    gains_ref,
    q_hbm,
    k_hbm,
    v_hbm,
    res_hbm,
    gain_hbm,
    wo_hbm,
    wg_ref,
    wu_ref,
    wd_ref,
    out_ref,
    probe_ref,
    sg_ref,
    su_ref,
    sd_ref,
    q_ref,
    res_ref,
    gain_ref,
    summed_ref,
    normed_ref,
    kb,
    vb,
    sib_send,
    sib_recv,
    own,
    y_send,
    y_recv,
    keep,
    send,
    recv,
    back,
    total,
    in_sem,
    w_send,
    w_recv,
    kv_send,
    kv_recv,
    s_send,
    s_recv,
    ys_send,
    ys_recv,
    send_sem,
    recv_sem,
    bsend_sem,
    brecv_sem,
    gu_sem,
    dn_sem,
):
    seq = lax.axis_index("seq")
    ex = lax.axis_index("exp")
    z, x = lax.div(seq, 4), lax.rem(seq, 4)
    y, core = lax.div(ex, 2), lax.rem(ex, 2)
    sibling = (seq, y * 2 + (1 - core))
    scale = 1.0 / math.sqrt(HD)
    order = (1, 3, 2)

    def z_peer(d):
        return (lax.rem(z + d, 4) * 4 + x, ex)

    def x_peer(d):
        return (z * 4 + lax.rem(x + d, 4), ex)

    def y_peer(d):
        return (seq, lax.rem(y + d, 4) * 2 + core)

    def peer(i, sign):
        dy = lax.rem(i, 4)
        dz = lax.rem(lax.div(i, 16) + dy, 4)
        dx = lax.rem(lax.rem(lax.div(i, 4), 4) + dy, 4)
        if sign < 0:
            dz, dx, dy = 4 - dz, 4 - dx, 4 - dy
        return (lax.rem(z + dz, 4) * 4 + lax.rem(x + dx, 4), lax.rem(y + dy, 4) * 2 + core)

    def remote(src, dst, ssem, rsem, peer):
        return pltpu.make_async_remote_copy(
            src_ref=src, dst_ref=dst, send_sem=ssem, recv_sem=rsem, device_id=peer, device_id_type=MESH
        )

    barrier = pltpu.get_barrier_semaphore()
    pl.semaphore_signal(barrier, inc=1, device_id=sibling, device_id_type=MESH)

    def greet(i, carry):
        pl.semaphore_signal(barrier, inc=1, device_id=peer(i, 1), device_id_type=MESH)
        return carry

    lax.fori_loop(1, CHIPS, greet, 0)
    k_in = pltpu.make_async_copy(k_hbm, kb.at[seq], in_sem.at[0])
    v_in = pltpu.make_async_copy(v_hbm, vb.at[seq], in_sem.at[1])
    q_in = pltpu.make_async_copy(q_hbm, q_ref, in_sem.at[2])
    res_in = pltpu.make_async_copy(res_hbm, res_ref, in_sem.at[3])
    gain_in = pltpu.make_async_copy(gain_hbm, gain_ref, in_sem.at[4])
    for copy in (k_in, v_in, q_in, res_in, gain_in):
        copy.start()
    k_in.wait()
    v_in.wait()
    pl.semaphore_wait(barrier, CHIPS)

    def weight_copy(which, part):
        source = (wg_ref, wu_ref, wd_ref)[which]
        place = (sg_ref, su_ref, sd_ref)[which]
        count = (D, D, FH)[which] // 4
        rows = pl.ds(pl.multiple_of(part * count, count), count)
        number = which * 4 + part
        return remote(source.at[0, rows, :], place.at[0, rows, :], w_send.at[number], w_recv.at[number], sibling)

    sides = (1, 3)
    kv_sent = []

    def origin(which, da, db):
        dz, dx = (da, db) if which == 0 else (db, da)
        return lax.rem(z + dz, 4) * 4 + lax.rem(x + dx, 4)

    def kv_copy(which, source, number, half, device):
        buf = (kb, vb)[which]
        if half is None:
            ref = buf.at[source]
        else:
            ref = buf.at[source, :, half * 64 : half * 64 + 64, :]
        arrival = kv_recv.at[which, source, 1 if half == 1 else 0]
        return remote(ref, ref, kv_send.at[number], arrival, device)

    def push(which, da, db, half, axis, d):
        first = (axis == 0) == (which == 0)
        copy = kv_copy(which, origin(which, da, db), len(kv_sent), half, z_peer(d) if first else x_peer(d))
        copy.start()
        kv_sent.append(copy)

    def arrived(which, da, db, half):
        kv_copy(which, origin(which, da, db), 0, half, z_peer(1)).wait_recv()

    for axis in (0, 1):
        for which in (0, 1):
            for d in sides:
                push(which, 0, 0, None, axis, d)
    for part in range(4):
        weight_copy(0, part).start()

    def attend(qs, qc, scores, slopes, att, wo):
        wo_copy = pltpu.make_async_copy(wo_hbm, wo, in_sem.at[5])
        wo_copy.start(priority=1)
        q_in.wait()
        for h in range(4):
            for s in range(3):
                qs[s, h * 128 : (h + 1) * 128, :] = q_ref[s, :, h * 128 : (h + 1) * 128]
        for t in (1, 2):
            qc[t - 1, :, :HD] = qs[t]
            qc[t - 1, :, HD:] = qs[0]

        def cross(which, da):
            for d in sides:
                arrived(which, da, d, None)
                push(which, da, d, 1 if d == 1 else 0, 1, 4 - d)

        def opposite(which, da, db):
            arrived(which, da, db, 0)
            arrived(which, da, db, 1)

        def score(dz):
            opposite(0, dz, 2)
            c = lax.rem(z + dz, 4)
            kc = kb[pl.ds(c * 4, 4)]
            k0 = kc[:, 0].reshape(512, HD)
            scores[c] = dot_nt(qs[0], k0) * scale
            for t in (1, 2):
                kt = kc[:, t].reshape(512, HD)
                slopes[t - 1, c] = dot_nt(qc[t - 1], jnp.concatenate([k0, kt], axis=1)) * scale

        for d in sides:
            for which in (0, 1):
                arrived(which, d, 0, None)
                push(which, d, 0, 1 if d == 1 else 0, 0, 4 - d)
                for e in sides:
                    push(which, d, 0, None, 1, e)
        for which in (0, 1):
            cross(which, 0)
        for which in (0, 1):
            opposite(which, 2, 0)
            for e in sides:
                push(which, 2, 0, None, 1, e)
        done = 0
        for da in (1, 3, 2):
            for which in (0, 1):
                cross(which, da)
            score(done)
            done = da
        score(done)
        for da in range(4):
            opposite(1, da, 2)

        def head(h, carry):
            rows = pl.ds(pl.multiple_of(h * 128, 128), 128)
            top = jnp.max(scores[0, rows, :], axis=1, keepdims=True)
            for c in (1, 2, 3):
                top = jnp.maximum(top, jnp.max(scores[c, rows, :], axis=1, keepdims=True))
            norm = jnp.zeros((128, 1), F32)
            r1 = jnp.zeros((128, 1), F32)
            r2 = jnp.zeros((128, 1), F32)
            acc = jnp.zeros((128, 3 * HD), F32)
            mixed = jnp.zeros((256, HD), F32)
            for c in range(4):
                p = jnp.exp(scores[c, rows, :] - top).astype(BF)
                pf = p.astype(F32)
                w1 = (pf * slopes[0, c, rows, :]).astype(BF)
                w2 = (pf * slopes[1, c, rows, :]).astype(BF)
                norm += jnp.sum(pf, axis=1, keepdims=True)
                r1 += jnp.sum(w1.astype(F32), axis=1, keepdims=True)
                r2 += jnp.sum(w2.astype(F32), axis=1, keepdims=True)
                v0 = vb[4 * c : 4 * c + 4, 0].reshape(512, HD)
                v1 = vb[4 * c : 4 * c + 4, 1].reshape(512, HD)
                v2 = vb[4 * c : 4 * c + 4, 2].reshape(512, HD)
                acc += dot(p, jnp.concatenate([v0, v1, v2], axis=1))
                mixed += dot(jnp.concatenate([w1, w2], axis=0), v0)
            inv = 1.0 / norm
            main = acc[:, :HD] * inv
            t1 = (mixed[:128] + acc[:, HD : 2 * HD]) * inv - (r1 * inv) * main
            t2 = (mixed[128:] + acc[:, 2 * HD :]) * inv - (r2 * inv) * main
            att[0, :, rows] = main.astype(BF)
            att[1, :, rows] = t1.astype(BF)
            att[2, :, rows] = t2.astype(BF)
            return carry

        lax.fori_loop(0, 4, head, 0)

        wo_copy.wait()

        def block_rows(parity):
            parts = []
            for d in range(4):
                j = lax.rem(y + d, 4) * 2 + parity
                rows = pl.ds(pl.multiple_of(j * TOK, TOK), TOK)
                for s in range(3):
                    parts.append(att[s, rows, :])
            return jnp.concatenate(parts, axis=0)

        sib_rows = block_rows(1 - core)
        sib_copies = []
        for n in range(4):
            sib_send[n] = dot(sib_rows, wo[:, n * 1024 : (n + 1) * 1024]).astype(BF)
            copy = remote(sib_send.at[n], sib_recv.at[n], s_send.at[n], s_recv.at[n], sibling)
            copy.start()
            sib_copies.append(copy)
        own_rows = block_rows(core)

        def y_copy(n, kind):
            up = kind in (0, 2, 3)
            device = y_peer(1) if up else y_peer(3)
            return remote(y_send.at[n, kind], y_recv.at[n, kind], ys_send.at[n, kind], ys_recv.at[n, kind], device)

        for n in range(4):
            lanes = slice(n * 1024, (n + 1) * 1024)
            product = dot(own_rows, wo[:, lanes])
            sib_copies[n].wait_recv()
            both = product + sib_recv[n].astype(F32)
            own[:, lanes] = both[:48]
            y_send[n, 0] = both[96:144, :512].astype(BF)
            y_copy(n, 0).start()
            y_send[n, 1] = both[96:144, 512:].astype(BF)
            y_copy(n, 1).start()
            y_send[n, 3] = both[48:96, 512:].astype(BF)
            y_copy(n, 3).start()
            y_send[n, 4] = both[144:, :512].astype(BF)
            y_copy(n, 4).start()
            keep[n, 0] = both[48:96, :512]
            keep[n, 1] = both[144:, 512:]
        for n in range(4):
            for side in (0, 1):
                y_copy(n, side).wait_recv()
                kind = 2 + 3 * side
                y_send[n, kind] = (keep[n, side] + y_recv[n, side].astype(F32)).astype(BF)
                y_copy(n, kind).start()
        for part in range(4):
            weight_copy(1, part).start()
        for part in range(4):
            weight_copy(2, part).start()
        res_in.wait()
        for n in range(4):
            for kind in (3, 4, 2, 5):
                y_copy(n, kind).wait_recv()
            for half in (0, 1):
                first = n * 1024 + half * 512
                lanes = slice(first, first + 512)
                part = own[:, lanes] + y_recv[n, 2 + half].astype(F32) + y_recv[n, 4 + half].astype(F32)
                for s in range(3):
                    summed_ref[s, :, lanes] = part[16 * s : 16 * (s + 1)] + res_ref[s, :, lanes].astype(F32)
        for n in range(4):
            for kind in range(6):
                y_copy(n, kind).wait_send()
        for copy in kv_sent + sib_copies:
            copy.wait_send()

    pl.run_scoped(
        attend,
        pltpu.VMEM((3, 512, HD), BF),
        pltpu.VMEM((2, 512, 2 * HD), BF),
        pltpu.VMEM((4, 512, 512), F32),
        pltpu.VMEM((2, 4, 512, 512), F32),
        pltpu.VMEM((3, KEYS, 512), BF),
        pltpu.VMEM((512, D), BF),
    )

    def out_copy(i):
        return remote(send.at[i], recv.at[i], send_sem.at[i], recv_sem.at[i], peer(i, 1))

    def back_copy(i):
        return remote(recv.at[i], back.at[i], bsend_sem.at[i], brecv_sem.at[i], peer(i, -1))

    def moe(rows_in, hidden, stage, wgu, wdn):
        def gu_copy(source, which, lanes, slot):
            place = wgu.at[slot, :, which * FT : (which + 1) * FT]
            return pltpu.make_async_copy(source.at[0, :, lanes], place, gu_sem.at[slot, which])

        def dn_copy(source, which, lanes, slot):
            place = wdn.at[slot, which * FH : (which + 1) * FH, :]
            return pltpu.make_async_copy(source.at[0, :, lanes], place, dn_sem.at[slot, which])

        def gu_start(t, slot):
            lanes = pl.ds(pl.multiple_of(lax.rem(t, 3) * FT, FT), FT)

            def go(gate, up):
                gu_copy(gate, 0, lanes, slot).start(priority=1)
                gu_copy(up, 1, lanes, slot).start(priority=1)

            @pl.when(t < 3)
            def _():
                go(wg_ref, wu_ref)

            @pl.when(t >= 3)
            def _():
                go(sg_ref, su_ref)

        def gu_wait(slot):
            gu_copy(wg_ref, 0, slice(0, FT), slot).wait()
            gu_copy(wu_ref, 1, slice(0, FT), slot).wait()

        def dn_start(n, slot):
            lanes = pl.ds(pl.multiple_of(n * NT, NT), NT)
            dn_copy(wd_ref, 0, lanes, slot).start(priority=1)
            dn_copy(sd_ref, 1, lanes, slot).start(priority=1)

        def dn_wait(slot):
            dn_copy(wd_ref, 0, slice(0, NT), slot).wait()
            dn_copy(sd_ref, 1, slice(0, NT), slot).wait()

        gu_start(0, 0)

        gain_in.wait()
        main_sum = summed_ref[0]
        recip = lax.rsqrt(jnp.mean(main_sum * main_sum, axis=-1, keepdims=True) + EPS)
        normed_ref[TOK] = jnp.zeros((3, FOLD, LANES), BF)
        for s in range(3):
            if s == 0:
                rows = main_sum * recip * gain_ref[...]
            else:
                inner = jnp.mean(main_sum * summed_ref[s], axis=-1, keepdims=True)
                rows = (summed_ref[s] * recip - main_sum * (recip * recip * recip * inner)) * gain_ref[...]
            for c in range(FOLD):
                for half in (0, 1):
                    first = c * LANES + half * 128
                    stage[half, pl.ds(c, TOK, stride=FOLD), :] = rows[:, first : first + 128]
            for half in (0, 1):
                normed_ref[:TOK, s, :, half * 128 : half * 128 + 128] = (
                    stage[half, : TOK * FOLD].reshape(TOK, FOLD, 128).astype(BF)
                )

        def dispatch(i, carry):
            for slot in range(SLOTS):
                token = tok_ref[i * SLOTS + slot]
                for s in range(3):
                    send[i, s * SLOTS + slot] = normed_ref[token, s]

            @pl.when(i > WINDOW)
            def _():
                out_copy(i - WINDOW).wait_send()

            out_copy(i).start()
            return carry

        lax.fori_loop(1, CHIPS, dispatch, 0)

        for slot in range(SLOTS):
            token = tok_ref[slot]
            for s in range(3):
                recv[0, s * SLOTS + slot] = normed_ref[token, s]
        for which in range(3):
            for part in range(4):
                weight_copy(which, part).wait()

        def chunk(g, carry):
            def arrive(i, carry):
                out_copy(i).wait_recv()
                return carry

            lax.fori_loop(jnp.where(g == 0, 1, HALF), (g + 1) * HALF, arrive, 0)

            def unfold(m, carry):
                v, part = lax.div(m, 2), lax.rem(m, 2)
                tiles = recv[pl.ds(g * HALF + part * 16, 16), v].astype(F32).reshape(16 * FOLD, LANES)
                for half in (0, 1):
                    stage[half, : 16 * FOLD] = tiles[:, half * 128 : half * 128 + 128]
                row = pl.multiple_of(v * HALF + part * 16, 16)
                for c in range(FOLD):
                    for half in (0, 1):
                        first = c * LANES + half * 128
                        rows_in[pl.ds(row, 16), first : first + 128] = stage[
                            half, pl.ds(c, 16, stride=FOLD), :
                        ].astype(BF)
                return carry

            lax.fori_loop(0, 2 * VECS, unfold, 0)

            def gate_up(t, carry):
                slot = lax.rem(t, 2)

                @pl.when(t < 5)
                def _():
                    gu_start(t + 1, 1 - slot)

                @pl.when(t == 5)
                def _():
                    dn_start(0, 0)

                gu_wait(slot)
                both = dot(rows_in[...], wgu[slot])
                g_all, u_all = both[:, :FT], both[:, FT:]
                n = SLOTS * HALF
                g0, u0 = g_all[:n], u_all[:n]
                sigma = 1.0 / (1.0 + jnp.exp(-g0))
                active = g0 * sigma
                slope = sigma * (1.0 + g0 * (1.0 - sigma)) * u0
                lanes = pl.ds(pl.multiple_of(t * FT, FT), FT)
                hidden[:n, lanes] = (active * u0).astype(BF)
                hidden[n : 2 * n, lanes] = (slope * g_all[n : 2 * n] + active * u_all[n : 2 * n]).astype(BF)
                hidden[2 * n :, lanes] = (slope * g_all[2 * n :] + active * u_all[2 * n :]).astype(BF)
                return carry

            lax.fori_loop(0, 6, gate_up, 0)

            def down(n, carry):
                slot = lax.rem(n, 2)

                @pl.when(n < D // NT - 1)
                def _():
                    dn_start(n + 1, 1 - slot)

                @pl.when((n == D // NT - 1) & (g == 0))
                def _():
                    gu_start(0, 0)

                dn_wait(slot)
                part = dot(hidden[...], wdn[slot])
                for q in range(NT // LANES):
                    for half in (0, 1):
                        first = q * LANES + half * 128
                        stage[half, pl.ds(n * (NT // LANES) + q, ROWS, stride=FOLD), :] = part[
                            :, first : first + 128
                        ]
                return carry

            lax.fori_loop(0, D // NT, down, 0)

            def fold(v, carry):
                for part in (0, 1):
                    row = pl.multiple_of((v * HALF + part * 16) * FOLD, 256)
                    for half in (0, 1):
                        recv[pl.ds(g * HALF + part * 16, 16), v, :, half * 128 : half * 128 + 128] = (
                            stage[half, pl.ds(row, 16 * FOLD), :].reshape(16, FOLD, 128).astype(BF)
                        )
                return carry

            lax.fori_loop(0, VECS, fold, 0)

            def give_back(i, carry):
                back_copy(i).start()
                return carry

            lax.fori_loop(jnp.where(g == 0, 1, HALF), (g + 1) * HALF, give_back, 0)
            return carry

        lax.fori_loop(0, 2, chunk, 0)

    pl.run_scoped(
        moe,
        pltpu.VMEM((ROWS, D), BF),
        pltpu.VMEM((ROWS, 2 * FH), BF),
        pltpu.VMEM((2, ROWS * FOLD, 128), F32),
        pltpu.VMEM((2, D, 2 * FT), BF),
        pltpu.VMEM((2, 2 * FH, NT), BF),
    )
    back[0] = recv[0]

    def collect(i, carry):
        @pl.when(i >= CHIPS - WINDOW)
        def _():
            out_copy(i).wait_send()

        back_copy(i).wait()
        return carry

    lax.fori_loop(1, CHIPS, collect, 0)

    def combine(tok, carry):
        sums = [jnp.zeros((FOLD, LANES), F32) for _ in range(3)]
        for r in range(8):
            where = pos_ref[r * TOK + tok]
            chip, slot = lax.div(where, SLOTS), lax.rem(where, SLOTS)
            weight = gains_ref[r, tok]
            for s in range(3):
                sums[s] += weight * back[chip, s * SLOTS + slot].astype(F32)
        row = pl.ds(pl.multiple_of(tok * FOLD, FOLD), FOLD)
        for s in range(3):
            for half in (0, 1):
                total[s, half, row, :] = sums[s][:, half * 128 : half * 128 + 128]
        return carry

    lax.fori_loop(0, TOK, combine, 0)
    probes = [jnp.zeros((TOK, 128), F32) for _ in range(2)]
    for c in range(FOLD):
        for half in (0, 1):
            first = c * LANES + half * 128
            lanes = slice(first, first + 128)
            for s in range(3):
                value = summed_ref[s, :, lanes] + total[s, half, pl.ds(c, TOK, stride=FOLD), :]
                out_ref[s, :, lanes] = value.astype(BF)
                if s:
                    probes[s - 1] += value * res_ref[s, :, lanes].astype(F32)
    diagonal = lax.broadcasted_iota(jnp.int32, (TOK, 128), 0) == lax.broadcasted_iota(jnp.int32, (TOK, 128), 1)
    for t in range(2):
        mean = jnp.sum(probes[t], axis=1, keepdims=True) * (1.0 / D)
        flat = jnp.sum(jnp.where(diagonal, mean, 0.0), axis=0, keepdims=True)
        probe_ref[t : t + 1, :] = flat[:, :TOK]


def layer(tok, pos, gains, q, k, v, residual, gain, w_out, w_gate, w_up, w_down):
    smem = pl.BlockSpec(memory_space=pltpu.SMEM)
    vmem = pl.BlockSpec(memory_space=pltpu.VMEM)
    hbm = pl.BlockSpec(memory_space=pltpu.HBM)
    dma = pltpu.SemaphoreType.DMA
    tiles = (CHIPS, VECS, FOLD, LANES)
    outs = pl.pallas_call(
        layer_kernel,
        out_shape=(
            jax.ShapeDtypeStruct((3, TOK, D), BF),
            jax.ShapeDtypeStruct((2, TOK), F32),
            jax.ShapeDtypeStruct(w_gate.shape, BF),
            jax.ShapeDtypeStruct(w_up.shape, BF),
            jax.ShapeDtypeStruct(w_down.shape, BF),
        ),
        in_specs=[smem] * 3 + [hbm] * 9,
        out_specs=(vmem, vmem, hbm, hbm, hbm),
        scratch_shapes=[
            pltpu.VMEM((3, KEYS, 512), BF),
            pltpu.VMEM((3, TOK, D), BF),
            pltpu.VMEM((1, D), F32),
            pltpu.VMEM((3, TOK, D), F32),
            pltpu.VMEM((TOK + 1, 3, FOLD, LANES), BF),
            pltpu.VMEM((SEQ, 3, KEYS, HD), BF),
            pltpu.VMEM((SEQ, 3, KEYS, HD), BF),
            pltpu.VMEM((4, 192, 1024), BF),
            pltpu.VMEM((4, 192, 1024), BF),
            pltpu.VMEM((48, D), F32),
            pltpu.VMEM((4, 6, 48, 512), BF),
            pltpu.VMEM((4, 6, 48, 512), BF),
            pltpu.VMEM((4, 2, 48, 512), F32),
            pltpu.VMEM(tiles, BF),
            pltpu.VMEM(tiles, BF),
            pltpu.VMEM(tiles, BF),
            pltpu.VMEM((3, 2, TOK * FOLD, 128), F32),
            dma((6,)),
            dma((12,)),
            dma((12,)),
            dma((40,)),
            dma((2, SEQ, 2)),
            dma((4,)),
            dma((4,)),
            dma((4, 6)),
            dma((4, 6)),
            dma((CHIPS,)),
            dma((CHIPS,)),
            dma((CHIPS,)),
            dma((CHIPS,)),
            dma((2, 2)),
            dma((2, 2)),
        ],
        compiler_params=pltpu.CompilerParams(
            collective_id=0, has_side_effects=True, vmem_limit_bytes=58 * 2**20
        ),
        name="layer",
    )(tok, pos, gains, q, k, v, residual, gain, w_out, w_gate, w_up, w_down)
    return outs[0], outs[1]


def plan(routes):
    seq, ex = lax.axis_index("seq"), lax.axis_index("exp")
    z, x, y = seq // 4, seq % 4, ex // 2
    flat = routes.T.reshape(-1)
    count = flat.shape[0]
    order = jnp.arange(count)
    earlier = (flat[:, None] == flat[None, :]) & (order[None, :] < order[:, None])
    slot = jnp.sum(earlier.astype(jnp.int32), axis=1)
    dz = (flat // 16 - z) % 4
    dx = (flat // 4 % 4 - x) % 4
    dy = (flat % 4 - y) % 4
    number = (dz - dy) % 4 * 16 + (dx - dy) % 4 * 4 + dy
    pos = number * SLOTS + slot
    hit = (jnp.arange(CHIPS * SLOTS)[:, None] == pos[None, :]).astype(jnp.int32)
    tok = TOK + jnp.sum(hit * (order % TOK - TOK)[None, :], axis=1)
    return tok.astype(jnp.int32), pos.astype(jnp.int32)


def shards(
    queries,
    key_rows,
    value_rows,
    residual,
    w_out,
    norm_gain,
    w_gate,
    w_up,
    w_down,
    routes,
    route_gain,
):
    tok, pos = plan(routes)
    return layer(
        tok,
        pos,
        route_gain.T,
        queries,
        key_rows,
        value_rows,
        residual,
        norm_gain[None, :],
        w_out,
        w_gate,
        w_up,
        w_down,
    )


def solution(mesh):
    return jax.shard_map(
        shards,
        mesh=mesh,
        in_specs=(
            P(None, "seq", "exp"),
            P(None, "seq", "exp"),
            P(None, "seq", "exp"),
            P(None, ("seq", "exp"), None),
            P("exp", None),
            P(),
            P(("seq", "exp"), None, None),
            P(("seq", "exp"), None, None),
            P(("seq", "exp"), None, None),
            P(("seq", "exp"), None),
            P(("seq", "exp"), None),
        ),
        out_specs=(P(None, ("seq", "exp"), None), P(None, ("seq", "exp"))),
        check_vma=False,
    )
```

```python
import math

import jax
import jax.numpy as jnp
from jax import lax
from jax.experimental import pallas as pl
from jax.experimental.pallas import tpu as pltpu
from jax.sharding import PartitionSpec as P

HD = 128
EPS = 1e-06
MESH = pl.DeviceIdType.MESH
BF = jnp.bfloat16
F32 = jnp.float32

SEQ = 16
KEYS = 128
TOK = 16
D = 4096
LANES = 256
FOLD = D // LANES
CHIPS = 64
SLOTS = 3
VECS = 3 * SLOTS
FH = 768
HALF = 32
ROWS = HALF * VECS
FT = 256
WINDOW = 14
NT = 512


def dot(a, b):
    return jnp.dot(a, b, preferred_element_type=F32)


def dot_nt(a, b):
    return lax.dot_general(a, b, (((1,), (1,)), ((), ())), preferred_element_type=F32)


def layer_kernel(
    tok_ref,
    pos_ref,
    gains_ref,
    q_hbm,
    k_hbm,
    v_hbm,
    res_hbm,
    gain_hbm,
    wo_hbm,
    wg_ref,
    wu_ref,
    wd_ref,
    out_ref,
    probe_ref,
    sg_ref,
    su_ref,
    sd_ref,
    q_ref,
    res_ref,
    gain_ref,
    summed_ref,
    normed_ref,
    kb,
    vb,
    sib_send,
    sib_recv,
    own,
    y_send,
    y_recv,
    send,
    recv,
    back,
    total,
    in_sem,
    w_send,
    w_recv,
    kv_send,
    kv_recv,
    s_send,
    s_recv,
    ys_send,
    ys_recv,
    send_sem,
    recv_sem,
    bsend_sem,
    brecv_sem,
    gu_sem,
    dn_sem,
):
    seq = lax.axis_index("seq")
    ex = lax.axis_index("exp")
    z, x = lax.div(seq, 4), lax.rem(seq, 4)
    y, core = lax.div(ex, 2), lax.rem(ex, 2)
    sibling = (seq, y * 2 + (1 - core))
    scale = 1.0 / math.sqrt(HD)
    order = (1, 3, 2)

    def z_peer(d):
        return (lax.rem(z + d, 4) * 4 + x, ex)

    def x_peer(d):
        return (z * 4 + lax.rem(x + d, 4), ex)

    def y_peer(d):
        return (seq, lax.rem(y + d, 4) * 2 + core)

    def peer(i, sign):
        dy = lax.rem(i, 4)
        dz = lax.rem(lax.div(i, 16) + dy, 4)
        dx = lax.rem(lax.rem(lax.div(i, 4), 4) + dy, 4)
        if sign < 0:
            dz, dx, dy = 4 - dz, 4 - dx, 4 - dy
        return (lax.rem(z + dz, 4) * 4 + lax.rem(x + dx, 4), lax.rem(y + dy, 4) * 2 + core)

    def remote(src, dst, ssem, rsem, peer):
        return pltpu.make_async_remote_copy(
            src_ref=src, dst_ref=dst, send_sem=ssem, recv_sem=rsem, device_id=peer, device_id_type=MESH
        )

    barrier = pltpu.get_barrier_semaphore()
    pl.semaphore_signal(barrier, inc=1, device_id=sibling, device_id_type=MESH)

    def greet(i, carry):
        pl.semaphore_signal(barrier, inc=1, device_id=peer(i, 1), device_id_type=MESH)
        return carry

    lax.fori_loop(1, CHIPS, greet, 0)
    k_in = pltpu.make_async_copy(k_hbm, kb.at[seq], in_sem.at[0])
    v_in = pltpu.make_async_copy(v_hbm, vb.at[seq], in_sem.at[1])
    q_in = pltpu.make_async_copy(q_hbm, q_ref, in_sem.at[2])
    res_in = pltpu.make_async_copy(res_hbm, res_ref, in_sem.at[3])
    gain_in = pltpu.make_async_copy(gain_hbm, gain_ref, in_sem.at[4])
    for copy in (k_in, v_in, q_in, res_in, gain_in):
        copy.start()
    k_in.wait()
    v_in.wait()
    pl.semaphore_wait(barrier, CHIPS)

    def weight_copy(which, part):
        source = (wg_ref, wu_ref, wd_ref)[which]
        place = (sg_ref, su_ref, sd_ref)[which]
        count = (D, D, FH)[which] // 4
        rows = pl.ds(pl.multiple_of(part * count, count), count)
        number = which * 4 + part
        return remote(source.at[0, rows, :], place.at[0, rows, :], w_send.at[number], w_recv.at[number], sibling)

    sides = (1, 3)
    kv_sent = []

    def origin(which, da, db):
        dz, dx = (da, db) if which == 0 else (db, da)
        return lax.rem(z + dz, 4) * 4 + lax.rem(x + dx, 4)

    def kv_copy(which, source, number, half, device):
        buf = (kb, vb)[which]
        if half is None:
            ref = buf.at[source]
        else:
            ref = buf.at[source, :, half * 64 : half * 64 + 64, :]
        arrival = kv_recv.at[which, source, 1 if half == 1 else 0]
        return remote(ref, ref, kv_send.at[number], arrival, device)

    def push(which, da, db, half, axis, d):
        first = (axis == 0) == (which == 0)
        copy = kv_copy(which, origin(which, da, db), len(kv_sent), half, z_peer(d) if first else x_peer(d))
        copy.start()
        kv_sent.append(copy)

    def arrived(which, da, db, half):
        kv_copy(which, origin(which, da, db), 0, half, z_peer(1)).wait_recv()

    for axis in (0, 1):
        for which in (0, 1):
            for d in sides:
                push(which, 0, 0, None, axis, d)
    for part in range(4):
        weight_copy(0, part).start()

    def attend(qs, qc, scores, slopes, att, wo):
        wo_copy = pltpu.make_async_copy(wo_hbm, wo, in_sem.at[5])
        wo_copy.start(priority=1)
        q_in.wait()
        for h in range(4):
            for s in range(3):
                qs[s, h * 128 : (h + 1) * 128, :] = q_ref[s, :, h * 128 : (h + 1) * 128]
        for t in (1, 2):
            qc[t - 1, :, :HD] = qs[t]
            qc[t - 1, :, HD:] = qs[0]

        def cross(which, da):
            for d in sides:
                arrived(which, da, d, None)
                push(which, da, d, 1 if d == 1 else 0, 1, 4 - d)

        def opposite(which, da, db):
            arrived(which, da, db, 0)
            arrived(which, da, db, 1)

        def score(dz):
            opposite(0, dz, 2)
            c = lax.rem(z + dz, 4)
            kc = kb[pl.ds(c * 4, 4)]
            k0 = kc[:, 0].reshape(512, HD)
            scores[c] = dot_nt(qs[0], k0) * scale
            for t in (1, 2):
                kt = kc[:, t].reshape(512, HD)
                slopes[t - 1, c] = dot_nt(qc[t - 1], jnp.concatenate([k0, kt], axis=1)) * scale

        for d in sides:
            for which in (0, 1):
                arrived(which, d, 0, None)
                push(which, d, 0, 1 if d == 1 else 0, 0, 4 - d)
                for e in sides:
                    push(which, d, 0, None, 1, e)
        for which in (0, 1):
            cross(which, 0)
        for which in (0, 1):
            opposite(which, 2, 0)
            for e in sides:
                push(which, 2, 0, None, 1, e)
        done = 0
        for da in (1, 3, 2):
            for which in (0, 1):
                cross(which, da)
            score(done)
            done = da
        score(done)
        for da in range(4):
            opposite(1, da, 2)

        def head(h, carry):
            rows = pl.ds(pl.multiple_of(h * 128, 128), 128)
            top = jnp.max(scores[0, rows, :], axis=1, keepdims=True)
            for c in (1, 2, 3):
                top = jnp.maximum(top, jnp.max(scores[c, rows, :], axis=1, keepdims=True))
            norm = jnp.zeros((128, 1), F32)
            r1 = jnp.zeros((128, 1), F32)
            r2 = jnp.zeros((128, 1), F32)
            acc = jnp.zeros((128, 3 * HD), F32)
            mixed = jnp.zeros((256, HD), F32)
            for c in range(4):
                p = jnp.exp(scores[c, rows, :] - top).astype(BF)
                pf = p.astype(F32)
                w1 = (pf * slopes[0, c, rows, :]).astype(BF)
                w2 = (pf * slopes[1, c, rows, :]).astype(BF)
                norm += jnp.sum(pf, axis=1, keepdims=True)
                r1 += jnp.sum(w1.astype(F32), axis=1, keepdims=True)
                r2 += jnp.sum(w2.astype(F32), axis=1, keepdims=True)
                v0 = vb[4 * c : 4 * c + 4, 0].reshape(512, HD)
                v1 = vb[4 * c : 4 * c + 4, 1].reshape(512, HD)
                v2 = vb[4 * c : 4 * c + 4, 2].reshape(512, HD)
                acc += dot(p, jnp.concatenate([v0, v1, v2], axis=1))
                mixed += dot(jnp.concatenate([w1, w2], axis=0), v0)
            inv = 1.0 / norm
            main = acc[:, :HD] * inv
            t1 = (mixed[:128] + acc[:, HD : 2 * HD]) * inv - (r1 * inv) * main
            t2 = (mixed[128:] + acc[:, 2 * HD :]) * inv - (r2 * inv) * main
            att[0, :, rows] = main.astype(BF)
            att[1, :, rows] = t1.astype(BF)
            att[2, :, rows] = t2.astype(BF)
            return carry

        lax.fori_loop(0, 4, head, 0)

        wo_copy.wait()

        def block_rows(parity):
            parts = []
            for d in range(4):
                j = lax.rem(y + d, 4) * 2 + parity
                rows = pl.ds(pl.multiple_of(j * TOK, TOK), TOK)
                for s in range(3):
                    parts.append(att[s, rows, :])
            return jnp.concatenate(parts, axis=0)

        sib_rows = block_rows(1 - core)
        sib_copies = []
        for n in range(4):
            sib_send[n] = dot(sib_rows, wo[:, n * 1024 : (n + 1) * 1024]).astype(BF)
            copy = remote(sib_send.at[n], sib_recv.at[n], s_send.at[n], s_recv.at[n], sibling)
            copy.start()
            sib_copies.append(copy)
        own_rows = block_rows(core)
        y_copies = []
        for n in range(4):
            lanes = slice(n * 1024, (n + 1) * 1024)
            product = dot(own_rows, wo[:, lanes])
            sib_copies[n].wait_recv()
            both = product + sib_recv[n].astype(F32)
            own[:, lanes] = both[:48]
            for d in order:
                y_send[n, d - 1] = both[48 * d : 48 * (d + 1)].astype(BF)
                copy = remote(
                    y_send.at[n, d - 1], y_recv.at[n, d - 1], ys_send.at[n, d - 1], ys_recv.at[n, d - 1], y_peer(d)
                )
                copy.start()
                y_copies.append(copy)
        for part in range(4):
            weight_copy(1, part).start()
        for part in range(4):
            weight_copy(2, part).start()
        res_in.wait()
        for n in range(4):
            for d in (1, 2, 3):
                y_copies[n * 3 + order.index(d)].wait_recv()
            lanes = slice(n * 1024, (n + 1) * 1024)
            part = own[:, lanes]
            for d in (1, 2, 3):
                part += y_recv[n, d - 1].astype(F32)
            for s in range(3):
                summed_ref[s, :, lanes] = part[16 * s : 16 * (s + 1)] + res_ref[s, :, lanes].astype(F32)
        for copy in kv_sent + sib_copies + y_copies:
            copy.wait_send()

    pl.run_scoped(
        attend,
        pltpu.VMEM((3, 512, HD), BF),
        pltpu.VMEM((2, 512, 2 * HD), BF),
        pltpu.VMEM((4, 512, 512), F32),
        pltpu.VMEM((2, 4, 512, 512), F32),
        pltpu.VMEM((3, KEYS, 512), BF),
        pltpu.VMEM((512, D), BF),
    )

    def out_copy(i):
        return remote(send.at[i], recv.at[i], send_sem.at[i], recv_sem.at[i], peer(i, 1))

    def back_copy(i):
        return remote(recv.at[i], back.at[i], bsend_sem.at[i], brecv_sem.at[i], peer(i, -1))

    def moe(rows_in, hidden, stage, wgu, wdn):
        def gu_copy(source, which, lanes, slot):
            place = wgu.at[slot, :, which * FT : (which + 1) * FT]
            return pltpu.make_async_copy(source.at[0, :, lanes], place, gu_sem.at[slot, which])

        def dn_copy(source, which, lanes, slot):
            place = wdn.at[slot, which * FH : (which + 1) * FH, :]
            return pltpu.make_async_copy(source.at[0, :, lanes], place, dn_sem.at[slot, which])

        def gu_start(t, slot):
            lanes = pl.ds(pl.multiple_of(lax.rem(t, 3) * FT, FT), FT)

            def go(gate, up):
                gu_copy(gate, 0, lanes, slot).start(priority=1)
                gu_copy(up, 1, lanes, slot).start(priority=1)

            @pl.when(t < 3)
            def _():
                go(wg_ref, wu_ref)

            @pl.when(t >= 3)
            def _():
                go(sg_ref, su_ref)

        def gu_wait(slot):
            gu_copy(wg_ref, 0, slice(0, FT), slot).wait()
            gu_copy(wu_ref, 1, slice(0, FT), slot).wait()

        def dn_start(n, slot):
            lanes = pl.ds(pl.multiple_of(n * NT, NT), NT)
            dn_copy(wd_ref, 0, lanes, slot).start(priority=1)
            dn_copy(sd_ref, 1, lanes, slot).start(priority=1)

        def dn_wait(slot):
            dn_copy(wd_ref, 0, slice(0, NT), slot).wait()
            dn_copy(sd_ref, 1, slice(0, NT), slot).wait()

        gu_start(0, 0)

        gain_in.wait()
        main_sum = summed_ref[0]
        recip = lax.rsqrt(jnp.mean(main_sum * main_sum, axis=-1, keepdims=True) + EPS)
        normed_ref[TOK] = jnp.zeros((3, FOLD, LANES), BF)
        for s in range(3):
            if s == 0:
                rows = main_sum * recip * gain_ref[...]
            else:
                inner = jnp.mean(main_sum * summed_ref[s], axis=-1, keepdims=True)
                rows = (summed_ref[s] * recip - main_sum * (recip * recip * recip * inner)) * gain_ref[...]
            for c in range(FOLD):
                for half in (0, 1):
                    first = c * LANES + half * 128
                    stage[half, pl.ds(c, TOK, stride=FOLD), :] = rows[:, first : first + 128]
            for half in (0, 1):
                normed_ref[:TOK, s, :, half * 128 : half * 128 + 128] = (
                    stage[half, : TOK * FOLD].reshape(TOK, FOLD, 128).astype(BF)
                )

        def dispatch(i, carry):
            for slot in range(SLOTS):
                token = tok_ref[i * SLOTS + slot]
                for s in range(3):
                    send[i, s * SLOTS + slot] = normed_ref[token, s]

            @pl.when(i > WINDOW)
            def _():
                out_copy(i - WINDOW).wait_send()

            out_copy(i).start()
            return carry

        lax.fori_loop(1, CHIPS, dispatch, 0)

        for slot in range(SLOTS):
            token = tok_ref[slot]
            for s in range(3):
                recv[0, s * SLOTS + slot] = normed_ref[token, s]
        for which in range(3):
            for part in range(4):
                weight_copy(which, part).wait()

        def chunk(g, carry):
            def arrive(i, carry):
                out_copy(i).wait_recv()
                return carry

            lax.fori_loop(jnp.where(g == 0, 1, HALF), (g + 1) * HALF, arrive, 0)

            def unfold(m, carry):
                v, part = lax.div(m, 2), lax.rem(m, 2)
                tiles = recv[pl.ds(g * HALF + part * 16, 16), v].astype(F32).reshape(16 * FOLD, LANES)
                for half in (0, 1):
                    stage[half, : 16 * FOLD] = tiles[:, half * 128 : half * 128 + 128]
                row = pl.multiple_of(v * HALF + part * 16, 16)
                for c in range(FOLD):
                    for half in (0, 1):
                        first = c * LANES + half * 128
                        rows_in[pl.ds(row, 16), first : first + 128] = stage[
                            half, pl.ds(c, 16, stride=FOLD), :
                        ].astype(BF)
                return carry

            lax.fori_loop(0, 2 * VECS, unfold, 0)

            def gate_up(t, carry):
                slot = lax.rem(t, 2)

                @pl.when(t < 5)
                def _():
                    gu_start(t + 1, 1 - slot)

                @pl.when(t == 5)
                def _():
                    dn_start(0, 0)

                gu_wait(slot)
                both = dot(rows_in[...], wgu[slot])
                g_all, u_all = both[:, :FT], both[:, FT:]
                n = SLOTS * HALF
                g0, u0 = g_all[:n], u_all[:n]
                sigma = 1.0 / (1.0 + jnp.exp(-g0))
                active = g0 * sigma
                slope = sigma * (1.0 + g0 * (1.0 - sigma)) * u0
                lanes = pl.ds(pl.multiple_of(t * FT, FT), FT)
                hidden[:n, lanes] = (active * u0).astype(BF)
                hidden[n : 2 * n, lanes] = (slope * g_all[n : 2 * n] + active * u_all[n : 2 * n]).astype(BF)
                hidden[2 * n :, lanes] = (slope * g_all[2 * n :] + active * u_all[2 * n :]).astype(BF)
                return carry

            lax.fori_loop(0, 6, gate_up, 0)

            def down(n, carry):
                slot = lax.rem(n, 2)

                @pl.when(n < D // NT - 1)
                def _():
                    dn_start(n + 1, 1 - slot)

                @pl.when((n == D // NT - 1) & (g == 0))
                def _():
                    gu_start(0, 0)

                dn_wait(slot)
                part = dot(hidden[...], wdn[slot])
                for q in range(NT // LANES):
                    for half in (0, 1):
                        first = q * LANES + half * 128
                        stage[half, pl.ds(n * (NT // LANES) + q, ROWS, stride=FOLD), :] = part[
                            :, first : first + 128
                        ]
                return carry

            lax.fori_loop(0, D // NT, down, 0)

            def fold(v, carry):
                for part in (0, 1):
                    row = pl.multiple_of((v * HALF + part * 16) * FOLD, 256)
                    for half in (0, 1):
                        recv[pl.ds(g * HALF + part * 16, 16), v, :, half * 128 : half * 128 + 128] = (
                            stage[half, pl.ds(row, 16 * FOLD), :].reshape(16, FOLD, 128).astype(BF)
                        )
                return carry

            lax.fori_loop(0, VECS, fold, 0)

            def give_back(i, carry):
                back_copy(i).start()
                return carry

            lax.fori_loop(jnp.where(g == 0, 1, HALF), (g + 1) * HALF, give_back, 0)
            return carry

        lax.fori_loop(0, 2, chunk, 0)

    pl.run_scoped(
        moe,
        pltpu.VMEM((ROWS, D), BF),
        pltpu.VMEM((ROWS, 2 * FH), BF),
        pltpu.VMEM((2, ROWS * FOLD, 128), F32),
        pltpu.VMEM((2, D, 2 * FT), BF),
        pltpu.VMEM((2, 2 * FH, NT), BF),
    )
    back[0] = recv[0]

    def collect(i, carry):
        @pl.when(i >= CHIPS - WINDOW)
        def _():
            out_copy(i).wait_send()

        back_copy(i).wait()
        return carry

    lax.fori_loop(1, CHIPS, collect, 0)

    def combine(tok, carry):
        sums = [jnp.zeros((FOLD, LANES), F32) for _ in range(3)]
        for r in range(8):
            where = pos_ref[r * TOK + tok]
            chip, slot = lax.div(where, SLOTS), lax.rem(where, SLOTS)
            weight = gains_ref[r, tok]
            for s in range(3):
                sums[s] += weight * back[chip, s * SLOTS + slot].astype(F32)
        row = pl.ds(pl.multiple_of(tok * FOLD, FOLD), FOLD)
        for s in range(3):
            for half in (0, 1):
                total[s, half, row, :] = sums[s][:, half * 128 : half * 128 + 128]
        return carry

    lax.fori_loop(0, TOK, combine, 0)
    probes = [jnp.zeros((TOK, 128), F32) for _ in range(2)]
    for c in range(FOLD):
        for half in (0, 1):
            first = c * LANES + half * 128
            lanes = slice(first, first + 128)
            for s in range(3):
                value = summed_ref[s, :, lanes] + total[s, half, pl.ds(c, TOK, stride=FOLD), :]
                out_ref[s, :, lanes] = value.astype(BF)
                if s:
                    probes[s - 1] += value * res_ref[s, :, lanes].astype(F32)
    diagonal = lax.broadcasted_iota(jnp.int32, (TOK, 128), 0) == lax.broadcasted_iota(jnp.int32, (TOK, 128), 1)
    for t in range(2):
        mean = jnp.sum(probes[t], axis=1, keepdims=True) * (1.0 / D)
        flat = jnp.sum(jnp.where(diagonal, mean, 0.0), axis=0, keepdims=True)
        probe_ref[t : t + 1, :] = flat[:, :TOK]


def layer(tok, pos, gains, q, k, v, residual, gain, w_out, w_gate, w_up, w_down):
    smem = pl.BlockSpec(memory_space=pltpu.SMEM)
    vmem = pl.BlockSpec(memory_space=pltpu.VMEM)
    hbm = pl.BlockSpec(memory_space=pltpu.HBM)
    dma = pltpu.SemaphoreType.DMA
    tiles = (CHIPS, VECS, FOLD, LANES)
    outs = pl.pallas_call(
        layer_kernel,
        out_shape=(
            jax.ShapeDtypeStruct((3, TOK, D), BF),
            jax.ShapeDtypeStruct((2, TOK), F32),
            jax.ShapeDtypeStruct(w_gate.shape, BF),
            jax.ShapeDtypeStruct(w_up.shape, BF),
            jax.ShapeDtypeStruct(w_down.shape, BF),
        ),
        in_specs=[smem] * 3 + [hbm] * 9,
        out_specs=(vmem, vmem, hbm, hbm, hbm),
        scratch_shapes=[
            pltpu.VMEM((3, KEYS, 512), BF),
            pltpu.VMEM((3, TOK, D), BF),
            pltpu.VMEM((1, D), F32),
            pltpu.VMEM((3, TOK, D), F32),
            pltpu.VMEM((TOK + 1, 3, FOLD, LANES), BF),
            pltpu.VMEM((SEQ, 3, KEYS, HD), BF),
            pltpu.VMEM((SEQ, 3, KEYS, HD), BF),
            pltpu.VMEM((4, 192, 1024), BF),
            pltpu.VMEM((4, 192, 1024), BF),
            pltpu.VMEM((48, D), F32),
            pltpu.VMEM((4, 3, 48, 1024), BF),
            pltpu.VMEM((4, 3, 48, 1024), BF),
            pltpu.VMEM(tiles, BF),
            pltpu.VMEM(tiles, BF),
            pltpu.VMEM(tiles, BF),
            pltpu.VMEM((3, 2, TOK * FOLD, 128), F32),
            dma((6,)),
            dma((12,)),
            dma((12,)),
            dma((40,)),
            dma((2, SEQ, 2)),
            dma((4,)),
            dma((4,)),
            dma((4, 3)),
            dma((4, 3)),
            dma((CHIPS,)),
            dma((CHIPS,)),
            dma((CHIPS,)),
            dma((CHIPS,)),
            dma((2, 2)),
            dma((2, 2)),
        ],
        compiler_params=pltpu.CompilerParams(
            collective_id=0, has_side_effects=True, vmem_limit_bytes=58 * 2**20
        ),
        name="layer",
    )(tok, pos, gains, q, k, v, residual, gain, w_out, w_gate, w_up, w_down)
    return outs[0], outs[1]


def plan(routes):
    seq, ex = lax.axis_index("seq"), lax.axis_index("exp")
    z, x, y = seq // 4, seq % 4, ex // 2
    flat = routes.T.reshape(-1)
    count = flat.shape[0]
    order = jnp.arange(count)
    earlier = (flat[:, None] == flat[None, :]) & (order[None, :] < order[:, None])
    slot = jnp.sum(earlier.astype(jnp.int32), axis=1)
    dz = (flat // 16 - z) % 4
    dx = (flat // 4 % 4 - x) % 4
    dy = (flat % 4 - y) % 4
    number = (dz - dy) % 4 * 16 + (dx - dy) % 4 * 4 + dy
    pos = number * SLOTS + slot
    hit = (jnp.arange(CHIPS * SLOTS)[:, None] == pos[None, :]).astype(jnp.int32)
    tok = TOK + jnp.sum(hit * (order % TOK - TOK)[None, :], axis=1)
    return tok.astype(jnp.int32), pos.astype(jnp.int32)


def shards(
    queries,
    key_rows,
    value_rows,
    residual,
    w_out,
    norm_gain,
    w_gate,
    w_up,
    w_down,
    routes,
    route_gain,
):
    tok, pos = plan(routes)
    return layer(
        tok,
        pos,
        route_gain.T,
        queries,
        key_rows,
        value_rows,
        residual,
        norm_gain[None, :],
        w_out,
        w_gate,
        w_up,
        w_down,
    )


def solution(mesh):
    return jax.shard_map(
        shards,
        mesh=mesh,
        in_specs=(
            P(None, "seq", "exp"),
            P(None, "seq", "exp"),
            P(None, "seq", "exp"),
            P(None, ("seq", "exp"), None),
            P("exp", None),
            P(),
            P(("seq", "exp"), None, None),
            P(("seq", "exp"), None, None),
            P(("seq", "exp"), None, None),
            P(("seq", "exp"), None),
            P(("seq", "exp"), None),
        ),
        out_specs=(P(None, ("seq", "exp"), None), P(None, ("seq", "exp"))),
        check_vma=False,
    )
```
